32 devices in a mesh: group: 1, tile: 32 (over z, y, x, core).
Axes of the slice: x: 2, y: 2, z: 4, core: 2. Of those that a mesh axis runs over, the one named last changes fastest.
Arguments:
- profiles: bfloat16 [16384, 384], P(('group', 'tile')), may hold values from -6 to 6
- radiances: bfloat16 [16384, 512], P(('group', 'tile')), may hold values from -6 to 6
- inner_weight: bfloat16 [384, 4096], replicated, may hold values from -0.3125 to 0.3125
- inner_bias: float32 [4096], replicated, may hold values from -4 to 4
- outer_weight: bfloat16 [4096, 512], replicated, may hold values from -0.09375 to 0.09375
- outer_bias: float32 [512], replicated, may hold values from -4 to 4
- channel_weight: float32 [512], replicated, may hold values from 0.25 to 4
- counts: int32 [32], P(('group', 'tile')), may hold values from 1 to 512, as said below
- owner: int32 [16384, 1], P(('group', 'tile')), may hold values from 0 to 31; in each aligned block of 512 rows (0 to 511, 512 to 1023, ...) at most 32 rows name the same one
- column: int32 [16384], P(('group', 'tile')), may hold values from 0 to 127
Outputs:
- state_gradient: float32 [4096, 384], P(('group', 'tile'))
The draws below stay inside these ranges and needn't reach their ends.
Inputs may be any that keep to these rules, and one draw needn't show every extreme that they name: `counts`: the largest count equals 512 in every draw. Among the 512 slots of one tile at most 32 name one owner, a bound that some block reaches.
All inputs are finite; a program needn't handle non-finite values.
Results may differ from the reference program's by a relative error of at most 0.0035.
Values may be sent and summed in bfloat16 or wider, within the bound.
No kernel may reach another device: no remote copies, remote signals or barrier semaphores. Data moves between devices by JAX's collectives and lax.ppermute only.
A program may use at most 64 MiB of HBM per device.

```python
import math
import jax
import jax.numpy as jnp
import numpy as np
from jax import lax

HID = 4096
CH = 512
SND_DEV = 512
COL_DEV = 128
PROF = 384
MOST = 32
SOUNDINGS = 16384
N_TILE = 32


def draw_counts(key, part):
    key = jax.random.fold_in(key, 7)
    first, second = jax.random.split(key)
    halving = jax.random.randint(first, (N_TILE,), 0, 4)
    values = jnp.right_shift(jnp.full((N_TILE,), SND_DEV, jnp.int32), halving.astype(jnp.int32))
    fullest = jax.random.randint(second, (), 0, N_TILE)
    return values.at[fullest].set(SND_DEV).astype(jnp.int32)


def touch_ends(values, key, low, top_value):
    shape = values.shape
    place = [jax.random.randint(jax.random.fold_in(key, axis), (), 0, shape[axis]) for axis in range(len(shape))]
    values = values.at[tuple(place)].set(low)
    longest = shape.index(max(shape))
    place[longest] = (place[longest] + 1) % shape[longest]
    return values.at[tuple(place)].set(top_value)


def shard_levels(rng, dims, cuts, least, high):
    loudness = 1.0
    for position, shards_of in cuts:
        heights = jax.random.uniform(jax.random.fold_in(jax.random.fold_in(rng, 6), position), (shards_of,), jnp.float32, least / len(cuts), high / len(cuts))
        loudness = loudness * jnp.repeat(jnp.exp(heights), dims[position] // shards_of).reshape((-1,) + (1,) * (len(dims) - 1 - position))
    return loudness


def assign_block(rng, own, number, rows, number_of, top, bound, lean):
    ranking = jax.random.permutation(rng, number_of)
    packed, usual = load_shares(number_of, rows * top, bound, lean, True), load_shares(number_of, rows * top, bound, lean, False)
    places = jnp.arange(number_of)

    def named(lengths, turn):
        used = int((lengths > 0).sum())
        fixed = max(1, used // 4)
        moved = fixed + (places - fixed + turn * (used - fixed)) % max(1, number_of - fixed)
        return jnp.zeros((number_of,), jnp.int32).at[ranking[jnp.where(places < fixed, places, moved)]].set(jnp.asarray(lengths, jnp.int32))

    lengths = jnp.where(number % 4 == 0, named(packed, number // 4), named(usual, number - number // 4 - 1))
    mixed = jax.random.permutation(jax.random.fold_in(own, 3), number_of)
    source_of, receiver = mixed[0:number_of // 2 * 2:2], mixed[1:number_of // 2 * 2:2]
    room = jnp.minimum(lengths[source_of] - 1, bound - lengths[receiver]) // 2
    room = jnp.where((source_of == ranking[0]) | (receiver == ranking[0]) | (lengths[receiver] == 0), 0, jnp.maximum(room, 0))
    moved = jax.random.randint(jax.random.fold_in(own, 4), (number_of // 2,), 0, 1 << 20) % (room + 1)
    lengths = lengths.at[source_of].add(-moved).at[receiver].add(moved)
    items = jnp.searchsorted(jnp.cumsum(lengths), jnp.arange(rows * top), side="right").astype(jnp.int32)
    grid = items.reshape(top, rows).T
    grid = grid[jax.random.permutation(jax.random.fold_in(own, 1), rows)]
    turn = jax.random.randint(jax.random.fold_in(own, 2), (rows, 1), 0, top)
    return jnp.take_along_axis(grid, (jnp.arange(top)[None, :] + turn) % top, axis=1)


def load_shares(count, total, bound, skew, full):
    portions = [(1 << 20) // math.isqrt(rank ** skew) + 1 for rank in range(1, count + 1)]
    largest = bound if full else min(bound, max(-(-total // count), total * portions[0] // sum(portions)))
    least = 1 if total - largest >= count - 1 else 0
    given, spare = [largest] + [least] * (count - 1), total - largest - least * (count - 1)
    while spare > 0:
        free = [i for i in range(1, count) if given[i] < largest] or [i for i in range(1, count) if given[i] < bound]
        mass, remaining = sum([portions[i] for i in free]), spare
        for i in free:
            extra = min(bound - given[i], max(1, remaining * portions[i] // mass), spare)
            given[i] = given[i] + extra
            spare = spare - extra
    return np.array(given)


def gaussian(own_key, shape, scale, bound, cuts=(), held_as=jnp.bfloat16):
    array = scale * jax.random.normal(own_key, shape, jnp.float32)
    if cuts:
        array = array * shard_levels(own_key, shape, cuts, -0.22, 0.18)
    return jnp.clip(array, -bound, bound).astype(held_as)


def setup_inputs(seed: int = 0, part: int = 0) -> dict:
    splits = jax.random.split(jax.random.key(seed), 11)
    part_splits = jax.random.split(jax.random.fold_in(splits[10], part), 11)
    profiles = gaussian(part_splits[0], (SOUNDINGS, PROF), 1.0, 6.0, ((0, 32),))
    radiances = gaussian(part_splits[1], (SOUNDINGS, CH), 1.0, 6.0, ((0, 32),))
    inner_weight = gaussian(splits[2], (PROF, HID), PROF ** -0.5, 0.3125)
    inner_bias = gaussian(splits[3], (HID,), 0.7, 4.0, (), jnp.float32)
    outer_weight = gaussian(splits[4], (HID, CH), HID ** -0.5, 0.09375)
    outer_bias = gaussian(splits[5], (CH,), 1.0, 4.0, (), jnp.float32)
    channel_weight = jnp.clip(jnp.exp(jax.random.uniform(splits[6], (CH,), jnp.float32, math.log(0.25), math.log(4.0))), 0.25, 4.0)
    counts = draw_counts(jax.random.fold_in(jax.random.fold_in(splits[10], part), 71), part)
    owner_keys = jax.random.split(jax.random.fold_in(part_splits[8], 1), SOUNDINGS // SND_DEV)
    owner_turns = jax.random.permutation(jax.random.fold_in(part_splits[8], 3), SOUNDINGS // SND_DEV)
    owner = jax.vmap(lambda own, number: assign_block(jax.random.fold_in(part_splits[8], 2), own, number, SND_DEV, N_TILE, 1, MOST, 0))(owner_keys, owner_turns).reshape((SOUNDINGS, 1))
    column = touch_ends(jax.random.randint(part_splits[9], (SOUNDINGS,), 0, COL_DEV), jax.random.fold_in(part_splits[9], 1), 0, COL_DEV - 1).astype(jnp.int32)
    return {"profiles": profiles, "radiances": radiances, "inner_weight": inner_weight, "inner_bias": inner_bias, "outer_weight": outer_weight, "outer_bias": outer_bias, "channel_weight": channel_weight, "counts": counts, "owner": owner, "column": column}


def sounding_block(prof_rows, rad_rows, alive, inner_weight, inner_bias, outer_weight, outer_bias, channel_weight):
    preact = jnp.dot(prof_rows, inner_weight, preferred_element_type=jnp.float32) + inner_bias
    hidden = jax.nn.silu(preact).astype(jnp.bfloat16)
    output = jnp.dot(hidden, outer_weight, preferred_element_type=jnp.float32) + outer_bias
    misfit = jnp.where(alive[:, None], channel_weight * (output - rad_rows.astype(jnp.float32)), 0.0).astype(jnp.bfloat16)
    back = lax.dot_general(misfit, outer_weight, (((1,), (1,)), ((), ())), preferred_element_type=jnp.float32)
    sigma = jax.nn.sigmoid(preact)
    slope = (back * sigma * (1.0 + preact * (1.0 - sigma))).astype(jnp.bfloat16)
    return lax.dot_general(slope, inner_weight, (((1,), (1,)), ((), ())), preferred_element_type=jnp.float32)


def reference(profiles, radiances, inner_weight, inner_bias, outer_weight, outer_bias, channel_weight, counts, owner, column):
    width = profiles.shape[1]
    tile_prof = profiles.reshape(N_TILE, SND_DEV, width)
    tile_rad = radiances.reshape(N_TILE, SND_DEV, radiances.shape[1])

    def one_tile(items):
        prof_rows, rad_rows, count = items
        alive = jnp.arange(SND_DEV, dtype=jnp.int32) < count
        return sounding_block(prof_rows, rad_rows, alive, inner_weight, inner_bias, outer_weight, outer_bias, channel_weight)

    grad_rows = lax.map(one_tile, (tile_prof, tile_rad, counts)).reshape(N_TILE * SND_DEV, width)
    target = (owner[:, 0] * COL_DEV + column).astype(jnp.int32)
    total = jnp.zeros((COL_DEV * N_TILE, width), jnp.float32)
    return total.at[target].add(grad_rows)
```

```python
import functools

import jax
import jax.numpy as jnp
from jax import lax
from jax.experimental import pallas as pl
from jax.experimental.pallas import tpu as pltpu
from jax.sharding import PartitionSpec as P

COL_DEV = 128
CHUNK = 512
NT = (((1,), (1,)), ((), ()))


def rows_kernel(
    most,
    count_ref,
    code_ref,
    prof_ref,
    rad_ref,
    w1_hbm,
    b1_ref,
    w2_hbm,
    b2_ref,
    cw_ref,
    out_ref,
    w1_ref,
    w2_ref,
    factor_ref,
    sem1,
    sem2,
):
    rows, width = prof_ref.shape
    hid = w1_ref.shape[1]
    chunks = hid // CHUNK
    copies = []
    for i in range(chunks):
        part = pl.ds(i * CHUNK, CHUNK)
        one = pltpu.make_async_copy(w1_hbm.at[:, part], w1_ref.at[:, part], sem1.at[i])
        two = pltpu.make_async_copy(w2_hbm.at[part, :], w2_ref.at[part, :], sem2.at[i])
        one.start()
        two.start()
        copies.append((one, two))

    code = code_ref[...]
    owner = lax.shift_right_arithmetic(code, 7)
    slots = out_ref.shape[0]
    tiles = slots // most
    one_hot = (lax.broadcasted_iota(jnp.int32, (tiles, rows), 0) == owner).astype(jnp.float32)
    upper = (
        lax.broadcasted_iota(jnp.int32, (rows, rows), 0)
        <= lax.broadcasted_iota(jnp.int32, (rows, rows), 1)
    ).astype(jnp.float32)
    running = jnp.dot(
        one_hot.astype(jnp.bfloat16),
        upper.astype(jnp.bfloat16),
        preferred_element_type=jnp.float32,
    )
    rank = jnp.sum(running * one_hot, axis=0, keepdims=True).astype(jnp.int32) - 1
    slot = jnp.where(code < 0, -1, owner * most + rank)
    placing = (
        (lax.broadcasted_iota(jnp.int32, (slots, rows), 0) == slot)
        .astype(jnp.float32)
        .astype(jnp.bfloat16)
    )

    prof = prof_ref[...]
    output = jnp.zeros((rows, rad_ref.shape[1]), jnp.float32)
    for i in range(chunks):
        part = pl.ds(i * CHUNK, CHUNK)
        copies[i][0].wait()
        preact = jnp.dot(prof, w1_ref[:, part], preferred_element_type=jnp.float32)
        preact = preact + b1_ref[:, part]
        sigma = 0.5 * jnp.tanh(0.5 * preact) + 0.5
        hidden = preact * sigma
        factor_ref[:, part] = sigma + hidden * (1.0 - sigma)
        copies[i][1].wait()
        output += jnp.dot(
            hidden.astype(jnp.bfloat16), w2_ref[part, :], preferred_element_type=jnp.float32
        )
    alive = lax.broadcasted_iota(jnp.int32, (rows, 1), 0) < count_ref[0]
    misfit = cw_ref[...] * (output + b2_ref[...] - rad_ref[...].astype(jnp.float32))
    misfit = jnp.where(alive, misfit, 0.0).astype(jnp.bfloat16)
    grads = jnp.zeros((rows, width), jnp.float32)
    for i in range(chunks):
        part = pl.ds(i * CHUNK, CHUNK)
        back = lax.dot_general(misfit, w2_ref[part, :], NT, preferred_element_type=jnp.float32)
        slope = (back * factor_ref[:, part]).astype(jnp.bfloat16)
        grads += lax.dot_general(slope, w1_ref[:, part], NT, preferred_element_type=jnp.float32)
    out_ref[...] = jnp.dot(
        placing, grads.astype(jnp.bfloat16), preferred_element_type=jnp.float32
    ).astype(jnp.bfloat16)


def selector_kernel(most, me_ref, codes_ref, out_ref):
    tiles, rows = codes_ref.shape
    me = me_ref[0]
    upper = (
        (
            lax.broadcasted_iota(jnp.int32, (rows, rows), 0)
            <= lax.broadcasted_iota(jnp.int32, (rows, rows), 1)
        )
        .astype(jnp.float32)
        .astype(jnp.bfloat16)
    )
    codes = codes_ref[...]
    mine = (lax.shift_right_arithmetic(codes, 7) == me).astype(jnp.float32)
    rank = (
        jnp.dot(mine.astype(jnp.bfloat16), upper, preferred_element_type=jnp.float32) * mine
    ).astype(jnp.int32) - 1
    column = jnp.where(mine > 0.0, codes & (COL_DEV - 1), -1)
    for t in range(tiles):
        col_hot = (
            (lax.broadcasted_iota(jnp.int32, (COL_DEV, rows), 0) == column[t : t + 1, :])
            .astype(jnp.float32)
            .astype(jnp.bfloat16)
        )
        rank_hot = (
            (lax.broadcasted_iota(jnp.int32, (most, rows), 0) == rank[t : t + 1, :])
            .astype(jnp.float32)
            .astype(jnp.bfloat16)
        )
        out_ref[:, t * most : (t + 1) * most] = lax.dot_general(
            col_hot, rank_hot, NT, preferred_element_type=jnp.float32
        ).astype(jnp.bfloat16)


def per_device(
    profiles,
    radiances,
    inner_weight,
    inner_bias,
    outer_weight,
    outer_bias,
    channel_weight,
    counts,
    owner,
    column,
):
    tiles = lax.axis_size("tile")
    rows, width = profiles.shape
    hid = inner_weight.shape[1]
    chan = radiances.shape[1]
    most = max(2, 2 * rows // tiles)
    slots = tiles * most
    chunks = hid // CHUNK
    alive = jnp.arange(rows, dtype=jnp.int32) < counts[0]
    code = jnp.where(alive, owner[:, 0] * COL_DEV + column, -1)
    codes = lax.all_gather(code, "tile", axis=0, tiled=False)
    vmem = pl.BlockSpec(memory_space=pltpu.VMEM)
    smem = pl.BlockSpec(memory_space=pltpu.SMEM)
    anywhere = pl.BlockSpec(memory_space=pl.ANY)
    flops = 4 * rows * hid * (width + chan)
    bucket = pl.pallas_call(
        functools.partial(rows_kernel, most),
        out_shape=jax.ShapeDtypeStruct((slots, width), jnp.bfloat16),
        in_specs=[smem, vmem, vmem, vmem, anywhere, vmem, anywhere, vmem, vmem],
        out_specs=vmem,
        scratch_shapes=[
            pltpu.VMEM((width, hid), jnp.bfloat16),
            pltpu.VMEM((hid, chan), jnp.bfloat16),
            pltpu.VMEM((rows, hid), jnp.float32),
            pltpu.SemaphoreType.DMA((chunks,)),
            pltpu.SemaphoreType.DMA((chunks,)),
        ],
        compiler_params=pltpu.CompilerParams(vmem_limit_bytes=48 * 1024 * 1024),
        cost_estimate=pl.CostEstimate(flops=flops, bytes_accessed=9 << 20, transcendentals=0),
        name="rows_kernel",
    )(
        counts,
        code.reshape(1, rows),
        profiles,
        radiances,
        inner_weight,
        inner_bias.reshape(1, hid),
        outer_weight,
        outer_bias.reshape(1, chan),
        channel_weight.reshape(1, chan),
    )
    got = lax.all_to_all(bucket, "tile", split_axis=0, concat_axis=0, tiled=True)
    me = lax.axis_index("tile").astype(jnp.int32).reshape(1)
    selector = pl.pallas_call(
        functools.partial(selector_kernel, most),
        out_shape=jax.ShapeDtypeStruct((COL_DEV, slots), jnp.bfloat16),
        in_specs=[smem, vmem],
        out_specs=vmem,
        compiler_params=pltpu.CompilerParams(vmem_limit_bytes=16 * 1024 * 1024),
        cost_estimate=pl.CostEstimate(flops=1 << 30, bytes_accessed=1 << 20, transcendentals=0),
        name="selector_kernel",
    )(me, codes)
    return jnp.dot(selector, got, preferred_element_type=jnp.float32)


def solution(mesh):
    placed = (
        P(("group", "tile"), None),
        P(("group", "tile"), None),
        P(),
        P(),
        P(),
        P(),
        P(),
        P(("group", "tile")),
        P(("group", "tile"), None),
        P(("group", "tile")),
    )
    return jax.shard_map(
        per_device,
        mesh=mesh,
        in_specs=placed,
        out_specs=P(("group", "tile"), None),
        check_vma=False,
    )
```

```python
import functools

import jax
import jax.numpy as jnp
from jax import lax
from jax.experimental import pallas as pl
from jax.experimental.pallas import tpu as pltpu
from jax.sharding import PartitionSpec as P

COL_DEV = 128
CHUNK = 512
LANES = 128
LABEL_ROWS = 8
NT = (((1,), (1,)), ((), ()))


def as_bf16(mask):
    return mask.astype(jnp.float32).astype(jnp.bfloat16)


def rows_kernel(
    most,
    me_ref,
    count_ref,
    owner_ref,
    column_ref,
    prof_hbm,
    rad_hbm,
    w1_hbm,
    b1_hbm,
    w2_hbm,
    b2_hbm,
    cw_hbm,
    out_ref,
    prof_ref,
    rad_ref,
    w1_ref,
    b1_ref,
    w2_ref,
    b2_ref,
    cw_ref,
    hidden_ref,
    factor_ref,
    sems,
):
    rows, width = prof_ref.shape
    hid = w1_ref.shape[1]
    chan = rad_ref.shape[1]
    half = hid // 2
    low, high = pl.ds(0, half), pl.ds(half, half)
    pairs = (
        (prof_hbm, prof_ref),
        (b1_hbm, b1_ref),
        (w1_hbm.at[:, low], w1_ref.at[:, low]),
        (w1_hbm.at[:, high], w1_ref.at[:, high]),
        (w2_hbm, w2_ref),
        (rad_hbm, rad_ref),
        (b2_hbm, b2_ref),
        (cw_hbm, cw_ref),
    )
    copies = [
        pltpu.make_async_copy(src, dst, sems.at[i]) for i, (src, dst) in enumerate(pairs)
    ]
    for copy in copies:
        copy.start()

    tiles = out_ref.shape[0]
    slots = tiles * most
    live = lax.broadcasted_iota(jnp.int32, (1, rows), 1) < count_ref[0]
    owner = jnp.where(live, owner_ref[...], -1)
    mine = lax.broadcasted_iota(jnp.int32, (tiles, rows), 0) == owner
    one_hot = mine.astype(jnp.float32)
    upper = as_bf16(
        lax.broadcasted_iota(jnp.int32, (rows, rows), 0)
        <= lax.broadcasted_iota(jnp.int32, (rows, rows), 1)
    )
    running = jnp.dot(one_hot.astype(jnp.bfloat16), upper, preferred_element_type=jnp.float32)
    rank = jnp.sum(running * one_hot, axis=0, keepdims=True).astype(jnp.int32) - 1
    slot = jnp.where(live, owner * most + rank, -1)
    placing = as_bf16(lax.broadcasted_iota(jnp.int32, (slots, rows), 0) == slot)
    lane = rank + lax.rem(me_ref[0], LANES // most) * most
    lane_hot = as_bf16(lax.broadcasted_iota(jnp.int32, (LANES, rows), 0) == lane)
    marked = jnp.where(mine, (column_ref[...] + 1).astype(jnp.float32), 0.0)
    labels = lax.dot_general(
        marked.astype(jnp.bfloat16), lane_hot, NT, preferred_element_type=jnp.float32
    )

    copies[0].wait()
    copies[1].wait()
    prof = (prof_ref[...].astype(jnp.float32) * 0.5).astype(jnp.bfloat16)
    for i in range(hid // CHUNK):
        part = pl.ds(i * CHUNK, CHUNK)
        if i == 0:
            copies[2].wait()
        if i == hid // CHUNK // 2:
            copies[3].wait()
        u = jnp.dot(prof, w1_ref[:, part], preferred_element_type=jnp.float32)
        u = u + 0.5 * b1_ref[:, part]
        p = jnp.tanh(u) + 1.0
        hidden = u * p
        hidden_ref[:, part] = hidden.astype(jnp.bfloat16)
        factor_ref[:, part] = p + hidden * (2.0 - p)
    for copy in copies[4:]:
        copy.wait()
    output = jnp.dot(hidden_ref[...], w2_ref[...], preferred_element_type=jnp.float32)
    misfit = (0.5 * cw_ref[...]) * (output + b2_ref[...] - rad_ref[...].astype(jnp.float32))
    alive = lax.broadcasted_iota(jnp.int32, (rows, 1), 0) < count_ref[0]
    misfit = jnp.where(alive, misfit, 0.0).astype(jnp.bfloat16)
    for i in range(hid // CHUNK):
        part = pl.ds(i * CHUNK, CHUNK)
        back = lax.dot_general(misfit, w2_ref[part, :], NT, preferred_element_type=jnp.float32)
        hidden_ref[:, part] = (back * factor_ref[:, part]).astype(jnp.bfloat16)
    grads = lax.dot_general(
        hidden_ref[...], w1_ref[...], NT, preferred_element_type=jnp.float32
    ).astype(jnp.bfloat16)
    placed = jnp.dot(placing, grads, preferred_element_type=jnp.float32).astype(jnp.bfloat16)
    parts = width // LANES
    for k in range(parts):
        out_ref[:, k * most : (k + 1) * most, :] = placed[
            :, k * LANES : (k + 1) * LANES
        ].reshape(tiles, most, LANES)
    out_ref[:, parts * most :, :] = jnp.broadcast_to(
        labels.reshape(tiles, 1, LANES), (tiles, LABEL_ROWS, LANES)
    ).astype(jnp.bfloat16)


def sums_kernel(most, got_ref, out_ref):
    tiles = got_ref.shape[0]
    parts = out_ref.shape[1] // LANES
    group = LANES // most
    marks = got_ref[:, parts * most :, :].astype(jnp.float32)[:, 0, :]
    index = lax.broadcasted_iota(jnp.int32, (COL_DEV, LANES), 0) + 1
    total = [jnp.zeros((COL_DEV, LANES), jnp.float32) for _ in range(parts)]
    for g in range(tiles // group):
        label = jnp.sum(marks[g * group : (g + 1) * group], axis=0, keepdims=True)
        chosen = as_bf16(index == label.astype(jnp.int32))
        for k in range(parts):
            block = got_ref[g * group : (g + 1) * group, k * most : (k + 1) * most, :]
            total[k] += jnp.dot(
                chosen, block.reshape(LANES, LANES), preferred_element_type=jnp.float32
            )
    for k in range(parts):
        out_ref[:, k * LANES : (k + 1) * LANES] = total[k]


def per_device(
    profiles,
    radiances,
    inner_weight,
    inner_bias,
    outer_weight,
    outer_bias,
    channel_weight,
    counts,
    owner,
    column,
):
    tiles = lax.axis_size("tile")
    rows, width = profiles.shape
    hid = inner_weight.shape[1]
    chan = radiances.shape[1]
    most = max(2, 2 * rows // tiles)
    high = width // LANES * most + LABEL_ROWS
    vmem = pl.BlockSpec(memory_space=pltpu.VMEM)
    smem = pl.BlockSpec(memory_space=pltpu.SMEM)
    anywhere = pl.BlockSpec(memory_space=pl.ANY)
    me = lax.axis_index("tile").astype(jnp.int32).reshape(1)
    bucket = pl.pallas_call(
        functools.partial(rows_kernel, most),
        out_shape=jax.ShapeDtypeStruct((tiles, high, LANES), jnp.bfloat16),
        in_specs=[smem, smem, vmem, vmem] + [anywhere] * 7,
        out_specs=vmem,
        scratch_shapes=[
            pltpu.VMEM((rows, width), jnp.bfloat16),
            pltpu.VMEM((rows, chan), jnp.bfloat16),
            pltpu.VMEM((width, hid), jnp.bfloat16),
            pltpu.VMEM((1, hid), jnp.float32),
            pltpu.VMEM((hid, chan), jnp.bfloat16),
            pltpu.VMEM((1, chan), jnp.float32),
            pltpu.VMEM((1, chan), jnp.float32),
            pltpu.VMEM((rows, hid), jnp.bfloat16),
            pltpu.VMEM((rows, hid), jnp.float32),
            pltpu.SemaphoreType.DMA((8,)),
        ],
        compiler_params=pltpu.CompilerParams(vmem_limit_bytes=60 * 1024 * 1024),
        name="rows_kernel",
    )(
        me,
        counts,
        owner.reshape(1, rows),
        column.reshape(1, rows),
        profiles,
        radiances,
        inner_weight,
        inner_bias.reshape(1, hid),
        outer_weight,
        outer_bias.reshape(1, chan),
        channel_weight.reshape(1, chan),
    )
    got = lax.all_to_all(bucket, "tile", split_axis=0, concat_axis=0, tiled=True)
    return pl.pallas_call(
        functools.partial(sums_kernel, most),
        out_shape=jax.ShapeDtypeStruct((COL_DEV, width), jnp.float32),
        in_specs=[vmem],
        out_specs=vmem,
        compiler_params=pltpu.CompilerParams(vmem_limit_bytes=16 * 1024 * 1024),
        name="sums_kernel",
    )(got)


def solution(mesh):
    placed = (
        P(("group", "tile"), None),
        P(("group", "tile"), None),
        P(),
        P(),
        P(),
        P(),
        P(),
        P(("group", "tile")),
        P(("group", "tile"), None),
        P(("group", "tile")),
    )
    return jax.shard_map(
        per_device,
        mesh=mesh,
        in_specs=placed,
        out_specs=P(("group", "tile"), None),
        check_vma=False,
    )
```

```python
import functools

import jax
import jax.numpy as jnp
from jax import lax
from jax.experimental import pallas as pl
from jax.experimental.pallas import tpu as pltpu
from jax.sharding import PartitionSpec as P

COL_DEV = 128
CHUNK = 512
LANES = 128
LABEL_ROWS = 8
INNER = 8
NT = (((1,), (1,)), ((), ()))


def as_bf16(mask):
    return mask.astype(jnp.float32).astype(jnp.bfloat16)


def rows_kernel(
    tiles,
    most,
    count_ref,
    owner_ref,
    column_ref,
    prof_hbm,
    rad_hbm,
    w1_hbm,
    b1_hbm,
    w2_hbm,
    b2_hbm,
    cw_hbm,
    out_ref,
    prof_ref,
    rad_ref,
    w1_ref,
    b1_ref,
    w2_ref,
    b2_ref,
    cw_ref,
    hidden_ref,
    factor_ref,
    sems,
):
    rows, width = prof_ref.shape
    hid = w1_ref.shape[1]
    chan = rad_ref.shape[1]
    half = hid // 2
    low, high = pl.ds(0, half), pl.ds(half, half)
    pairs = (
        (prof_hbm, prof_ref),
        (b1_hbm, b1_ref),
        (w1_hbm.at[:, low], w1_ref.at[:, low]),
        (w1_hbm.at[:, high], w1_ref.at[:, high]),
        (w2_hbm, w2_ref),
        (rad_hbm, rad_ref),
        (b2_hbm, b2_ref),
        (cw_hbm, cw_ref),
    )
    copies = [
        pltpu.make_async_copy(src, dst, sems.at[i]) for i, (src, dst) in enumerate(pairs)
    ]
    for copy in copies:
        copy.start()

    inner = out_ref.shape[0]
    live = lax.broadcasted_iota(jnp.int32, (1, rows), 1) < count_ref[0]
    owner = jnp.where(live, owner_ref[...], -1)
    mine = lax.broadcasted_iota(jnp.int32, (tiles, rows), 0) == owner
    one_hot = mine.astype(jnp.float32)
    upper = as_bf16(
        lax.broadcasted_iota(jnp.int32, (rows, rows), 0)
        <= lax.broadcasted_iota(jnp.int32, (rows, rows), 1)
    )
    running = jnp.dot(one_hot.astype(jnp.bfloat16), upper, preferred_element_type=jnp.float32)
    rank = jnp.sum(running * one_hot, axis=0, keepdims=True).astype(jnp.int32) - 1
    place = owner & (inner - 1)
    lane = lax.shift_right_arithmetic(owner, inner.bit_length() - 1) * most + rank
    slot = jnp.where(live, place * LANES + lane, -1)
    placing = as_bf16(lax.broadcasted_iota(jnp.int32, (inner * LANES, rows), 0) == slot)
    lane_hot = as_bf16(lax.broadcasted_iota(jnp.int32, (LANES, rows), 0) == lane)
    here = live & (lax.broadcasted_iota(jnp.int32, (inner, rows), 0) == place)
    marked = jnp.where(here, (column_ref[...] + 1).astype(jnp.float32), 0.0)
    labels = lax.dot_general(
        marked.astype(jnp.bfloat16), lane_hot, NT, preferred_element_type=jnp.float32
    )

    copies[0].wait()
    copies[1].wait()
    prof = (prof_ref[...].astype(jnp.float32) * 0.5).astype(jnp.bfloat16)
    for i in range(hid // CHUNK):
        part = pl.ds(i * CHUNK, CHUNK)
        if i == 0:
            copies[2].wait()
        if i == hid // CHUNK // 2:
            copies[3].wait()
        u = jnp.dot(prof, w1_ref[:, part], preferred_element_type=jnp.float32)
        u = u + 0.5 * b1_ref[:, part]
        p = jnp.tanh(u) + 1.0
        hidden = u * p
        hidden_ref[:, part] = hidden.astype(jnp.bfloat16)
        factor_ref[:, part] = p + hidden * (2.0 - p)
    for copy in copies[4:]:
        copy.wait()
    output = jnp.dot(hidden_ref[...], w2_ref[...], preferred_element_type=jnp.float32)
    misfit = (0.5 * cw_ref[...]) * (output + b2_ref[...] - rad_ref[...].astype(jnp.float32))
    alive = lax.broadcasted_iota(jnp.int32, (rows, 1), 0) < count_ref[0]
    misfit = jnp.where(alive, misfit, 0.0).astype(jnp.bfloat16)
    for i in range(hid // CHUNK):
        part = pl.ds(i * CHUNK, CHUNK)
        back = lax.dot_general(misfit, w2_ref[part, :], NT, preferred_element_type=jnp.float32)
        hidden_ref[:, part] = (back * factor_ref[:, part]).astype(jnp.bfloat16)
    grads = lax.dot_general(
        hidden_ref[...], w1_ref[...], NT, preferred_element_type=jnp.float32
    ).astype(jnp.bfloat16)
    placed = jnp.dot(placing, grads, preferred_element_type=jnp.float32).astype(jnp.bfloat16)
    parts = width // LANES
    for k in range(parts):
        out_ref[:, k * LANES : (k + 1) * LANES, :] = placed[
            :, k * LANES : (k + 1) * LANES
        ].reshape(inner, LANES, LANES)
    out_ref[:, parts * LANES :, :] = jnp.broadcast_to(
        labels.reshape(inner, 1, LANES), (inner, LABEL_ROWS, LANES)
    ).astype(jnp.bfloat16)


def blocks_kernel(most, me_ref, got_ref, *out_refs):
    inner = got_ref.shape[0]
    outer = len(out_refs)
    parts = out_refs[0].shape[1] // LANES
    marks = got_ref[:, parts * LANES :, :].astype(jnp.float32)[:, 0, :].astype(jnp.int32)
    lane = lax.broadcasted_iota(jnp.int32, (inner, LANES), 1)
    turn = lax.shift_right_arithmetic(lane, most.bit_length() - 1) - me_ref[0]
    turn = jnp.where(turn < 0, turn + outer, turn)
    code = jnp.where(marks > 0, turn * COL_DEV + marks - 1, -1)
    index = lax.broadcasted_iota(jnp.int32, (outer * COL_DEV, LANES), 0)
    chosen = jnp.concatenate(
        [as_bf16(index == code[s : s + 1, :]) for s in range(inner)], axis=1
    )
    for k in range(parts):
        block = got_ref[:, k * LANES : (k + 1) * LANES, :].reshape(inner * LANES, LANES)
        total = jnp.dot(chosen, block, preferred_element_type=jnp.float32)
        for d in range(outer):
            out_refs[d][:, k * LANES : (k + 1) * LANES] = total[
                d * COL_DEV : (d + 1) * COL_DEV
            ].astype(jnp.bfloat16)


def per_device(
    profiles,
    radiances,
    inner_weight,
    inner_bias,
    outer_weight,
    outer_bias,
    channel_weight,
    counts,
    owner,
    column,
):
    tiles = lax.axis_size("tile")
    rows, width = profiles.shape
    hid = inner_weight.shape[1]
    chan = radiances.shape[1]
    most = max(2, 2 * rows // tiles)
    inner = INNER
    outer = tiles // inner
    high = width + LABEL_ROWS
    vmem = pl.BlockSpec(memory_space=pltpu.VMEM)
    smem = pl.BlockSpec(memory_space=pltpu.SMEM)
    anywhere = pl.BlockSpec(memory_space=pl.ANY)
    bucket = pl.pallas_call(
        functools.partial(rows_kernel, tiles, most),
        out_shape=jax.ShapeDtypeStruct((inner, high, LANES), jnp.bfloat16),
        in_specs=[smem, vmem, vmem] + [anywhere] * 7,
        out_specs=vmem,
        scratch_shapes=[
            pltpu.VMEM((rows, width), jnp.bfloat16),
            pltpu.VMEM((rows, chan), jnp.bfloat16),
            pltpu.VMEM((width, hid), jnp.bfloat16),
            pltpu.VMEM((1, hid), jnp.float32),
            pltpu.VMEM((hid, chan), jnp.bfloat16),
            pltpu.VMEM((1, chan), jnp.float32),
            pltpu.VMEM((1, chan), jnp.float32),
            pltpu.VMEM((rows, hid), jnp.bfloat16),
            pltpu.VMEM((rows, hid), jnp.float32),
            pltpu.SemaphoreType.DMA((8,)),
        ],
        compiler_params=pltpu.CompilerParams(vmem_limit_bytes=60 * 1024 * 1024),
        name="rows_kernel",
    )(
        counts,
        owner.reshape(1, rows),
        column.reshape(1, rows),
        profiles,
        radiances,
        inner_weight,
        inner_bias.reshape(1, hid),
        outer_weight,
        outer_bias.reshape(1, chan),
        channel_weight.reshape(1, chan),
    )
    planes = [[o * inner + i for i in range(inner)] for o in range(outer)]
    got = lax.all_to_all(
        bucket, "tile", split_axis=0, concat_axis=0, axis_index_groups=planes, tiled=True
    )
    me = lax.div(lax.axis_index("tile"), inner).astype(jnp.int32).reshape(1)
    blocks = pl.pallas_call(
        functools.partial(blocks_kernel, most),
        out_shape=[jax.ShapeDtypeStruct((COL_DEV, width), jnp.bfloat16)] * outer,
        in_specs=[smem, vmem],
        out_specs=[vmem] * outer,
        compiler_params=pltpu.CompilerParams(vmem_limit_bytes=24 * 1024 * 1024),
        name="blocks_kernel",
    )(me, got)
    total = blocks[0].astype(jnp.float32)
    for d in range(1, outer):
        pairs = [(t, (t + d * inner) % tiles) for t in range(tiles)]
        total = total + lax.ppermute(blocks[d], "tile", pairs).astype(jnp.float32)
    return total


def solution(mesh):
    placed = (
        P(("group", "tile"), None),
        P(("group", "tile"), None),
        P(),
        P(),
        P(),
        P(),
        P(),
        P(("group", "tile")),
        P(("group", "tile"), None),
        P(("group", "tile")),
    )
    return jax.shard_map(
        per_device,
        mesh=mesh,
        in_specs=placed,
        out_specs=P(("group", "tile"), None),
        check_vma=False,
    )
```

```python
import functools

import jax
import jax.numpy as jnp
from jax import lax
from jax.experimental import pallas as pl
from jax.experimental.pallas import tpu as pltpu
from jax.sharding import PartitionSpec as P

COL_DEV = 128
CHUNK = 512
LANES = 128
LABEL_ROWS = 8
OUTER = 2
NT = (((1,), (1,)), ((), ()))


def as_bf16(mask):
    return mask.astype(jnp.float32).astype(jnp.bfloat16)


def rows_kernel(
    tiles,
    most,
    me_ref,
    count_ref,
    owner_ref,
    column_ref,
    prof_hbm,
    rad_hbm,
    w1_hbm,
    b1_hbm,
    w2_hbm,
    b2_hbm,
    cw_hbm,
    out_ref,
    prof_ref,
    rad_ref,
    w1_ref,
    b1_ref,
    w2_ref,
    b2_ref,
    cw_ref,
    hidden_ref,
    factor_ref,
    sems,
):
    rows, width = prof_ref.shape
    hid = w1_ref.shape[1]
    chan = rad_ref.shape[1]
    half = hid // 2
    low, high = pl.ds(0, half), pl.ds(half, half)
    pairs = (
        (prof_hbm, prof_ref),
        (b1_hbm, b1_ref),
        (w1_hbm.at[:, low], w1_ref.at[:, low]),
        (w1_hbm.at[:, high], w1_ref.at[:, high]),
        (w2_hbm, w2_ref),
        (rad_hbm, rad_ref),
        (b2_hbm, b2_ref),
        (cw_hbm, cw_ref),
    )
    copies = [
        pltpu.make_async_copy(src, dst, sems.at[i]) for i, (src, dst) in enumerate(pairs)
    ]
    for copy in copies:
        copy.start()

    inner = out_ref.shape[0]
    live = lax.broadcasted_iota(jnp.int32, (1, rows), 1) < count_ref[0]
    owner = jnp.where(live, owner_ref[...], -1)
    mine = lax.broadcasted_iota(jnp.int32, (tiles, rows), 0) == owner
    one_hot = mine.astype(jnp.float32)
    upper = as_bf16(
        lax.broadcasted_iota(jnp.int32, (rows, rows), 0)
        <= lax.broadcasted_iota(jnp.int32, (rows, rows), 1)
    )
    running = jnp.dot(one_hot.astype(jnp.bfloat16), upper, preferred_element_type=jnp.float32)
    rank = jnp.sum(running * one_hot, axis=0, keepdims=True).astype(jnp.int32) - 1
    pool = tiles // inner * most
    place = owner & (inner - 1)
    order = lax.shift_right_arithmetic(owner, inner.bit_length() - 1) * most + rank
    slot = jnp.where(live, place * pool + order, -1)
    placing = as_bf16(lax.broadcasted_iota(jnp.int32, (inner * pool, rows), 0) == slot)
    lane = order + lax.rem(me_ref[0], LANES // pool) * pool
    lane_hot = as_bf16(lax.broadcasted_iota(jnp.int32, (LANES, rows), 0) == lane)
    here = live & (lax.broadcasted_iota(jnp.int32, (inner, rows), 0) == place)
    marked = jnp.where(here, (column_ref[...] + 1).astype(jnp.float32), 0.0)
    labels = lax.dot_general(
        marked.astype(jnp.bfloat16), lane_hot, NT, preferred_element_type=jnp.float32
    )

    copies[0].wait()
    copies[1].wait()
    prof = (prof_ref[...].astype(jnp.float32) * 0.5).astype(jnp.bfloat16)
    for i in range(hid // CHUNK):
        part = pl.ds(i * CHUNK, CHUNK)
        if i == 0:
            copies[2].wait()
        if i == hid // CHUNK // 2:
            copies[3].wait()
        u = jnp.dot(prof, w1_ref[:, part], preferred_element_type=jnp.float32)
        u = u + 0.5 * b1_ref[:, part]
        p = jnp.tanh(u) + 1.0
        hidden = u * p
        hidden_ref[:, part] = hidden.astype(jnp.bfloat16)
        factor_ref[:, part] = p + hidden * (2.0 - p)
    for copy in copies[4:]:
        copy.wait()
    output = jnp.dot(hidden_ref[...], w2_ref[...], preferred_element_type=jnp.float32)
    misfit = (0.5 * cw_ref[...]) * (output + b2_ref[...] - rad_ref[...].astype(jnp.float32))
    alive = lax.broadcasted_iota(jnp.int32, (rows, 1), 0) < count_ref[0]
    misfit = jnp.where(alive, misfit, 0.0).astype(jnp.bfloat16)
    for i in range(hid // CHUNK):
        part = pl.ds(i * CHUNK, CHUNK)
        back = lax.dot_general(misfit, w2_ref[part, :], NT, preferred_element_type=jnp.float32)
        hidden_ref[:, part] = (back * factor_ref[:, part]).astype(jnp.bfloat16)
    grads = lax.dot_general(
        hidden_ref[...], w1_ref[...], NT, preferred_element_type=jnp.float32
    ).astype(jnp.bfloat16)
    placed = jnp.dot(placing, grads, preferred_element_type=jnp.float32).astype(jnp.bfloat16)
    parts = width // LANES
    for k in range(parts):
        out_ref[:, k * pool : (k + 1) * pool, :] = placed[
            :, k * LANES : (k + 1) * LANES
        ].reshape(inner, pool, LANES)
    out_ref[:, parts * pool :, :] = jnp.broadcast_to(
        labels.reshape(inner, 1, LANES), (inner, LABEL_ROWS, LANES)
    ).astype(jnp.bfloat16)


def blocks_kernel(tiles, most, me_ref, got_ref, own_ref, other_ref):
    inner = got_ref.shape[0]
    outer = tiles // inner
    pool = outer * most
    group = LANES // pool
    parts = own_ref.shape[1] // LANES
    marks = got_ref[:, parts * pool :, :].astype(jnp.float32)[:, 0, :]
    index = lax.broadcasted_iota(jnp.int32, (outer * COL_DEV, LANES), 0)
    lane = lax.broadcasted_iota(jnp.int32, (1, LANES), 1) & (pool - 1)
    turn = lax.shift_right_arithmetic(lane, most.bit_length() - 1) ^ (
        lax.shift_right_arithmetic(me_ref[0], inner.bit_length() - 1)
    )
    chosen = []
    for g in range(inner // group):
        label = jnp.sum(marks[g * group : (g + 1) * group], axis=0, keepdims=True)
        label = label.astype(jnp.int32)
        code = jnp.where(label > 0, turn * COL_DEV + label - 1, -1)
        chosen.append(as_bf16(index == code))
    chosen = jnp.concatenate(chosen, axis=1)
    for k in range(parts):
        block = got_ref[:, k * pool : (k + 1) * pool, :].reshape(inner * pool, LANES)
        total = jnp.dot(chosen, block, preferred_element_type=jnp.float32)
        own_ref[:, k * LANES : (k + 1) * LANES] = total[:COL_DEV]
        other_ref[:, k * LANES : (k + 1) * LANES] = total[COL_DEV:].astype(jnp.bfloat16)


def per_device(
    profiles,
    radiances,
    inner_weight,
    inner_bias,
    outer_weight,
    outer_bias,
    channel_weight,
    counts,
    owner,
    column,
):
    tiles = lax.axis_size("tile")
    rows, width = profiles.shape
    hid = inner_weight.shape[1]
    chan = radiances.shape[1]
    most = max(2, 2 * rows // tiles)
    inner = tiles // OUTER
    pool = OUTER * most
    high = width // LANES * pool + LABEL_ROWS
    me = lax.axis_index("tile").astype(jnp.int32).reshape(1)
    vmem = pl.BlockSpec(memory_space=pltpu.VMEM)
    smem = pl.BlockSpec(memory_space=pltpu.SMEM)
    anywhere = pl.BlockSpec(memory_space=pl.ANY)
    bucket = pl.pallas_call(
        functools.partial(rows_kernel, tiles, most),
        out_shape=jax.ShapeDtypeStruct((inner, high, LANES), jnp.bfloat16),
        in_specs=[smem, smem, vmem, vmem] + [anywhere] * 7,
        out_specs=vmem,
        scratch_shapes=[
            pltpu.VMEM((rows, width), jnp.bfloat16),
            pltpu.VMEM((rows, chan), jnp.bfloat16),
            pltpu.VMEM((width, hid), jnp.bfloat16),
            pltpu.VMEM((1, hid), jnp.float32),
            pltpu.VMEM((hid, chan), jnp.bfloat16),
            pltpu.VMEM((1, chan), jnp.float32),
            pltpu.VMEM((1, chan), jnp.float32),
            pltpu.VMEM((rows, hid), jnp.bfloat16),
            pltpu.VMEM((rows, hid), jnp.float32),
            pltpu.SemaphoreType.DMA((8,)),
        ],
        compiler_params=pltpu.CompilerParams(vmem_limit_bytes=60 * 1024 * 1024),
        name="rows_kernel",
    )(
        me,
        counts,
        owner.reshape(1, rows),
        column.reshape(1, rows),
        profiles,
        radiances,
        inner_weight,
        inner_bias.reshape(1, hid),
        outer_weight,
        outer_bias.reshape(1, chan),
        channel_weight.reshape(1, chan),
    )
    halves = [[o * inner + i for i in range(inner)] for o in range(OUTER)]
    got = lax.all_to_all(
        bucket, "tile", split_axis=0, concat_axis=0, axis_index_groups=halves, tiled=True
    )
    own, other = pl.pallas_call(
        functools.partial(blocks_kernel, tiles, most),
        out_shape=[
            jax.ShapeDtypeStruct((COL_DEV, width), jnp.float32),
            jax.ShapeDtypeStruct((COL_DEV, width), jnp.bfloat16),
        ],
        in_specs=[smem, vmem],
        out_specs=[vmem, vmem],
        compiler_params=pltpu.CompilerParams(vmem_limit_bytes=24 * 1024 * 1024),
        name="blocks_kernel",
    )(me, got)
    pairs = [(t, (t + inner) % tiles) for t in range(tiles)]
    return own + lax.ppermute(other, "tile", pairs).astype(jnp.float32)


def solution(mesh):
    placed = (
        P(("group", "tile"), None),
        P(("group", "tile"), None),
        P(),
        P(),
        P(),
        P(),
        P(),
        P(("group", "tile")),
        P(("group", "tile"), None),
        P(("group", "tile")),
    )
    return jax.shard_map(
        per_device,
        mesh=mesh,
        in_specs=placed,
        out_specs=P(("group", "tile"), None),
        check_vma=False,
    )
```

```python
import functools

import jax
import jax.numpy as jnp
from jax import lax
from jax.experimental import pallas as pl
from jax.experimental.pallas import tpu as pltpu
from jax.sharding import PartitionSpec as P

COL_DEV = 128
CHUNK = 512
LANES = 128
LABEL_ROWS = 8
OUTER = 2
NT = (((1,), (1,)), ((), ()))


def as_bf16(mask):
    return mask.astype(jnp.float32).astype(jnp.bfloat16)


def rows_kernel(
    tiles,
    most,
    me_ref,
    count_ref,
    owner_ref,
    column_ref,
    prof_hbm,
    rad_hbm,
    w1_hbm,
    b1_hbm,
    w2_hbm,
    b2_hbm,
    cw_hbm,
    out_ref,
    prof_ref,
    rad_ref,
    w1_ref,
    b1_ref,
    w2_ref,
    b2_ref,
    cw_ref,
    factor_ref,
    even_ref,
    odd_ref,
    output_ref,
    grads_ref,
    sems,
    sems1,
    sems2,
):
    rows, width = prof_ref.shape
    chunks = w1_ref.shape[0]
    pairs = (
        (prof_hbm, prof_ref),
        (b1_hbm, b1_ref),
        (rad_hbm, rad_ref),
        (b2_hbm, b2_ref),
        (cw_hbm, cw_ref),
    )
    copies = [
        pltpu.make_async_copy(src, dst, sems.at[i]) for i, (src, dst) in enumerate(pairs)
    ]

    def copy1(i):
        part = pl.ds(pl.multiple_of(i * CHUNK, CHUNK), CHUNK)
        return pltpu.make_async_copy(w1_hbm.at[:, part], w1_ref.at[i], sems1.at[i])

    def copy2(i):
        part = pl.ds(pl.multiple_of(i * CHUNK, CHUNK), CHUNK)
        return pltpu.make_async_copy(w2_hbm.at[part, :], w2_ref.at[i], sems2.at[i])

    copies[0].start()
    copies[1].start()
    copy1(0).start()
    copy1(1).start()
    copy2(0).start()

    def start_rest(i, carry):
        copy1(i + 1).start()
        copy2(i).start()
        return carry

    lax.fori_loop(1, chunks - 1, start_rest, 0)
    copy2(chunks - 1).start()
    for copy in copies[2:]:
        copy.start()

    inner = out_ref.shape[0]
    live = lax.broadcasted_iota(jnp.int32, (1, rows), 1) < count_ref[0]
    owner = jnp.where(live, owner_ref[...], -1)
    mine = lax.broadcasted_iota(jnp.int32, (tiles, rows), 0) == owner
    one_hot = mine.astype(jnp.float32)
    upper = as_bf16(
        lax.broadcasted_iota(jnp.int32, (rows, rows), 0)
        <= lax.broadcasted_iota(jnp.int32, (rows, rows), 1)
    )
    running = jnp.dot(one_hot.astype(jnp.bfloat16), upper, preferred_element_type=jnp.float32)
    rank = jnp.sum(running * one_hot, axis=0, keepdims=True).astype(jnp.int32) - 1
    pool = tiles // inner * most
    place = owner & (inner - 1)
    order = lax.shift_right_arithmetic(owner, inner.bit_length() - 1) * most + rank
    slot = jnp.where(live, place * pool + order, -1)
    placing = as_bf16(lax.broadcasted_iota(jnp.int32, (inner * pool, rows), 0) == slot)
    lane = order + lax.rem(me_ref[0], LANES // pool) * pool
    lane_hot = as_bf16(lax.broadcasted_iota(jnp.int32, (LANES, rows), 0) == lane)
    here = live & (lax.broadcasted_iota(jnp.int32, (inner, rows), 0) == place)
    marked = jnp.where(here, (column_ref[...] + 1).astype(jnp.float32), 0.0)
    labels = lax.dot_general(
        marked.astype(jnp.bfloat16), lane_hot, NT, preferred_element_type=jnp.float32
    )

    copies[0].wait()
    copies[1].wait()
    prof_ref[...] = (prof_ref[...].astype(jnp.float32) * 0.5).astype(jnp.bfloat16)

    def enter(i, half_ref):
        half_ref[...] = jnp.dot(prof_ref[...], w1_ref[i], preferred_element_type=jnp.float32)

    def leave(i, half_ref):
        u = half_ref[...] + 0.5 * b1_ref[i]
        p = jnp.tanh(u) + 1.0
        hidden = u * p
        factor_ref[i] = p + hidden * (2.0 - p)
        output_ref[...] += jnp.dot(
            hidden.astype(jnp.bfloat16), w2_ref[i], preferred_element_type=jnp.float32
        )

    def forward_pair(j, carry):
        i = 2 * j
        copy1(i + 1).wait()
        copy2(i).wait()
        enter(i + 1, odd_ref)
        leave(i, even_ref)
        copy1(i + 2).wait()
        copy2(i + 1).wait()
        enter(i + 2, even_ref)
        leave(i + 1, odd_ref)
        return carry

    output_ref[...] = jnp.zeros_like(output_ref)
    copy1(0).wait()
    enter(0, even_ref)
    lax.fori_loop(0, chunks // 2 - 1, forward_pair, 0)
    copy1(chunks - 1).wait()
    copy2(chunks - 2).wait()
    enter(chunks - 1, odd_ref)
    leave(chunks - 2, even_ref)
    copy2(chunks - 1).wait()
    for copy in copies[2:]:
        copy.wait()
    leave(chunks - 1, odd_ref)

    misfit = output_ref[...] + b2_ref[...] - rad_ref[...].astype(jnp.float32)
    misfit = (0.5 * cw_ref[...]) * misfit
    alive = lax.broadcasted_iota(jnp.int32, (rows, 1), 0) < count_ref[0]
    rad_ref[...] = jnp.where(alive, misfit, 0.0).astype(jnp.bfloat16)

    def enter_back(i, half_ref):
        half_ref[...] = lax.dot_general(
            rad_ref[...], w2_ref[i], NT, preferred_element_type=jnp.float32
        )

    def leave_back(i, half_ref):
        slope = (half_ref[...] * factor_ref[i]).astype(jnp.bfloat16)
        grads_ref[...] += lax.dot_general(
            slope, w1_ref[i], NT, preferred_element_type=jnp.float32
        )

    def backward_pair(j, carry):
        i = 2 * j
        enter_back(i + 1, odd_ref)
        leave_back(i, even_ref)
        enter_back(i + 2, even_ref)
        leave_back(i + 1, odd_ref)
        return carry

    grads_ref[...] = jnp.zeros_like(grads_ref)
    enter_back(0, even_ref)
    lax.fori_loop(0, chunks // 2 - 1, backward_pair, 0)
    enter_back(chunks - 1, odd_ref)
    leave_back(chunks - 2, even_ref)
    leave_back(chunks - 1, odd_ref)
    grads = grads_ref[...].astype(jnp.bfloat16)
    placed = jnp.dot(placing, grads, preferred_element_type=jnp.float32).astype(jnp.bfloat16)
    parts = width // LANES
    for k in range(parts):
        out_ref[:, k * pool : (k + 1) * pool, :] = placed[
            :, k * LANES : (k + 1) * LANES
        ].reshape(inner, pool, LANES)
    out_ref[:, parts * pool :, :] = jnp.broadcast_to(
        labels.reshape(inner, 1, LANES), (inner, LABEL_ROWS, LANES)
    ).astype(jnp.bfloat16)


def blocks_kernel(tiles, most, me_ref, got_ref, own_ref, other_ref):
    inner = got_ref.shape[0]
    outer = tiles // inner
    pool = outer * most
    group = LANES // pool
    parts = own_ref.shape[1] // LANES
    marks = got_ref[:, parts * pool :, :].astype(jnp.float32)[:, 0, :]
    index = lax.broadcasted_iota(jnp.int32, (outer * COL_DEV, LANES), 0)
    lane = lax.broadcasted_iota(jnp.int32, (1, LANES), 1) & (pool - 1)
    turn = lax.shift_right_arithmetic(lane, most.bit_length() - 1) ^ (
        lax.shift_right_arithmetic(me_ref[0], inner.bit_length() - 1)
    )
    chosen = []
    for g in range(inner // group):
        label = jnp.sum(marks[g * group : (g + 1) * group], axis=0, keepdims=True)
        label = label.astype(jnp.int32)
        code = jnp.where(label > 0, turn * COL_DEV + label - 1, -1)
        chosen.append(as_bf16(index == code))
    chosen = jnp.concatenate(chosen, axis=1)
    for k in range(parts):
        block = got_ref[:, k * pool : (k + 1) * pool, :].reshape(inner * pool, LANES)
        total = jnp.dot(chosen, block, preferred_element_type=jnp.float32)
        own_ref[:, k * LANES : (k + 1) * LANES] = total[:COL_DEV]
        other_ref[:, k * LANES : (k + 1) * LANES] = total[COL_DEV:].astype(jnp.bfloat16)


def per_device(
    profiles,
    radiances,
    inner_weight,
    inner_bias,
    outer_weight,
    outer_bias,
    channel_weight,
    counts,
    owner,
    column,
):
    tiles = lax.axis_size("tile")
    rows, width = profiles.shape
    hid = inner_weight.shape[1]
    chan = radiances.shape[1]
    most = max(2, 2 * rows // tiles)
    chunks = hid // CHUNK
    inner = tiles // OUTER
    pool = OUTER * most
    high = width // LANES * pool + LABEL_ROWS
    me = lax.axis_index("tile").astype(jnp.int32).reshape(1)
    vmem = pl.BlockSpec(memory_space=pltpu.VMEM)
    smem = pl.BlockSpec(memory_space=pltpu.SMEM)
    anywhere = pl.BlockSpec(memory_space=pl.ANY)
    bucket = pl.pallas_call(
        functools.partial(rows_kernel, tiles, most),
        out_shape=jax.ShapeDtypeStruct((inner, high, LANES), jnp.bfloat16),
        in_specs=[smem, smem, vmem, vmem] + [anywhere] * 7,
        out_specs=vmem,
        scratch_shapes=[
            pltpu.VMEM((rows, width), jnp.bfloat16),
            pltpu.VMEM((rows, chan), jnp.bfloat16),
            pltpu.VMEM((chunks, width, CHUNK), jnp.bfloat16),
            pltpu.VMEM((chunks, 1, CHUNK), jnp.float32),
            pltpu.VMEM((chunks, CHUNK, chan), jnp.bfloat16),
            pltpu.VMEM((1, chan), jnp.float32),
            pltpu.VMEM((1, chan), jnp.float32),
            pltpu.VMEM((chunks, rows, CHUNK), jnp.float32),
            pltpu.VMEM((rows, CHUNK), jnp.float32),
            pltpu.VMEM((rows, CHUNK), jnp.float32),
            pltpu.VMEM((rows, chan), jnp.float32),
            pltpu.VMEM((rows, width), jnp.float32),
            pltpu.SemaphoreType.DMA((5,)),
            pltpu.SemaphoreType.DMA((chunks,)),
            pltpu.SemaphoreType.DMA((chunks,)),
        ],
        compiler_params=pltpu.CompilerParams(vmem_limit_bytes=60 * 1024 * 1024),
        name="rows_kernel",
    )(
        me,
        counts,
        owner.reshape(1, rows),
        column.reshape(1, rows),
        profiles,
        radiances,
        inner_weight,
        inner_bias.reshape(chunks, 1, CHUNK),
        outer_weight,
        outer_bias.reshape(1, chan),
        channel_weight.reshape(1, chan),
    )
    halves = [[o * inner + i for i in range(inner)] for o in range(OUTER)]
    got = lax.all_to_all(
        bucket, "tile", split_axis=0, concat_axis=0, axis_index_groups=halves, tiled=True
    )
    own, other = pl.pallas_call(
        functools.partial(blocks_kernel, tiles, most),
        out_shape=[
            jax.ShapeDtypeStruct((COL_DEV, width), jnp.float32),
            jax.ShapeDtypeStruct((COL_DEV, width), jnp.bfloat16),
        ],
        in_specs=[smem, vmem],
        out_specs=[vmem, vmem],
        compiler_params=pltpu.CompilerParams(vmem_limit_bytes=24 * 1024 * 1024),
        name="blocks_kernel",
    )(me, got)
    pairs = [(t, (t + inner) % tiles) for t in range(tiles)]
    return own + lax.ppermute(other, "tile", pairs).astype(jnp.float32)


def solution(mesh):
    placed = (
        P(("group", "tile"), None),
        P(("group", "tile"), None),
        P(),
        P(),
        P(),
        P(),
        P(),
        P(("group", "tile")),
        P(("group", "tile"), None),
        P(("group", "tile")),
    )
    return jax.shard_map(
        per_device,
        mesh=mesh,
        in_specs=placed,
        out_specs=P(("group", "tile"), None),
        check_vma=False,
    )
```

```python
import functools

import jax
import jax.numpy as jnp
from jax import lax
from jax.experimental import pallas as pl
from jax.experimental.pallas import tpu as pltpu
from jax.sharding import PartitionSpec as P

COL_DEV = 128
CHUNK = 512
LANES = 128
LABEL_ROWS = 8
OUTER = 2
FIRST = 256
QUARTERS = 4
NT = (((1,), (1,)), ((), ()))


def as_bf16(mask):
    return mask.astype(jnp.float32).astype(jnp.bfloat16)


def rows_kernel(
    tiles,
    most,
    me_ref,
    count_ref,
    owner_ref,
    column_ref,
    prof_hbm,
    rad_hbm,
    w1_hbm,
    b1_hbm,
    w2_hbm,
    b2_hbm,
    cw_hbm,
    out_ref,
    slot_ref,
    slope_hbm,
    prof_ref,
    rad_ref,
    w1_ref,
    b1_ref,
    w2_ref,
    b2_ref,
    cw_ref,
    hidden_ref,
    factor_ref,
    sems,
    out_sems,
):
    rows, width = prof_ref.shape
    hid = w1_ref.shape[1]
    quarter = hid // QUARTERS
    pieces = [pl.ds(i * quarter, quarter) for i in range(QUARTERS)]
    pairs = (
        [(prof_hbm, prof_ref), (b1_hbm, b1_ref)]
        + [(w1_hbm.at[:, piece], w1_ref.at[:, piece]) for piece in pieces]
        + [(w2_hbm, w2_ref), (rad_hbm, rad_ref), (b2_hbm, b2_ref), (cw_hbm, cw_ref)]
    )
    copies = [
        pltpu.make_async_copy(src, dst, sems.at[i]) for i, (src, dst) in enumerate(pairs)
    ]
    for copy in copies:
        copy.start()

    inner = out_ref.shape[0]
    live = lax.broadcasted_iota(jnp.int32, (1, rows), 1) < count_ref[0]
    owner = jnp.where(live, owner_ref[...], -1)
    mine = lax.broadcasted_iota(jnp.int32, (tiles, rows), 0) == owner
    one_hot = mine.astype(jnp.float32)
    upper = as_bf16(
        lax.broadcasted_iota(jnp.int32, (rows, rows), 0)
        <= lax.broadcasted_iota(jnp.int32, (rows, rows), 1)
    )
    running = jnp.dot(one_hot.astype(jnp.bfloat16), upper, preferred_element_type=jnp.float32)
    rank = jnp.sum(running * one_hot, axis=0, keepdims=True).astype(jnp.int32) - 1
    pool = tiles // inner * most
    place = owner & (inner - 1)
    order = lax.shift_right_arithmetic(owner, inner.bit_length() - 1) * most + rank
    slot = jnp.where(live, place * pool + order, -1)
    slot_ref[...] = slot
    placing = as_bf16(lax.broadcasted_iota(jnp.int32, (inner * pool, rows), 0) == slot)
    lane = order + lax.rem(me_ref[0], LANES // pool) * pool
    lane_hot = as_bf16(lax.broadcasted_iota(jnp.int32, (LANES, rows), 0) == lane)
    here = live & (lax.broadcasted_iota(jnp.int32, (inner, rows), 0) == place)
    marked = jnp.where(here, (column_ref[...] + 1).astype(jnp.float32), 0.0)
    labels = lax.dot_general(
        marked.astype(jnp.bfloat16), lane_hot, NT, preferred_element_type=jnp.float32
    )

    copies[0].wait()
    copies[1].wait()
    prof = (prof_ref[...].astype(jnp.float32) * 0.5).astype(jnp.bfloat16)
    for i in range(hid // CHUNK):
        part = pl.ds(i * CHUNK, CHUNK)
        if i * CHUNK % quarter == 0:
            copies[2 + i * CHUNK // quarter].wait()
        u = jnp.dot(prof, w1_ref[:, part], preferred_element_type=jnp.float32)
        u = u + 0.5 * b1_ref[:, part]
        p = jnp.tanh(u) + 1.0
        hidden = u * p
        hidden_ref[:, part] = hidden.astype(jnp.bfloat16)
        factor_ref[:, part] = p + hidden * (2.0 - p)
    for copy in copies[2 + QUARTERS :]:
        copy.wait()
    output = jnp.dot(hidden_ref[...], w2_ref[...], preferred_element_type=jnp.float32)
    misfit = (0.5 * cw_ref[...]) * (output + b2_ref[...] - rad_ref[...].astype(jnp.float32))
    alive = lax.broadcasted_iota(jnp.int32, (rows, 1), 0) < count_ref[0]
    misfit = jnp.where(alive, misfit, 0.0).astype(jnp.bfloat16)
    sent = []
    for i in range(hid // CHUNK):
        part = pl.ds(i * CHUNK, CHUNK)
        back = lax.dot_general(misfit, w2_ref[part, :], NT, preferred_element_type=jnp.float32)
        hidden_ref[:, part] = (back * factor_ref[:, part]).astype(jnp.bfloat16)
        sent.append(
            pltpu.make_async_copy(hidden_ref.at[:, part], slope_hbm.at[:, part], out_sems.at[i])
        )
        sent[-1].start()
    parts = FIRST // LANES
    grads = lax.dot_general(
        hidden_ref[...], w1_ref[:FIRST, :], NT, preferred_element_type=jnp.float32
    ).astype(jnp.bfloat16)
    placed = jnp.dot(placing, grads, preferred_element_type=jnp.float32).astype(jnp.bfloat16)
    for k in range(parts):
        out_ref[:, k * pool : (k + 1) * pool, :] = placed[
            :, k * LANES : (k + 1) * LANES
        ].reshape(inner, pool, LANES)
    out_ref[:, parts * pool :, :] = jnp.broadcast_to(
        labels.reshape(inner, 1, LANES), (inner, LABEL_ROWS, LANES)
    ).astype(jnp.bfloat16)
    for copy in sent:
        copy.wait()


def rest_kernel(pool, slot_ref, slope_hbm, w1_hbm, out_ref, slope_ref, w1_ref, sems):
    inner = out_ref.shape[0]
    rows, hid = slope_ref.shape
    quarter = hid // QUARTERS
    pieces = [pl.ds(i * quarter, quarter) for i in range(QUARTERS)]
    pairs = [(w1_hbm.at[pl.ds(FIRST, w1_ref.shape[0]), :], w1_ref)]
    pairs += [(slope_hbm.at[:, piece], slope_ref.at[:, piece]) for piece in pieces]
    copies = [
        pltpu.make_async_copy(src, dst, sems.at[i]) for i, (src, dst) in enumerate(pairs)
    ]
    for copy in copies:
        copy.start()
    slots = inner * pool
    placing = as_bf16(lax.broadcasted_iota(jnp.int32, (slots, rows), 0) == slot_ref[...])
    copies[0].wait()
    grads = jnp.zeros((rows, w1_ref.shape[0]), jnp.float32)
    for i, piece in enumerate(pieces):
        copies[1 + i].wait()
        grads += lax.dot_general(
            slope_ref[:, piece], w1_ref[:, piece], NT, preferred_element_type=jnp.float32
        )
    placed = jnp.dot(placing, grads.astype(jnp.bfloat16), preferred_element_type=jnp.float32)
    placed = placed.astype(jnp.bfloat16)
    for k in range(w1_ref.shape[0] // LANES):
        out_ref[:, k * pool : (k + 1) * pool, :] = placed[
            :, k * LANES : (k + 1) * LANES
        ].reshape(inner, pool, LANES)


def blocks_kernel(tiles, most, marks_row, me_ref, got_ref, first_ref, own_ref, other_ref):
    inner = got_ref.shape[0]
    outer = tiles // inner
    pool = outer * most
    group = LANES // pool
    parts = own_ref.shape[1] // LANES
    marks = first_ref[:, marks_row:, :].astype(jnp.float32)[:, 0, :]
    index = lax.broadcasted_iota(jnp.int32, (outer * COL_DEV, LANES), 0)
    lane = lax.broadcasted_iota(jnp.int32, (1, LANES), 1) & (pool - 1)
    turn = lax.shift_right_arithmetic(lane, most.bit_length() - 1) ^ (
        lax.shift_right_arithmetic(me_ref[0], inner.bit_length() - 1)
    )
    chosen = []
    for g in range(inner // group):
        label = jnp.sum(marks[g * group : (g + 1) * group], axis=0, keepdims=True)
        label = label.astype(jnp.int32)
        code = jnp.where(label > 0, turn * COL_DEV + label - 1, -1)
        chosen.append(as_bf16(index == code))
    chosen = jnp.concatenate(chosen, axis=1)
    for k in range(parts):
        block = got_ref[:, k * pool : (k + 1) * pool, :].reshape(inner * pool, LANES)
        total = jnp.dot(chosen, block, preferred_element_type=jnp.float32)
        own_ref[:, k * LANES : (k + 1) * LANES] = total[:COL_DEV]
        other_ref[:, k * LANES : (k + 1) * LANES] = total[COL_DEV:].astype(jnp.bfloat16)


def add_kernel(own_ref, came_ref, own_rest_ref, came_rest_ref, out_ref):
    out_ref[:, :FIRST] = own_ref[...] + came_ref[...].astype(jnp.float32)
    out_ref[:, FIRST:] = own_rest_ref[...] + came_rest_ref[...].astype(jnp.float32)


def per_device(
    profiles,
    radiances,
    inner_weight,
    inner_bias,
    outer_weight,
    outer_bias,
    channel_weight,
    counts,
    owner,
    column,
):
    tiles = lax.axis_size("tile")
    rows, width = profiles.shape
    hid = inner_weight.shape[1]
    chan = radiances.shape[1]
    most = max(2, 2 * rows // tiles)
    inner = tiles // OUTER
    pool = OUTER * most
    marks_row = FIRST // LANES * pool
    high = marks_row + LABEL_ROWS
    me = lax.axis_index("tile").astype(jnp.int32).reshape(1)
    halves = [[o * inner + i for i in range(inner)] for o in range(OUTER)]
    vmem = pl.BlockSpec(memory_space=pltpu.VMEM)
    smem = pl.BlockSpec(memory_space=pltpu.SMEM)
    anywhere = pl.BlockSpec(memory_space=pl.ANY)
    bucket, slot, slope = pl.pallas_call(
        functools.partial(rows_kernel, tiles, most),
        out_shape=[
            jax.ShapeDtypeStruct((inner, high, LANES), jnp.bfloat16),
            jax.ShapeDtypeStruct((1, rows), jnp.int32),
            jax.ShapeDtypeStruct((rows, hid), jnp.bfloat16),
        ],
        in_specs=[smem, smem, vmem, vmem] + [anywhere] * 7,
        out_specs=[vmem, vmem, anywhere],
        scratch_shapes=[
            pltpu.VMEM((rows, width), jnp.bfloat16),
            pltpu.VMEM((rows, chan), jnp.bfloat16),
            pltpu.VMEM((width, hid), jnp.bfloat16),
            pltpu.VMEM((1, hid), jnp.float32),
            pltpu.VMEM((hid, chan), jnp.bfloat16),
            pltpu.VMEM((1, chan), jnp.float32),
            pltpu.VMEM((1, chan), jnp.float32),
            pltpu.VMEM((rows, hid), jnp.bfloat16),
            pltpu.VMEM((rows, hid), jnp.float32),
            pltpu.SemaphoreType.DMA((QUARTERS + 6,)),
            pltpu.SemaphoreType.DMA((hid // CHUNK,)),
        ],
        compiler_params=pltpu.CompilerParams(vmem_limit_bytes=60 * 1024 * 1024),
        name="rows_kernel",
    )(
        me,
        counts,
        owner.reshape(1, rows),
        column.reshape(1, rows),
        profiles,
        radiances,
        inner_weight,
        inner_bias.reshape(1, hid),
        outer_weight,
        outer_bias.reshape(1, chan),
        channel_weight.reshape(1, chan),
    )
    rest = width - FIRST
    bucket_rest = pl.pallas_call(
        functools.partial(rest_kernel, pool),
        out_shape=jax.ShapeDtypeStruct((inner, rest // LANES * pool, LANES), jnp.bfloat16),
        in_specs=[vmem, anywhere, anywhere],
        out_specs=vmem,
        scratch_shapes=[
            pltpu.VMEM((rows, hid), jnp.bfloat16),
            pltpu.VMEM((rest, hid), jnp.bfloat16),
            pltpu.SemaphoreType.DMA((QUARTERS + 1,)),
        ],
        compiler_params=pltpu.CompilerParams(vmem_limit_bytes=60 * 1024 * 1024),
        cost_estimate=pl.CostEstimate(flops=3 << 30, bytes_accessed=7 << 20, transcendentals=0),
        name="rest_kernel",
    )(slot, slope, inner_weight)

    def exchange(block):
        return lax.all_to_all(
            block, "tile", split_axis=0, concat_axis=0, axis_index_groups=halves, tiled=True
        )

    def blocks(block, first, features):
        return pl.pallas_call(
            functools.partial(blocks_kernel, tiles, most, marks_row),
            out_shape=[
                jax.ShapeDtypeStruct((COL_DEV, features), jnp.float32),
                jax.ShapeDtypeStruct((COL_DEV, features), jnp.bfloat16),
            ],
            in_specs=[smem, vmem, vmem],
            out_specs=[vmem, vmem],
            compiler_params=pltpu.CompilerParams(vmem_limit_bytes=24 * 1024 * 1024),
            cost_estimate=pl.CostEstimate(
                flops=1 << 28, bytes_accessed=1 << 20, transcendentals=0
            ),
            name="blocks_kernel",
        )(me, block, first)

    pairs = [(t, (t + inner) % tiles) for t in range(tiles)]
    got = exchange(bucket)
    got_rest = exchange(bucket_rest)
    own, other = blocks(got, got, FIRST)
    came = lax.ppermute(other, "tile", pairs)
    own_rest, other_rest = blocks(got_rest, got, rest)
    came_rest = lax.ppermute(other_rest, "tile", pairs)
    return pl.pallas_call(
        add_kernel,
        out_shape=jax.ShapeDtypeStruct((COL_DEV, width), jnp.float32),
        in_specs=[vmem] * 4,
        out_specs=vmem,
        name="add_kernel",
    )(own, came, own_rest, came_rest)


def solution(mesh):
    placed = (
        P(("group", "tile"), None),
        P(("group", "tile"), None),
        P(),
        P(),
        P(),
        P(),
        P(),
        P(("group", "tile")),
        P(("group", "tile"), None),
        P(("group", "tile")),
    )
    return jax.shard_map(
        per_device,
        mesh=mesh,
        in_specs=placed,
        out_specs=P(("group", "tile"), None),
        check_vma=False,
    )
```

```python
import functools

import jax
import jax.numpy as jnp
from jax import lax
from jax.experimental import pallas as pl
from jax.experimental.pallas import tpu as pltpu
from jax.sharding import PartitionSpec as P

COL_DEV = 128
CHUNK = 512
LANES = 128
LABEL_ROWS = 8
OUTER = 2
QUARTERS = 4
NT = (((1,), (1,)), ((), ()))


def as_bf16(mask):
    return mask.astype(jnp.float32).astype(jnp.bfloat16)


def rows_kernel(
    tiles,
    most,
    me_ref,
    count_ref,
    owner_ref,
    column_ref,
    prof_hbm,
    rad_hbm,
    w1_hbm,
    b1_hbm,
    w2_hbm,
    b2_hbm,
    cw_hbm,
    out_ref,
    prof_ref,
    rad_ref,
    w1_ref,
    b1_ref,
    w2_ref,
    b2_ref,
    cw_ref,
    w1t_ref,
    w2t_ref,
    hidden_ref,
    factor_ref,
    sems,
):
    rows, width = prof_ref.shape
    hid = w1_ref.shape[1]
    quarter = hid // QUARTERS
    pieces = [pl.ds(i * quarter, quarter) for i in range(QUARTERS)]
    pairs = (
        [(prof_hbm, prof_ref), (b1_hbm, b1_ref)]
        + [(w1_hbm.at[:, piece], w1_ref.at[:, piece]) for piece in pieces]
        + [(w2_hbm.at[piece, :], w2_ref.at[piece, :]) for piece in pieces]
        + [(rad_hbm, rad_ref), (b2_hbm, b2_ref), (cw_hbm, cw_ref)]
    )
    copies = [
        pltpu.make_async_copy(src, dst, sems.at[i]) for i, (src, dst) in enumerate(pairs)
    ]
    for copy in copies:
        copy.start()

    inner = out_ref.shape[0]
    live = lax.broadcasted_iota(jnp.int32, (1, rows), 1) < count_ref[0]
    owner = jnp.where(live, owner_ref[...], -1)
    mine = lax.broadcasted_iota(jnp.int32, (tiles, rows), 0) == owner
    one_hot = mine.astype(jnp.float32)
    upper = as_bf16(
        lax.broadcasted_iota(jnp.int32, (rows, rows), 0)
        <= lax.broadcasted_iota(jnp.int32, (rows, rows), 1)
    )
    running = jnp.dot(one_hot.astype(jnp.bfloat16), upper, preferred_element_type=jnp.float32)
    rank = jnp.sum(running * one_hot, axis=0, keepdims=True).astype(jnp.int32) - 1
    pool = tiles // inner * most
    place = owner & (inner - 1)
    order = lax.shift_right_arithmetic(owner, inner.bit_length() - 1) * most + rank
    slot = jnp.where(live, place * pool + order, -1)
    placing = as_bf16(lax.broadcasted_iota(jnp.int32, (inner * pool, rows), 0) == slot)
    lane = order + lax.rem(me_ref[0], LANES // pool) * pool
    lane_hot = as_bf16(lax.broadcasted_iota(jnp.int32, (LANES, rows), 0) == lane)
    here = live & (lax.broadcasted_iota(jnp.int32, (inner, rows), 0) == place)
    marked = jnp.where(here, (column_ref[...] + 1).astype(jnp.float32), 0.0)
    labels = lax.dot_general(
        marked.astype(jnp.bfloat16), lane_hot, NT, preferred_element_type=jnp.float32
    )

    copies[0].wait()
    copies[1].wait()
    prof = (prof_ref[...].astype(jnp.float32) * 0.5).astype(jnp.bfloat16)
    for i in range(hid // CHUNK):
        part = pl.ds(i * CHUNK, CHUNK)
        if i * CHUNK % quarter == 0:
            copies[2 + i * CHUNK // quarter].wait()
        u = jnp.dot(prof, w1_ref[:, part], preferred_element_type=jnp.float32)
        u = u + 0.5 * b1_ref[:, part]
        p = jnp.tanh(u) + 1.0
        hidden = u * p
        hidden_ref[:, part] = hidden.astype(jnp.bfloat16)
        factor_ref[:, part] = p + hidden * (2.0 - p)
        w1t_ref[part, :] = w1_ref[:, part].T
    for copy in copies[2 + QUARTERS :]:
        copy.wait()
    for i in range(hid // CHUNK):
        part = pl.ds(i * CHUNK, CHUNK)
        w2t_ref[:, part] = w2_ref[part, :].T
    output = jnp.dot(hidden_ref[...], w2_ref[...], preferred_element_type=jnp.float32)
    misfit = (0.5 * cw_ref[...]) * (output + b2_ref[...] - rad_ref[...].astype(jnp.float32))
    alive = lax.broadcasted_iota(jnp.int32, (rows, 1), 0) < count_ref[0]
    misfit = jnp.where(alive, misfit, 0.0).astype(jnp.bfloat16)
    for i in range(hid // CHUNK):
        part = pl.ds(i * CHUNK, CHUNK)
        back = jnp.dot(misfit, w2t_ref[:, part], preferred_element_type=jnp.float32)
        hidden_ref[:, part] = (back * factor_ref[:, part]).astype(jnp.bfloat16)
    grads = jnp.dot(
        hidden_ref[...], w1t_ref[...], preferred_element_type=jnp.float32
    ).astype(jnp.bfloat16)
    placed = jnp.dot(placing, grads, preferred_element_type=jnp.float32).astype(jnp.bfloat16)
    parts = width // LANES
    for k in range(parts):
        out_ref[:, k * pool : (k + 1) * pool, :] = placed[
            :, k * LANES : (k + 1) * LANES
        ].reshape(inner, pool, LANES)
    out_ref[:, parts * pool :, :] = jnp.broadcast_to(
        labels.reshape(inner, 1, LANES), (inner, LABEL_ROWS, LANES)
    ).astype(jnp.bfloat16)


def blocks_kernel(tiles, most, me_ref, got_ref, own_ref, other_ref):
    inner = got_ref.shape[0]
    outer = tiles // inner
    pool = outer * most
    group = LANES // pool
    parts = own_ref.shape[1] // LANES
    marks = got_ref[:, parts * pool :, :].astype(jnp.float32)[:, 0, :]
    index = lax.broadcasted_iota(jnp.int32, (outer * COL_DEV, LANES), 0)
    lane = lax.broadcasted_iota(jnp.int32, (1, LANES), 1) & (pool - 1)
    turn = lax.shift_right_arithmetic(lane, most.bit_length() - 1) ^ (
        lax.shift_right_arithmetic(me_ref[0], inner.bit_length() - 1)
    )
    chosen = []
    for g in range(inner // group):
        label = jnp.sum(marks[g * group : (g + 1) * group], axis=0, keepdims=True)
        label = label.astype(jnp.int32)
        code = jnp.where(label > 0, turn * COL_DEV + label - 1, -1)
        chosen.append(as_bf16(index == code))
    chosen = jnp.concatenate(chosen, axis=1)
    for k in range(parts):
        block = got_ref[:, k * pool : (k + 1) * pool, :].reshape(inner * pool, LANES)
        total = jnp.dot(chosen, block, preferred_element_type=jnp.float32)
        own_ref[:, k * LANES : (k + 1) * LANES] = total[:COL_DEV]
        other_ref[:, k * LANES : (k + 1) * LANES] = total[COL_DEV:].astype(jnp.bfloat16)


def per_device(
    profiles,
    radiances,
    inner_weight,
    inner_bias,
    outer_weight,
    outer_bias,
    channel_weight,
    counts,
    owner,
    column,
):
    tiles = lax.axis_size("tile")
    rows, width = profiles.shape
    hid = inner_weight.shape[1]
    chan = radiances.shape[1]
    most = max(2, 2 * rows // tiles)
    inner = tiles // OUTER
    pool = OUTER * most
    high = width // LANES * pool + LABEL_ROWS
    me = lax.axis_index("tile").astype(jnp.int32).reshape(1)
    vmem = pl.BlockSpec(memory_space=pltpu.VMEM)
    smem = pl.BlockSpec(memory_space=pltpu.SMEM)
    anywhere = pl.BlockSpec(memory_space=pl.ANY)
    bucket = pl.pallas_call(
        functools.partial(rows_kernel, tiles, most),
        out_shape=jax.ShapeDtypeStruct((inner, high, LANES), jnp.bfloat16),
        in_specs=[smem, smem, vmem, vmem] + [anywhere] * 7,
        out_specs=vmem,
        scratch_shapes=[
            pltpu.VMEM((rows, width), jnp.bfloat16),
            pltpu.VMEM((rows, chan), jnp.bfloat16),
            pltpu.VMEM((width, hid), jnp.bfloat16),
            pltpu.VMEM((1, hid), jnp.float32),
            pltpu.VMEM((hid, chan), jnp.bfloat16),
            pltpu.VMEM((1, chan), jnp.float32),
            pltpu.VMEM((1, chan), jnp.float32),
            pltpu.VMEM((hid, width), jnp.bfloat16),
            pltpu.VMEM((chan, hid), jnp.bfloat16),
            pltpu.VMEM((rows, hid), jnp.bfloat16),
            pltpu.VMEM((rows, hid), jnp.float32),
            pltpu.SemaphoreType.DMA((2 * QUARTERS + 5,)),
        ],
        compiler_params=pltpu.CompilerParams(vmem_limit_bytes=60 * 1024 * 1024),
        name="rows_kernel",
    )(
        me,
        counts,
        owner.reshape(1, rows),
        column.reshape(1, rows),
        profiles,
        radiances,
        inner_weight,
        inner_bias.reshape(1, hid),
        outer_weight,
        outer_bias.reshape(1, chan),
        channel_weight.reshape(1, chan),
    )
    halves = [[o * inner + i for i in range(inner)] for o in range(OUTER)]
    got = lax.all_to_all(
        bucket, "tile", split_axis=0, concat_axis=0, axis_index_groups=halves, tiled=True
    )
    own, other = pl.pallas_call(
        functools.partial(blocks_kernel, tiles, most),
        out_shape=[
            jax.ShapeDtypeStruct((COL_DEV, width), jnp.float32),
            jax.ShapeDtypeStruct((COL_DEV, width), jnp.bfloat16),
        ],
        in_specs=[smem, vmem],
        out_specs=[vmem, vmem],
        compiler_params=pltpu.CompilerParams(vmem_limit_bytes=24 * 1024 * 1024),
        name="blocks_kernel",
    )(me, got)
    pairs = [(t, (t + inner) % tiles) for t in range(tiles)]
    return own + lax.ppermute(other, "tile", pairs).astype(jnp.float32)


def solution(mesh):
    placed = (
        P(("group", "tile"), None),
        P(("group", "tile"), None),
        P(),
        P(),
        P(),
        P(),
        P(),
        P(("group", "tile")),
        P(("group", "tile"), None),
        P(("group", "tile")),
    )
    return jax.shard_map(
        per_device,
        mesh=mesh,
        in_specs=placed,
        out_specs=P(("group", "tile"), None),
        check_vma=False,
    )
```

```python
import functools

import jax
import jax.numpy as jnp
from jax import lax
from jax.experimental import pallas as pl
from jax.experimental.pallas import tpu as pltpu
from jax.sharding import PartitionSpec as P

COL_DEV = 128
CHUNK = 512
LANES = 128
LABEL_ROWS = 8
OUTER = 2
QUARTERS = 4
NT = (((1,), (1,)), ((), ()))


def as_bf16(mask):
    return mask.astype(jnp.float32).astype(jnp.bfloat16)


def rows_kernel(
    tiles,
    most,
    me_ref,
    count_ref,
    owner_ref,
    column_ref,
    prof_hbm,
    rad_hbm,
    w1_hbm,
    b1_hbm,
    w2_hbm,
    b2_hbm,
    cw_hbm,
    out_ref,
    prof_ref,
    rad_ref,
    w1_ref,
    b1_ref,
    w2_ref,
    b2_ref,
    cw_ref,
    hidden_ref,
    factor_ref,
    sems,
):
    rows, width = prof_ref.shape
    hid = w1_ref.shape[1]
    chan = rad_ref.shape[1]
    quarter = hid // QUARTERS
    pieces = [pl.ds(i * quarter, quarter) for i in range(QUARTERS)]
    pairs = (
        [(prof_hbm, prof_ref), (b1_hbm, b1_ref)]
        + [(w1_hbm.at[:, piece], w1_ref.at[:, piece]) for piece in pieces]
        + [(w2_hbm.at[piece, :], w2_ref.at[piece, :]) for piece in pieces]
        + [(rad_hbm, rad_ref), (b2_hbm, b2_ref), (cw_hbm, cw_ref)]
    )
    copies = [
        pltpu.make_async_copy(src, dst, sems.at[i]) for i, (src, dst) in enumerate(pairs)
    ]
    for i in range(2 + QUARTERS):
        copies[i].start(priority=0)
    for i in range(2 + QUARTERS, len(copies)):
        copies[i].start(priority=1)

    inner = out_ref.shape[0]
    live = lax.broadcasted_iota(jnp.int32, (1, rows), 1) < count_ref[0]
    owner = jnp.where(live, owner_ref[...], -1)
    mine = lax.broadcasted_iota(jnp.int32, (tiles, rows), 0) == owner
    one_hot = mine.astype(jnp.float32)
    upper = as_bf16(
        lax.broadcasted_iota(jnp.int32, (rows, rows), 0)
        <= lax.broadcasted_iota(jnp.int32, (rows, rows), 1)
    )
    running = jnp.dot(one_hot.astype(jnp.bfloat16), upper, preferred_element_type=jnp.float32)
    rank = jnp.sum(running * one_hot, axis=0, keepdims=True).astype(jnp.int32) - 1
    pool = tiles // inner * most
    place = owner & (inner - 1)
    order = lax.shift_right_arithmetic(owner, inner.bit_length() - 1) * most + rank
    slot = jnp.where(live, place * pool + order, -1)
    placing = as_bf16(lax.broadcasted_iota(jnp.int32, (inner * pool, rows), 0) == slot)
    lane = order + lax.rem(me_ref[0], LANES // pool) * pool
    lane_hot = as_bf16(lax.broadcasted_iota(jnp.int32, (LANES, rows), 0) == lane)
    here = live & (lax.broadcasted_iota(jnp.int32, (inner, rows), 0) == place)
    marked = jnp.where(here, (column_ref[...] + 1).astype(jnp.float32), 0.0)
    labels = lax.dot_general(
        marked.astype(jnp.bfloat16), lane_hot, NT, preferred_element_type=jnp.float32
    )

    copies[0].wait()
    copies[1].wait()
    prof = (prof_ref[...].astype(jnp.float32) * 0.5).astype(jnp.bfloat16)
    output = jnp.zeros((rows, chan), jnp.float32)
    for q in range(QUARTERS):
        copies[2 + q].wait()
        for i in range(quarter // CHUNK):
            part = pl.ds(q * quarter + i * CHUNK, CHUNK)
            u = jnp.dot(prof, w1_ref[:, part], preferred_element_type=jnp.float32)
            u = u + 0.5 * b1_ref[:, part]
            p = jnp.tanh(u) + 1.0
            hidden = u * p
            hidden_ref[:, part] = hidden.astype(jnp.bfloat16)
            factor_ref[:, part] = p + hidden * (2.0 - p)
        copies[2 + QUARTERS + q].wait()
        output += jnp.dot(
            hidden_ref[:, pieces[q]], w2_ref[pieces[q], :], preferred_element_type=jnp.float32
        )
    for copy in copies[2 + 2 * QUARTERS :]:
        copy.wait()
    misfit = (0.5 * cw_ref[...]) * (output + b2_ref[...] - rad_ref[...].astype(jnp.float32))
    alive = lax.broadcasted_iota(jnp.int32, (rows, 1), 0) < count_ref[0]
    misfit = jnp.where(alive, misfit, 0.0).astype(jnp.bfloat16)
    for i in range(hid // CHUNK):
        part = pl.ds(i * CHUNK, CHUNK)
        back = lax.dot_general(misfit, w2_ref[part, :], NT, preferred_element_type=jnp.float32)
        hidden_ref[:, part] = (back * factor_ref[:, part]).astype(jnp.bfloat16)
    grads = lax.dot_general(
        hidden_ref[...], w1_ref[...], NT, preferred_element_type=jnp.float32
    ).astype(jnp.bfloat16)
    placed = jnp.dot(placing, grads, preferred_element_type=jnp.float32).astype(jnp.bfloat16)
    parts = width // LANES
    for k in range(parts):
        out_ref[:, k * pool : (k + 1) * pool, :] = placed[
            :, k * LANES : (k + 1) * LANES
        ].reshape(inner, pool, LANES)
    out_ref[:, parts * pool :, :] = jnp.broadcast_to(
        labels.reshape(inner, 1, LANES), (inner, LABEL_ROWS, LANES)
    ).astype(jnp.bfloat16)


def blocks_kernel(tiles, most, me_ref, got_ref, own_ref, other_ref):
    inner = got_ref.shape[0]
    outer = tiles // inner
    pool = outer * most
    group = LANES // pool
    parts = own_ref.shape[1] // LANES
    marks = got_ref[:, parts * pool :, :].astype(jnp.float32)[:, 0, :]
    index = lax.broadcasted_iota(jnp.int32, (outer * COL_DEV, LANES), 0)
    lane = lax.broadcasted_iota(jnp.int32, (1, LANES), 1) & (pool - 1)
    turn = lax.shift_right_arithmetic(lane, most.bit_length() - 1) ^ (
        lax.shift_right_arithmetic(me_ref[0], inner.bit_length() - 1)
    )
    chosen = []
    for g in range(inner // group):
        label = jnp.sum(marks[g * group : (g + 1) * group], axis=0, keepdims=True)
        label = label.astype(jnp.int32)
        code = jnp.where(label > 0, turn * COL_DEV + label - 1, -1)
        chosen.append(as_bf16(index == code))
    chosen = jnp.concatenate(chosen, axis=1)
    for k in range(parts):
        block = got_ref[:, k * pool : (k + 1) * pool, :].reshape(inner * pool, LANES)
        total = jnp.dot(chosen, block, preferred_element_type=jnp.float32)
        own_ref[:, k * LANES : (k + 1) * LANES] = total[:COL_DEV]
        other_ref[:, k * LANES : (k + 1) * LANES] = total[COL_DEV:].astype(jnp.bfloat16)


def per_device(
    profiles,
    radiances,
    inner_weight,
    inner_bias,
    outer_weight,
    outer_bias,
    channel_weight,
    counts,
    owner,
    column,
):
    tiles = lax.axis_size("tile")
    rows, width = profiles.shape
    hid = inner_weight.shape[1]
    chan = radiances.shape[1]
    most = max(2, 2 * rows // tiles)
    inner = tiles // OUTER
    pool = OUTER * most
    high = width // LANES * pool + LABEL_ROWS
    me = lax.axis_index("tile").astype(jnp.int32).reshape(1)
    vmem = pl.BlockSpec(memory_space=pltpu.VMEM)
    smem = pl.BlockSpec(memory_space=pltpu.SMEM)
    anywhere = pl.BlockSpec(memory_space=pl.ANY)
    bucket = pl.pallas_call(
        functools.partial(rows_kernel, tiles, most),
        out_shape=jax.ShapeDtypeStruct((inner, high, LANES), jnp.bfloat16),
        in_specs=[smem, smem, vmem, vmem] + [anywhere] * 7,
        out_specs=vmem,
        scratch_shapes=[
            pltpu.VMEM((rows, width), jnp.bfloat16),
            pltpu.VMEM((rows, chan), jnp.bfloat16),
            pltpu.VMEM((width, hid), jnp.bfloat16),
            pltpu.VMEM((1, hid), jnp.float32),
            pltpu.VMEM((hid, chan), jnp.bfloat16),
            pltpu.VMEM((1, chan), jnp.float32),
            pltpu.VMEM((1, chan), jnp.float32),
            pltpu.VMEM((rows, hid), jnp.bfloat16),
            pltpu.VMEM((rows, hid), jnp.float32),
            pltpu.SemaphoreType.DMA((2 * QUARTERS + 5,)),
        ],
        compiler_params=pltpu.CompilerParams(vmem_limit_bytes=60 * 1024 * 1024),
        name="rows_kernel",
    )(
        me,
        counts,
        owner.reshape(1, rows),
        column.reshape(1, rows),
        profiles,
        radiances,
        inner_weight,
        inner_bias.reshape(1, hid),
        outer_weight,
        outer_bias.reshape(1, chan),
        channel_weight.reshape(1, chan),
    )
    halves = [[o * inner + i for i in range(inner)] for o in range(OUTER)]
    got = lax.all_to_all(
        bucket, "tile", split_axis=0, concat_axis=0, axis_index_groups=halves, tiled=True
    )
    own, other = pl.pallas_call(
        functools.partial(blocks_kernel, tiles, most),
        out_shape=[
            jax.ShapeDtypeStruct((COL_DEV, width), jnp.float32),
            jax.ShapeDtypeStruct((COL_DEV, width), jnp.bfloat16),
        ],
        in_specs=[smem, vmem],
        out_specs=[vmem, vmem],
        compiler_params=pltpu.CompilerParams(vmem_limit_bytes=24 * 1024 * 1024),
        name="blocks_kernel",
    )(me, got)
    pairs = [(t, (t + inner) % tiles) for t in range(tiles)]
    return own + lax.ppermute(other, "tile", pairs).astype(jnp.float32)


def solution(mesh):
    placed = (
        P(("group", "tile"), None),
        P(("group", "tile"), None),
        P(),
        P(),
        P(),
        P(),
        P(),
        P(("group", "tile")),
        P(("group", "tile"), None),
        P(("group", "tile")),
    )
    return jax.shard_map(
        per_device,
        mesh=mesh,
        in_specs=placed,
        out_specs=P(("group", "tile"), None),
        check_vma=False,
    )
```

```python
import functools

import jax
import jax.numpy as jnp
from jax import lax
from jax.experimental import pallas as pl
from jax.experimental.pallas import tpu as pltpu
from jax.sharding import PartitionSpec as P

COL_DEV = 128
CHUNK = 512
LANES = 128
LABEL_ROWS = 8
OUTER = 2
ROWS = 256
NT = (((1,), (1,)), ((), ()))


def as_bf16(mask):
    return mask.astype(jnp.float32).astype(jnp.bfloat16)


def rows_kernel(
    tiles,
    most,
    me_ref,
    count_ref,
    owner_ref,
    column_ref,
    prof_hbm,
    rad_hbm,
    w1_hbm,
    b1_hbm,
    w2_hbm,
    b2_hbm,
    cw_hbm,
    out_ref,
    prof_ref,
    rad_ref,
    w1_ref,
    b1_ref,
    w2_ref,
    b2_ref,
    cw_ref,
    hidden_ref,
    factor_ref,
    sems,
):
    rows, width = prof_ref.shape
    hid = w1_ref.shape[1]
    chan = rad_ref.shape[1]
    half = hid // 2
    low, high = pl.ds(0, half), pl.ds(half, half)
    pairs = (
        (prof_hbm, prof_ref),
        (b1_hbm, b1_ref),
        (w1_hbm.at[:, low], w1_ref.at[:, low]),
        (w1_hbm.at[:, high], w1_ref.at[:, high]),
        (w2_hbm, w2_ref),
        (rad_hbm, rad_ref),
        (b2_hbm, b2_ref),
        (cw_hbm, cw_ref),
    )
    copies = [
        pltpu.make_async_copy(src, dst, sems.at[i]) for i, (src, dst) in enumerate(pairs)
    ]
    for copy in copies:
        copy.start()

    inner = out_ref.shape[0]
    live = lax.broadcasted_iota(jnp.int32, (1, rows), 1) < count_ref[0]
    owner = jnp.where(live, owner_ref[...], -1)
    mine = lax.broadcasted_iota(jnp.int32, (tiles, rows), 0) == owner
    one_hot = mine.astype(jnp.float32)
    upper = as_bf16(
        lax.broadcasted_iota(jnp.int32, (rows, rows), 0)
        <= lax.broadcasted_iota(jnp.int32, (rows, rows), 1)
    )
    running = jnp.dot(one_hot.astype(jnp.bfloat16), upper, preferred_element_type=jnp.float32)
    rank = jnp.sum(running * one_hot, axis=0, keepdims=True).astype(jnp.int32) - 1
    pool = tiles // inner * most
    place = owner & (inner - 1)
    order = lax.shift_right_arithmetic(owner, inner.bit_length() - 1) * most + rank
    slot = jnp.where(live, place * pool + order, -1)
    placing = as_bf16(lax.broadcasted_iota(jnp.int32, (inner * pool, rows), 0) == slot)
    lane = order + lax.rem(me_ref[0], LANES // pool) * pool
    lane_hot = as_bf16(lax.broadcasted_iota(jnp.int32, (LANES, rows), 0) == lane)
    here = live & (lax.broadcasted_iota(jnp.int32, (inner, rows), 0) == place)
    marked = jnp.where(here, (column_ref[...] + 1).astype(jnp.float32), 0.0)
    labels = lax.dot_general(
        marked.astype(jnp.bfloat16), lane_hot, NT, preferred_element_type=jnp.float32
    )

    copies[0].wait()
    copies[1].wait()
    prof_ref[...] = (prof_ref[...].astype(jnp.float32) * 0.5).astype(jnp.bfloat16)
    blocks = [pl.ds(i, ROWS) for i in range(0, rows, ROWS)]
    for i in range(hid // CHUNK):
        part = pl.ds(i * CHUNK, CHUNK)
        if i == 0:
            copies[2].wait()
        if i == hid // CHUNK // 2:
            copies[3].wait()
        for m in blocks:
            u = jnp.dot(prof_ref[m, :], w1_ref[:, part], preferred_element_type=jnp.float32)
            u = u + 0.5 * b1_ref[:, part]
            p = jnp.tanh(u) + 1.0
            hidden = u * p
            hidden_ref[m, part] = hidden.astype(jnp.bfloat16)
            factor_ref[m, part] = p + hidden * (2.0 - p)
    for copy in copies[4:]:
        copy.wait()
    scale = 0.5 * cw_ref[...]
    for n, m in enumerate(blocks):
        output = jnp.dot(hidden_ref[m, :], w2_ref[...], preferred_element_type=jnp.float32)
        misfit = scale * (output + b2_ref[...] - rad_ref[m, :].astype(jnp.float32))
        alive = lax.broadcasted_iota(jnp.int32, (ROWS, 1), 0) + n * ROWS < count_ref[0]
        rad_ref[m, :] = jnp.where(alive, misfit, 0.0).astype(jnp.bfloat16)
    for i in range(hid // CHUNK):
        part = pl.ds(i * CHUNK, CHUNK)
        for m in blocks:
            back = lax.dot_general(
                rad_ref[m, :], w2_ref[part, :], NT, preferred_element_type=jnp.float32
            )
            hidden_ref[m, part] = (back * factor_ref[m, part]).astype(jnp.bfloat16)
    for m in blocks:
        grads = lax.dot_general(
            hidden_ref[m, :], w1_ref[...], NT, preferred_element_type=jnp.float32
        )
        prof_ref[m, :] = grads.astype(jnp.bfloat16)
    grads = prof_ref[...]
    placed = jnp.dot(placing, grads, preferred_element_type=jnp.float32).astype(jnp.bfloat16)
    parts = width // LANES
    for k in range(parts):
        out_ref[:, k * pool : (k + 1) * pool, :] = placed[
            :, k * LANES : (k + 1) * LANES
        ].reshape(inner, pool, LANES)
    out_ref[:, parts * pool :, :] = jnp.broadcast_to(
        labels.reshape(inner, 1, LANES), (inner, LABEL_ROWS, LANES)
    ).astype(jnp.bfloat16)


def blocks_kernel(tiles, most, me_ref, got_ref, own_ref, other_ref):
    inner = got_ref.shape[0]
    outer = tiles // inner
    pool = outer * most
    group = LANES // pool
    parts = own_ref.shape[1] // LANES
    marks = got_ref[:, parts * pool :, :].astype(jnp.float32)[:, 0, :]
    index = lax.broadcasted_iota(jnp.int32, (outer * COL_DEV, LANES), 0)
    lane = lax.broadcasted_iota(jnp.int32, (1, LANES), 1) & (pool - 1)
    turn = lax.shift_right_arithmetic(lane, most.bit_length() - 1) ^ (
        lax.shift_right_arithmetic(me_ref[0], inner.bit_length() - 1)
    )
    chosen = []
    for g in range(inner // group):
        label = jnp.sum(marks[g * group : (g + 1) * group], axis=0, keepdims=True)
        label = label.astype(jnp.int32)
        code = jnp.where(label > 0, turn * COL_DEV + label - 1, -1)
        chosen.append(as_bf16(index == code))
    chosen = jnp.concatenate(chosen, axis=1)
    for k in range(parts):
        block = got_ref[:, k * pool : (k + 1) * pool, :].reshape(inner * pool, LANES)
        total = jnp.dot(chosen, block, preferred_element_type=jnp.float32)
        own_ref[:, k * LANES : (k + 1) * LANES] = total[:COL_DEV]
        other_ref[:, k * LANES : (k + 1) * LANES] = total[COL_DEV:].astype(jnp.bfloat16)


def per_device(
    profiles,
    radiances,
    inner_weight,
    inner_bias,
    outer_weight,
    outer_bias,
    channel_weight,
    counts,
    owner,
    column,
):
    tiles = lax.axis_size("tile")
    rows, width = profiles.shape
    hid = inner_weight.shape[1]
    chan = radiances.shape[1]
    most = max(2, 2 * rows // tiles)
    inner = tiles // OUTER
    pool = OUTER * most
    high = width // LANES * pool + LABEL_ROWS
    me = lax.axis_index("tile").astype(jnp.int32).reshape(1)
    vmem = pl.BlockSpec(memory_space=pltpu.VMEM)
    smem = pl.BlockSpec(memory_space=pltpu.SMEM)
    anywhere = pl.BlockSpec(memory_space=pl.ANY)
    bucket = pl.pallas_call(
        functools.partial(rows_kernel, tiles, most),
        out_shape=jax.ShapeDtypeStruct((inner, high, LANES), jnp.bfloat16),
        in_specs=[smem, smem, vmem, vmem] + [anywhere] * 7,
        out_specs=vmem,
        scratch_shapes=[
            pltpu.VMEM((rows, width), jnp.bfloat16),
            pltpu.VMEM((rows, chan), jnp.bfloat16),
            pltpu.VMEM((width, hid), jnp.bfloat16),
            pltpu.VMEM((1, hid), jnp.float32),
            pltpu.VMEM((hid, chan), jnp.bfloat16),
            pltpu.VMEM((1, chan), jnp.float32),
            pltpu.VMEM((1, chan), jnp.float32),
            pltpu.VMEM((rows, hid), jnp.bfloat16),
            pltpu.VMEM((rows, hid), jnp.float32),
            pltpu.SemaphoreType.DMA((8,)),
        ],
        compiler_params=pltpu.CompilerParams(vmem_limit_bytes=60 * 1024 * 1024),
        name="rows_kernel",
    )(
        me,
        counts,
        owner.reshape(1, rows),
        column.reshape(1, rows),
        profiles,
        radiances,
        inner_weight,
        inner_bias.reshape(1, hid),
        outer_weight,
        outer_bias.reshape(1, chan),
        channel_weight.reshape(1, chan),
    )
    halves = [[o * inner + i for i in range(inner)] for o in range(OUTER)]
    got = lax.all_to_all(
        bucket, "tile", split_axis=0, concat_axis=0, axis_index_groups=halves, tiled=True
    )
    own, other = pl.pallas_call(
        functools.partial(blocks_kernel, tiles, most),
        out_shape=[
            jax.ShapeDtypeStruct((COL_DEV, width), jnp.float32),
            jax.ShapeDtypeStruct((COL_DEV, width), jnp.bfloat16),
        ],
        in_specs=[smem, vmem],
        out_specs=[vmem, vmem],
        compiler_params=pltpu.CompilerParams(vmem_limit_bytes=24 * 1024 * 1024),
        name="blocks_kernel",
    )(me, got)
    pairs = [(t, (t + inner) % tiles) for t in range(tiles)]
    return own + lax.ppermute(other, "tile", pairs).astype(jnp.float32)


def solution(mesh):
    placed = (
        P(("group", "tile"), None),
        P(("group", "tile"), None),
        P(),
        P(),
        P(),
        P(),
        P(),
        P(("group", "tile")),
        P(("group", "tile"), None),
        P(("group", "tile")),
    )
    return jax.shard_map(
        per_device,
        mesh=mesh,
        in_specs=placed,
        out_specs=P(("group", "tile"), None),
        check_vma=False,
    )
```

```python
import functools

import jax
import jax.numpy as jnp
from jax import lax
from jax.experimental import pallas as pl
from jax.experimental.pallas import tpu as pltpu
from jax.sharding import PartitionSpec as P

COL_DEV = 128
CHUNK = 512
LANES = 128
LABEL_ROWS = 8
OUTER = 2
ROWS = 256
NT = (((1,), (1,)), ((), ()))


def as_bf16(mask):
    return mask.astype(jnp.float32).astype(jnp.bfloat16)


def rows_kernel(
    tiles,
    most,
    me_ref,
    count_ref,
    owner_ref,
    column_ref,
    prof_hbm,
    rad_hbm,
    w1_hbm,
    b1_hbm,
    w2_hbm,
    b2_hbm,
    cw_hbm,
    out_hbm,
    prof_ref,
    rad_ref,
    w1_ref,
    b1_ref,
    w2_ref,
    b2_ref,
    cw_ref,
    hidden_ref,
    factor_ref,
    out_ref,
    sems,
    out_sems,
):
    rows, width = prof_ref.shape
    hid = w1_ref.shape[1]
    chan = rad_ref.shape[1]
    starts = [0, CHUNK, 2 * CHUNK, 4 * CHUNK, hid]
    pieces = [pl.ds(lo, hi - lo) for lo, hi in zip(starts[:-1], starts[1:])]
    pairs = (
        [(prof_hbm, prof_ref), (b1_hbm, b1_ref)]
        + [(w1_hbm.at[:, piece], w1_ref.at[:, piece]) for piece in pieces]
        + [(w2_hbm, w2_ref), (rad_hbm, rad_ref), (b2_hbm, b2_ref), (cw_hbm, cw_ref)]
    )
    copies = [
        pltpu.make_async_copy(src, dst, sems.at[i]) for i, (src, dst) in enumerate(pairs)
    ]
    for copy in copies:
        copy.start()

    copies[0].wait()
    copies[1].wait()
    prof_ref[...] = (prof_ref[...].astype(jnp.float32) * 0.5).astype(jnp.bfloat16)
    blocks = [pl.ds(i, ROWS) for i in range(0, rows, ROWS)]
    for i in range(hid // CHUNK):
        part = pl.ds(i * CHUNK, CHUNK)
        if i * CHUNK in starts:
            copies[2 + starts.index(i * CHUNK)].wait()
        for m in blocks:
            u = jnp.dot(prof_ref[m, :], w1_ref[:, part], preferred_element_type=jnp.float32)
            u = u + 0.5 * b1_ref[:, part]
            p = jnp.tanh(u) + 1.0
            hidden = u * p
            hidden_ref[m, part] = hidden.astype(jnp.bfloat16)
            factor_ref[m, part] = p + hidden * (2.0 - p)
    for copy in copies[2 + len(pieces) :]:
        copy.wait()
    scale = 0.5 * cw_ref[...]
    for n, m in enumerate(blocks):
        output = jnp.dot(hidden_ref[m, :], w2_ref[...], preferred_element_type=jnp.float32)
        misfit = scale * (output + b2_ref[...] - rad_ref[m, :].astype(jnp.float32))
        alive = lax.broadcasted_iota(jnp.int32, (ROWS, 1), 0) + n * ROWS < count_ref[0]
        rad_ref[m, :] = jnp.where(alive, misfit, 0.0).astype(jnp.bfloat16)
    inner = out_ref.shape[0]
    live = lax.broadcasted_iota(jnp.int32, (1, rows), 1) < count_ref[0]
    owner = jnp.where(live, owner_ref[...], -1)
    mine = lax.broadcasted_iota(jnp.int32, (tiles, rows), 0) == owner
    one_hot = mine.astype(jnp.float32)
    upper = as_bf16(
        lax.broadcasted_iota(jnp.int32, (rows, rows), 0)
        <= lax.broadcasted_iota(jnp.int32, (rows, rows), 1)
    )
    running = jnp.dot(one_hot.astype(jnp.bfloat16), upper, preferred_element_type=jnp.float32)
    rank = jnp.sum(running * one_hot, axis=0, keepdims=True).astype(jnp.int32) - 1
    pool = tiles // inner * most
    place = owner & (inner - 1)
    order = lax.shift_right_arithmetic(owner, inner.bit_length() - 1) * most + rank
    slot = jnp.where(live, place * pool + order, -1)
    placing = as_bf16(lax.broadcasted_iota(jnp.int32, (inner * pool, rows), 0) == slot)
    lane = order + lax.rem(me_ref[0], LANES // pool) * pool
    lane_hot = as_bf16(lax.broadcasted_iota(jnp.int32, (LANES, rows), 0) == lane)
    here = live & (lax.broadcasted_iota(jnp.int32, (inner, rows), 0) == place)
    marked = jnp.where(here, (column_ref[...] + 1).astype(jnp.float32), 0.0)
    labels = lax.dot_general(
        marked.astype(jnp.bfloat16), lane_hot, NT, preferred_element_type=jnp.float32
    )

    for i in range(hid // CHUNK):
        part = pl.ds(i * CHUNK, CHUNK)
        for m in blocks:
            back = lax.dot_general(
                rad_ref[m, :], w2_ref[part, :], NT, preferred_element_type=jnp.float32
            )
            hidden_ref[m, part] = (back * factor_ref[m, part]).astype(jnp.bfloat16)
    for m in blocks:
        grads = lax.dot_general(
            hidden_ref[m, :], w1_ref[...], NT, preferred_element_type=jnp.float32
        )
        prof_ref[m, :] = grads.astype(jnp.bfloat16)
    grads = prof_ref[...]
    parts = width // LANES
    wide = ROWS // pool
    out_ref[:, parts * pool :, :] = jnp.broadcast_to(
        labels.reshape(inner, 1, LANES), (inner, LABEL_ROWS, LANES)
    ).astype(jnp.bfloat16)
    sent = []
    for n in range(inner // wide):
        placed = jnp.dot(
            placing[n * ROWS : (n + 1) * ROWS], grads, preferred_element_type=jnp.float32
        ).astype(jnp.bfloat16)
        some = pl.ds(n * wide, wide)
        for k in range(parts):
            out_ref[some, k * pool : (k + 1) * pool, :] = placed[
                :, k * LANES : (k + 1) * LANES
            ].reshape(wide, pool, LANES)
        sent.append(pltpu.make_async_copy(out_ref.at[some], out_hbm.at[some], out_sems.at[n]))
        sent[-1].start()
    for copy in sent:
        copy.wait()


def blocks_kernel(tiles, most, me_ref, got_ref, own_ref, other_ref):
    inner = got_ref.shape[0]
    outer = tiles // inner
    pool = outer * most
    group = LANES // pool
    parts = own_ref.shape[1] // LANES
    marks = got_ref[:, parts * pool :, :].astype(jnp.float32)[:, 0, :]
    index = lax.broadcasted_iota(jnp.int32, (outer * COL_DEV, LANES), 0)
    lane = lax.broadcasted_iota(jnp.int32, (1, LANES), 1) & (pool - 1)
    turn = lax.shift_right_arithmetic(lane, most.bit_length() - 1) ^ (
        lax.shift_right_arithmetic(me_ref[0], inner.bit_length() - 1)
    )
    chosen = []
    for g in range(inner // group):
        label = jnp.sum(marks[g * group : (g + 1) * group], axis=0, keepdims=True)
        label = label.astype(jnp.int32)
        code = jnp.where(label > 0, turn * COL_DEV + label - 1, -1)
        chosen.append(as_bf16(index == code))
    chosen = jnp.concatenate(chosen, axis=1)
    for k in range(parts):
        block = got_ref[:, k * pool : (k + 1) * pool, :].reshape(inner * pool, LANES)
        total = jnp.dot(chosen, block, preferred_element_type=jnp.float32)
        own_ref[:, k * LANES : (k + 1) * LANES] = total[:COL_DEV]
        other_ref[:, k * LANES : (k + 1) * LANES] = total[COL_DEV:].astype(jnp.bfloat16)


def per_device(
    profiles,
    radiances,
    inner_weight,
    inner_bias,
    outer_weight,
    outer_bias,
    channel_weight,
    counts,
    owner,
    column,
):
    tiles = lax.axis_size("tile")
    rows, width = profiles.shape
    hid = inner_weight.shape[1]
    chan = radiances.shape[1]
    most = max(2, 2 * rows // tiles)
    inner = tiles // OUTER
    pool = OUTER * most
    high = width // LANES * pool + LABEL_ROWS
    me = lax.axis_index("tile").astype(jnp.int32).reshape(1)
    vmem = pl.BlockSpec(memory_space=pltpu.VMEM)
    smem = pl.BlockSpec(memory_space=pltpu.SMEM)
    anywhere = pl.BlockSpec(memory_space=pl.ANY)
    bucket = pl.pallas_call(
        functools.partial(rows_kernel, tiles, most),
        out_shape=jax.ShapeDtypeStruct((inner, high, LANES), jnp.bfloat16),
        in_specs=[smem, smem, vmem, vmem] + [anywhere] * 7,
        out_specs=anywhere,
        scratch_shapes=[
            pltpu.VMEM((rows, width), jnp.bfloat16),
            pltpu.VMEM((rows, chan), jnp.bfloat16),
            pltpu.VMEM((width, hid), jnp.bfloat16),
            pltpu.VMEM((1, hid), jnp.float32),
            pltpu.VMEM((hid, chan), jnp.bfloat16),
            pltpu.VMEM((1, chan), jnp.float32),
            pltpu.VMEM((1, chan), jnp.float32),
            pltpu.VMEM((rows, hid), jnp.bfloat16),
            pltpu.VMEM((rows, hid), jnp.float32),
            pltpu.VMEM((inner, high, LANES), jnp.bfloat16),
            pltpu.SemaphoreType.DMA((10,)),
            pltpu.SemaphoreType.DMA((inner * pool // ROWS,)),
        ],
        compiler_params=pltpu.CompilerParams(vmem_limit_bytes=60 * 1024 * 1024),
        name="rows_kernel",
    )(
        me,
        counts,
        owner.reshape(1, rows),
        column.reshape(1, rows),
        profiles,
        radiances,
        inner_weight,
        inner_bias.reshape(1, hid),
        outer_weight,
        outer_bias.reshape(1, chan),
        channel_weight.reshape(1, chan),
    )
    halves = [[o * inner + i for i in range(inner)] for o in range(OUTER)]
    got = lax.all_to_all(
        bucket, "tile", split_axis=0, concat_axis=0, axis_index_groups=halves, tiled=True
    )
    own, other = pl.pallas_call(
        functools.partial(blocks_kernel, tiles, most),
        out_shape=[
            jax.ShapeDtypeStruct((COL_DEV, width), jnp.float32),
            jax.ShapeDtypeStruct((COL_DEV, width), jnp.bfloat16),
        ],
        in_specs=[smem, vmem],
        out_specs=[vmem, vmem],
        compiler_params=pltpu.CompilerParams(vmem_limit_bytes=24 * 1024 * 1024),
        name="blocks_kernel",
    )(me, got)
    pairs = [(t, (t + inner) % tiles) for t in range(tiles)]
    return own + lax.ppermute(other, "tile", pairs).astype(jnp.float32)


def solution(mesh):
    placed = (
        P(("group", "tile"), None),
        P(("group", "tile"), None),
        P(),
        P(),
        P(),
        P(),
        P(),
        P(("group", "tile")),
        P(("group", "tile"), None),
        P(("group", "tile")),
    )
    return jax.shard_map(
        per_device,
        mesh=mesh,
        in_specs=placed,
        out_specs=P(("group", "tile"), None),
        check_vma=False,
    )
```

```python
import functools

import jax
import jax.numpy as jnp
from jax import lax
from jax.experimental import pallas as pl
from jax.experimental.pallas import tpu as pltpu
from jax.sharding import PartitionSpec as P

COL_DEV = 128
CHUNK = 512
LANES = 128
LABEL_ROWS = 8
LOG2E = 1.4426950408889634
OUTER = 2
ROWS = 256
NT = (((1,), (1,)), ((), ()))


def as_bf16(mask):
    return mask.astype(jnp.float32).astype(jnp.bfloat16)


def rows_kernel(
    tiles,
    most,
    me_ref,
    count_ref,
    owner_ref,
    column_ref,
    prof_hbm,
    rad_hbm,
    w1_hbm,
    b1_hbm,
    w2_hbm,
    b2_hbm,
    cw_hbm,
    out_hbm,
    prof_ref,
    rad_ref,
    w1_ref,
    b1_ref,
    w2_ref,
    b2_ref,
    cw_ref,
    hidden_ref,
    factor_ref,
    out_ref,
    sems,
    out_sems,
):
    rows, width = prof_ref.shape
    hid = w1_ref.shape[1]
    chan = rad_ref.shape[1]
    starts = [0, CHUNK, 2 * CHUNK, 4 * CHUNK, hid]
    pieces = [pl.ds(lo, hi - lo) for lo, hi in zip(starts[:-1], starts[1:])]
    pairs = (
        [(prof_hbm, prof_ref), (b1_hbm, b1_ref)]
        + [(w1_hbm.at[:, piece], w1_ref.at[:, piece]) for piece in pieces]
        + [(w2_hbm, w2_ref), (rad_hbm, rad_ref), (b2_hbm, b2_ref), (cw_hbm, cw_ref)]
    )
    copies = [
        pltpu.make_async_copy(src, dst, sems.at[i]) for i, (src, dst) in enumerate(pairs)
    ]
    for copy in copies:
        copy.start()

    copies[0].wait()
    copies[1].wait()
    blocks = [pl.ds(i, ROWS) for i in range(0, rows, ROWS)]
    for i in range(hid // CHUNK):
        part = pl.ds(i * CHUNK, CHUNK)
        if i * CHUNK in starts:
            copies[2 + starts.index(i * CHUNK)].wait()
        for m in blocks:
            x = jnp.dot(prof_ref[m, :], w1_ref[:, part], preferred_element_type=jnp.float32)
            x = x + b1_ref[:, part]
            sigma = pl.reciprocal(1.0 + jnp.exp2(x * -LOG2E), approx=True)
            hidden = x * sigma
            hidden_ref[m, part] = hidden.astype(jnp.bfloat16)
            factor_ref[m, part] = sigma + hidden * (1.0 - sigma)
    for copy in copies[2 + len(pieces) :]:
        copy.wait()
    scale = cw_ref[...]
    for n, m in enumerate(blocks):
        output = jnp.dot(hidden_ref[m, :], w2_ref[...], preferred_element_type=jnp.float32)
        misfit = scale * (output + b2_ref[...] - rad_ref[m, :].astype(jnp.float32))
        alive = lax.broadcasted_iota(jnp.int32, (ROWS, 1), 0) + n * ROWS < count_ref[0]
        rad_ref[m, :] = jnp.where(alive, misfit, 0.0).astype(jnp.bfloat16)
    inner = out_ref.shape[0]
    live = lax.broadcasted_iota(jnp.int32, (1, rows), 1) < count_ref[0]
    owner = jnp.where(live, owner_ref[...], -1)
    mine = lax.broadcasted_iota(jnp.int32, (tiles, rows), 0) == owner
    one_hot = mine.astype(jnp.float32)
    upper = as_bf16(
        lax.broadcasted_iota(jnp.int32, (rows, rows), 0)
        <= lax.broadcasted_iota(jnp.int32, (rows, rows), 1)
    )
    running = jnp.dot(one_hot.astype(jnp.bfloat16), upper, preferred_element_type=jnp.float32)
    rank = jnp.sum(running * one_hot, axis=0, keepdims=True).astype(jnp.int32) - 1
    pool = tiles // inner * most
    place = owner & (inner - 1)
    order = lax.shift_right_arithmetic(owner, inner.bit_length() - 1) * most + rank
    slot = jnp.where(live, place * pool + order, -1)
    placing = as_bf16(lax.broadcasted_iota(jnp.int32, (inner * pool, rows), 0) == slot)
    lane = order + lax.rem(me_ref[0], LANES // pool) * pool
    lane_hot = as_bf16(lax.broadcasted_iota(jnp.int32, (LANES, rows), 0) == lane)
    here = live & (lax.broadcasted_iota(jnp.int32, (inner, rows), 0) == place)
    marked = jnp.where(here, (column_ref[...] + 1).astype(jnp.float32), 0.0)
    labels = lax.dot_general(
        marked.astype(jnp.bfloat16), lane_hot, NT, preferred_element_type=jnp.float32
    )

    for i in range(hid // CHUNK):
        part = pl.ds(i * CHUNK, CHUNK)
        for m in blocks:
            back = lax.dot_general(
                rad_ref[m, :], w2_ref[part, :], NT, preferred_element_type=jnp.float32
            )
            hidden_ref[m, part] = (back * factor_ref[m, part]).astype(jnp.bfloat16)
    for m in blocks:
        grads = lax.dot_general(
            hidden_ref[m, :], w1_ref[...], NT, preferred_element_type=jnp.float32
        )
        prof_ref[m, :] = grads.astype(jnp.bfloat16)
    grads = prof_ref[...]
    parts = width // LANES
    wide = ROWS // pool
    out_ref[:, parts * pool :, :] = jnp.broadcast_to(
        labels.reshape(inner, 1, LANES), (inner, LABEL_ROWS, LANES)
    ).astype(jnp.bfloat16)
    sent = []
    for n in range(inner // wide):
        placed = jnp.dot(
            placing[n * ROWS : (n + 1) * ROWS], grads, preferred_element_type=jnp.float32
        ).astype(jnp.bfloat16)
        some = pl.ds(n * wide, wide)
        for k in range(parts):
            out_ref[some, k * pool : (k + 1) * pool, :] = placed[
                :, k * LANES : (k + 1) * LANES
            ].reshape(wide, pool, LANES)
        sent.append(pltpu.make_async_copy(out_ref.at[some], out_hbm.at[some], out_sems.at[n]))
        sent[-1].start()
    for copy in sent:
        copy.wait()


def blocks_kernel(tiles, most, me_ref, got_ref, own_ref, other_ref):
    inner = got_ref.shape[0]
    outer = tiles // inner
    pool = outer * most
    group = LANES // pool
    parts = own_ref.shape[1] // LANES
    marks = got_ref[:, parts * pool :, :].astype(jnp.float32)[:, 0, :]
    index = lax.broadcasted_iota(jnp.int32, (outer * COL_DEV, LANES), 0)
    lane = lax.broadcasted_iota(jnp.int32, (1, LANES), 1) & (pool - 1)
    turn = lax.shift_right_arithmetic(lane, most.bit_length() - 1) ^ (
        lax.shift_right_arithmetic(me_ref[0], inner.bit_length() - 1)
    )
    chosen = []
    for g in range(inner // group):
        label = jnp.sum(marks[g * group : (g + 1) * group], axis=0, keepdims=True)
        label = label.astype(jnp.int32)
        code = jnp.where(label > 0, turn * COL_DEV + label - 1, -1)
        chosen.append(as_bf16(index == code))
    chosen = jnp.concatenate(chosen, axis=1)
    for k in range(parts):
        block = got_ref[:, k * pool : (k + 1) * pool, :].reshape(inner * pool, LANES)
        total = jnp.dot(chosen, block, preferred_element_type=jnp.float32)
        own_ref[:, k * LANES : (k + 1) * LANES] = total[:COL_DEV]
        other_ref[:, k * LANES : (k + 1) * LANES] = total[COL_DEV:].astype(jnp.bfloat16)


def per_device(
    profiles,
    radiances,
    inner_weight,
    inner_bias,
    outer_weight,
    outer_bias,
    channel_weight,
    counts,
    owner,
    column,
):
    tiles = lax.axis_size("tile")
    rows, width = profiles.shape
    hid = inner_weight.shape[1]
    chan = radiances.shape[1]
    most = max(2, 2 * rows // tiles)
    inner = tiles // OUTER
    pool = OUTER * most
    high = width // LANES * pool + LABEL_ROWS
    me = lax.axis_index("tile").astype(jnp.int32).reshape(1)
    vmem = pl.BlockSpec(memory_space=pltpu.VMEM)
    smem = pl.BlockSpec(memory_space=pltpu.SMEM)
    anywhere = pl.BlockSpec(memory_space=pl.ANY)
    bucket = pl.pallas_call(
        functools.partial(rows_kernel, tiles, most),
        out_shape=jax.ShapeDtypeStruct((inner, high, LANES), jnp.bfloat16),
        in_specs=[smem, smem, vmem, vmem] + [anywhere] * 7,
        out_specs=anywhere,
        scratch_shapes=[
            pltpu.VMEM((rows, width), jnp.bfloat16),
            pltpu.VMEM((rows, chan), jnp.bfloat16),
            pltpu.VMEM((width, hid), jnp.bfloat16),
            pltpu.VMEM((1, hid), jnp.float32),
            pltpu.VMEM((hid, chan), jnp.bfloat16),
            pltpu.VMEM((1, chan), jnp.float32),
            pltpu.VMEM((1, chan), jnp.float32),
            pltpu.VMEM((rows, hid), jnp.bfloat16),
            pltpu.VMEM((rows, hid), jnp.float32),
            pltpu.VMEM((inner, high, LANES), jnp.bfloat16),
            pltpu.SemaphoreType.DMA((10,)),
            pltpu.SemaphoreType.DMA((inner * pool // ROWS,)),
        ],
        compiler_params=pltpu.CompilerParams(vmem_limit_bytes=60 * 1024 * 1024),
        name="rows_kernel",
    )(
        me,
        counts,
        owner.reshape(1, rows),
        column.reshape(1, rows),
        profiles,
        radiances,
        inner_weight,
        inner_bias.reshape(1, hid),
        outer_weight,
        outer_bias.reshape(1, chan),
        channel_weight.reshape(1, chan),
    )
    halves = [[o * inner + i for i in range(inner)] for o in range(OUTER)]
    got = lax.all_to_all(
        bucket, "tile", split_axis=0, concat_axis=0, axis_index_groups=halves, tiled=True
    )
    own, other = pl.pallas_call(
        functools.partial(blocks_kernel, tiles, most),
        out_shape=[
            jax.ShapeDtypeStruct((COL_DEV, width), jnp.float32),
            jax.ShapeDtypeStruct((COL_DEV, width), jnp.bfloat16),
        ],
        in_specs=[smem, vmem],
        out_specs=[vmem, vmem],
        compiler_params=pltpu.CompilerParams(vmem_limit_bytes=24 * 1024 * 1024),
        name="blocks_kernel",
    )(me, got)
    pairs = [(t, (t + inner) % tiles) for t in range(tiles)]
    return own + lax.ppermute(other, "tile", pairs).astype(jnp.float32)


def solution(mesh):
    placed = (
        P(("group", "tile"), None),
        P(("group", "tile"), None),
        P(),
        P(),
        P(),
        P(),
        P(),
        P(("group", "tile")),
        P(("group", "tile"), None),
        P(("group", "tile")),
    )
    return jax.shard_map(
        per_device,
        mesh=mesh,
        in_specs=placed,
        out_specs=P(("group", "tile"), None),
        check_vma=False,
    )
```

```python
import functools

import jax
import jax.numpy as jnp
from jax import lax
from jax.experimental import pallas as pl
from jax.experimental.pallas import tpu as pltpu
from jax.sharding import PartitionSpec as P

COL_DEV = 128
CHUNK = 256
LANES = 128
LABEL_ROWS = 8
OUTER = 2
ROWS = 256
NT = (((1,), (1,)), ((), ()))


def as_bf16(mask):
    return mask.astype(jnp.float32).astype(jnp.bfloat16)


def rows_kernel(
    tiles,
    most,
    me_ref,
    count_ref,
    owner_ref,
    column_ref,
    prof_hbm,
    rad_hbm,
    w1_hbm,
    b1_hbm,
    w2_hbm,
    b2_hbm,
    cw_hbm,
    out_hbm,
    prof_ref,
    rad_ref,
    w1_ref,
    b1_ref,
    w2_ref,
    b2_ref,
    cw_ref,
    hidden_ref,
    factor_ref,
    out_ref,
    sems,
    out_sems,
):
    rows, width = prof_ref.shape
    hid = w1_ref.shape[1]
    chan = rad_ref.shape[1]
    starts = [0, 2 * CHUNK, 4 * CHUNK, 8 * CHUNK, hid]
    pieces = [pl.ds(lo, hi - lo) for lo, hi in zip(starts[:-1], starts[1:])]
    pairs = (
        [(prof_hbm, prof_ref), (b1_hbm, b1_ref)]
        + [(w1_hbm.at[:, piece], w1_ref.at[:, piece]) for piece in pieces]
        + [(w2_hbm, w2_ref), (rad_hbm, rad_ref), (b2_hbm, b2_ref), (cw_hbm, cw_ref)]
    )
    copies = [
        pltpu.make_async_copy(src, dst, sems.at[i]) for i, (src, dst) in enumerate(pairs)
    ]
    for copy in copies:
        copy.start()

    copies[0].wait()
    copies[1].wait()
    prof_ref[...] = (prof_ref[...].astype(jnp.float32) * 0.5).astype(jnp.bfloat16)
    blocks = [pl.ds(i, ROWS) for i in range(0, rows, ROWS)]
    for i in range(hid // CHUNK):
        part = pl.ds(i * CHUNK, CHUNK)
        if i * CHUNK in starts:
            copies[2 + starts.index(i * CHUNK)].wait()
        for m in blocks:
            u = jnp.dot(prof_ref[m, :], w1_ref[:, part], preferred_element_type=jnp.float32)
            u = u + 0.5 * b1_ref[:, part]
            p = jnp.tanh(u) + 1.0
            hidden = u * p
            hidden_ref[m, part] = hidden.astype(jnp.bfloat16)
            factor_ref[m, part] = p + hidden * (2.0 - p)
    for copy in copies[2 + len(pieces) :]:
        copy.wait()
    scale = 0.5 * cw_ref[...]
    for n, m in enumerate(blocks):
        output = jnp.dot(hidden_ref[m, :], w2_ref[...], preferred_element_type=jnp.float32)
        misfit = scale * (output + b2_ref[...] - rad_ref[m, :].astype(jnp.float32))
        alive = lax.broadcasted_iota(jnp.int32, (ROWS, 1), 0) + n * ROWS < count_ref[0]
        rad_ref[m, :] = jnp.where(alive, misfit, 0.0).astype(jnp.bfloat16)
    inner = out_ref.shape[0]
    live = lax.broadcasted_iota(jnp.int32, (1, rows), 1) < count_ref[0]
    owner = jnp.where(live, owner_ref[...], -1)
    mine = lax.broadcasted_iota(jnp.int32, (tiles, rows), 0) == owner
    one_hot = mine.astype(jnp.float32)
    upper = as_bf16(
        lax.broadcasted_iota(jnp.int32, (rows, rows), 0)
        <= lax.broadcasted_iota(jnp.int32, (rows, rows), 1)
    )
    running = jnp.dot(one_hot.astype(jnp.bfloat16), upper, preferred_element_type=jnp.float32)
    rank = jnp.sum(running * one_hot, axis=0, keepdims=True).astype(jnp.int32) - 1
    pool = tiles // inner * most
    place = owner & (inner - 1)
    order = lax.shift_right_arithmetic(owner, inner.bit_length() - 1) * most + rank
    slot = jnp.where(live, place * pool + order, -1)
    placing = as_bf16(lax.broadcasted_iota(jnp.int32, (inner * pool, rows), 0) == slot)
    lane = order + lax.rem(me_ref[0], LANES // pool) * pool
    lane_hot = as_bf16(lax.broadcasted_iota(jnp.int32, (LANES, rows), 0) == lane)
    here = live & (lax.broadcasted_iota(jnp.int32, (inner, rows), 0) == place)
    marked = jnp.where(here, (column_ref[...] + 1).astype(jnp.float32), 0.0)
    labels = lax.dot_general(
        marked.astype(jnp.bfloat16), lane_hot, NT, preferred_element_type=jnp.float32
    )

    for i in range(hid // CHUNK):
        part = pl.ds(i * CHUNK, CHUNK)
        for m in blocks:
            back = lax.dot_general(
                rad_ref[m, :], w2_ref[part, :], NT, preferred_element_type=jnp.float32
            )
            hidden_ref[m, part] = (back * factor_ref[m, part]).astype(jnp.bfloat16)
    for m in blocks:
        grads = lax.dot_general(
            hidden_ref[m, :], w1_ref[...], NT, preferred_element_type=jnp.float32
        )
        prof_ref[m, :] = grads.astype(jnp.bfloat16)
    grads = prof_ref[...]
    parts = width // LANES
    wide = ROWS // pool
    out_ref[:, parts * pool :, :] = jnp.broadcast_to(
        labels.reshape(inner, 1, LANES), (inner, LABEL_ROWS, LANES)
    ).astype(jnp.bfloat16)
    sent = []
    for n in range(inner // wide):
        placed = jnp.dot(
            placing[n * ROWS : (n + 1) * ROWS], grads, preferred_element_type=jnp.float32
        ).astype(jnp.bfloat16)
        some = pl.ds(n * wide, wide)
        for k in range(parts):
            out_ref[some, k * pool : (k + 1) * pool, :] = placed[
                :, k * LANES : (k + 1) * LANES
            ].reshape(wide, pool, LANES)
        sent.append(pltpu.make_async_copy(out_ref.at[some], out_hbm.at[some], out_sems.at[n]))
        sent[-1].start()
    for copy in sent:
        copy.wait()


def blocks_kernel(tiles, most, me_ref, got_ref, own_ref, other_ref):
    inner = got_ref.shape[0]
    outer = tiles // inner
    pool = outer * most
    group = LANES // pool
    parts = own_ref.shape[1] // LANES
    marks = got_ref[:, parts * pool :, :].astype(jnp.float32)[:, 0, :]
    index = lax.broadcasted_iota(jnp.int32, (outer * COL_DEV, LANES), 0)
    lane = lax.broadcasted_iota(jnp.int32, (1, LANES), 1) & (pool - 1)
    turn = lax.shift_right_arithmetic(lane, most.bit_length() - 1) ^ (
        lax.shift_right_arithmetic(me_ref[0], inner.bit_length() - 1)
    )
    chosen = []
    for g in range(inner // group):
        label = jnp.sum(marks[g * group : (g + 1) * group], axis=0, keepdims=True)
        label = label.astype(jnp.int32)
        code = jnp.where(label > 0, turn * COL_DEV + label - 1, -1)
        chosen.append(as_bf16(index == code))
    chosen = jnp.concatenate(chosen, axis=1)
    for k in range(parts):
        block = got_ref[:, k * pool : (k + 1) * pool, :].reshape(inner * pool, LANES)
        total = jnp.dot(chosen, block, preferred_element_type=jnp.float32)
        own_ref[:, k * LANES : (k + 1) * LANES] = total[:COL_DEV]
        other_ref[:, k * LANES : (k + 1) * LANES] = total[COL_DEV:].astype(jnp.bfloat16)


def per_device(
    profiles,
    radiances,
    inner_weight,
    inner_bias,
    outer_weight,
    outer_bias,
    channel_weight,
    counts,
    owner,
    column,
):
    tiles = lax.axis_size("tile")
    rows, width = profiles.shape
    hid = inner_weight.shape[1]
    chan = radiances.shape[1]
    most = max(2, 2 * rows // tiles)
    inner = tiles // OUTER
    pool = OUTER * most
    high = width // LANES * pool + LABEL_ROWS
    me = lax.axis_index("tile").astype(jnp.int32).reshape(1)
    vmem = pl.BlockSpec(memory_space=pltpu.VMEM)
    smem = pl.BlockSpec(memory_space=pltpu.SMEM)
    anywhere = pl.BlockSpec(memory_space=pl.ANY)
    bucket = pl.pallas_call(
        functools.partial(rows_kernel, tiles, most),
        out_shape=jax.ShapeDtypeStruct((inner, high, LANES), jnp.bfloat16),
        in_specs=[smem, smem, vmem, vmem] + [anywhere] * 7,
        out_specs=anywhere,
        scratch_shapes=[
            pltpu.VMEM((rows, width), jnp.bfloat16),
            pltpu.VMEM((rows, chan), jnp.bfloat16),
            pltpu.VMEM((width, hid), jnp.bfloat16),
            pltpu.VMEM((1, hid), jnp.float32),
            pltpu.VMEM((hid, chan), jnp.bfloat16),
            pltpu.VMEM((1, chan), jnp.float32),
            pltpu.VMEM((1, chan), jnp.float32),
            pltpu.VMEM((rows, hid), jnp.bfloat16),
            pltpu.VMEM((rows, hid), jnp.float32),
            pltpu.VMEM((inner, high, LANES), jnp.bfloat16),
            pltpu.SemaphoreType.DMA((10,)),
            pltpu.SemaphoreType.DMA((inner * pool // ROWS,)),
        ],
        compiler_params=pltpu.CompilerParams(vmem_limit_bytes=60 * 1024 * 1024),
        name="rows_kernel",
    )(
        me,
        counts,
        owner.reshape(1, rows),
        column.reshape(1, rows),
        profiles,
        radiances,
        inner_weight,
        inner_bias.reshape(1, hid),
        outer_weight,
        outer_bias.reshape(1, chan),
        channel_weight.reshape(1, chan),
    )
    halves = [[o * inner + i for i in range(inner)] for o in range(OUTER)]
    got = lax.all_to_all(
        bucket, "tile", split_axis=0, concat_axis=0, axis_index_groups=halves, tiled=True
    )
    own, other = pl.pallas_call(
        functools.partial(blocks_kernel, tiles, most),
        out_shape=[
            jax.ShapeDtypeStruct((COL_DEV, width), jnp.float32),
            jax.ShapeDtypeStruct((COL_DEV, width), jnp.bfloat16),
        ],
        in_specs=[smem, vmem],
        out_specs=[vmem, vmem],
        compiler_params=pltpu.CompilerParams(vmem_limit_bytes=24 * 1024 * 1024),
        name="blocks_kernel",
    )(me, got)
    pairs = [(t, (t + inner) % tiles) for t in range(tiles)]
    return own + lax.ppermute(other, "tile", pairs).astype(jnp.float32)


def solution(mesh):
    placed = (
        P(("group", "tile"), None),
        P(("group", "tile"), None),
        P(),
        P(),
        P(),
        P(),
        P(),
        P(("group", "tile")),
        P(("group", "tile"), None),
        P(("group", "tile")),
    )
    return jax.shard_map(
        per_device,
        mesh=mesh,
        in_specs=placed,
        out_specs=P(("group", "tile"), None),
        check_vma=False,
    )
```

```python
import functools

import jax
import jax.numpy as jnp
from jax import lax
from jax.experimental import pallas as pl
from jax.experimental.pallas import tpu as pltpu
from jax.sharding import PartitionSpec as P

COL_DEV = 128
CHUNK = 256
LANES = 128
LABEL_ROWS = 8
OUTER = 2
ROWS = 256
NT = (((1,), (1,)), ((), ()))


def as_bf16(mask):
    return mask.astype(jnp.float32).astype(jnp.bfloat16)


def rows_kernel(
    tiles,
    most,
    me_ref,
    count_ref,
    owner_ref,
    column_ref,
    prof_hbm,
    rad_hbm,
    w1_hbm,
    b1_hbm,
    w2_hbm,
    b2_hbm,
    cw_hbm,
    out_hbm,
    prof_ref,
    rad_ref,
    w1_ref,
    b1_ref,
    w2_ref,
    b2_ref,
    cw_ref,
    hidden_ref,
    factor_ref,
    out_ref,
    sems,
    out_sems,
):
    rows, width = prof_ref.shape
    hid = w1_ref.shape[1]
    chan = rad_ref.shape[1]
    starts = [0, hid // 4, hid]
    pieces = [pl.ds(lo, hi - lo) for lo, hi in zip(starts[:-1], starts[1:])]
    pairs = (
        [(prof_hbm, prof_ref), (b1_hbm, b1_ref)]
        + [(w1_hbm.at[:, piece], w1_ref.at[:, piece]) for piece in pieces]
        + [(w2_hbm, w2_ref), (rad_hbm, rad_ref), (b2_hbm, b2_ref), (cw_hbm, cw_ref)]
    )
    copies = [
        pltpu.make_async_copy(src, dst, sems.at[i]) for i, (src, dst) in enumerate(pairs)
    ]
    for copy in copies:
        copy.start()

    inner = out_ref.shape[0]
    live = lax.broadcasted_iota(jnp.int32, (1, rows), 1) < count_ref[0]
    owner = jnp.where(live, owner_ref[...], -1)
    mine = lax.broadcasted_iota(jnp.int32, (tiles, rows), 0) == owner
    one_hot = mine.astype(jnp.float32)
    upper = as_bf16(
        lax.broadcasted_iota(jnp.int32, (rows, rows), 0)
        <= lax.broadcasted_iota(jnp.int32, (rows, rows), 1)
    )
    running = jnp.dot(one_hot.astype(jnp.bfloat16), upper, preferred_element_type=jnp.float32)
    rank = jnp.sum(running * one_hot, axis=0, keepdims=True).astype(jnp.int32) - 1
    pool = tiles // inner * most
    place = owner & (inner - 1)
    order = lax.shift_right_arithmetic(owner, inner.bit_length() - 1) * most + rank
    slot = jnp.where(live, place * pool + order, -1)
    placing = as_bf16(lax.broadcasted_iota(jnp.int32, (inner * pool, rows), 0) == slot)
    lane = order + lax.rem(me_ref[0], LANES // pool) * pool
    lane_hot = as_bf16(lax.broadcasted_iota(jnp.int32, (LANES, rows), 0) == lane)
    here = live & (lax.broadcasted_iota(jnp.int32, (inner, rows), 0) == place)
    marked = jnp.where(here, (column_ref[...] + 1).astype(jnp.float32), 0.0)
    labels = lax.dot_general(
        marked.astype(jnp.bfloat16), lane_hot, NT, preferred_element_type=jnp.float32
    )

    parts = width // LANES
    out_ref[:, parts * pool :, :] = jnp.broadcast_to(
        labels.reshape(inner, 1, LANES), (inner, LABEL_ROWS, LANES)
    ).astype(jnp.bfloat16)

    copies[0].wait()
    copies[1].wait()
    prof_ref[...] = (prof_ref[...].astype(jnp.float32) * 0.5).astype(jnp.bfloat16)
    blocks = [pl.ds(i, ROWS) for i in range(0, rows, ROWS)]
    for i in range(hid // CHUNK):
        part = pl.ds(i * CHUNK, CHUNK)
        if i * CHUNK in starts:
            copies[2 + starts.index(i * CHUNK)].wait()
        for m in blocks:
            u = jnp.dot(prof_ref[m, :], w1_ref[:, part], preferred_element_type=jnp.float32)
            u = u + 0.5 * b1_ref[:, part]
            p = jnp.tanh(u) + 1.0
            hidden = u * p
            hidden_ref[m, part] = hidden.astype(jnp.bfloat16)
            factor_ref[m, part] = p + hidden * (2.0 - p)
    for copy in copies[2 + len(pieces) :]:
        copy.wait()
    scale = 0.5 * cw_ref[...]
    for n, m in enumerate(blocks):
        output = jnp.dot(hidden_ref[m, :], w2_ref[...], preferred_element_type=jnp.float32)
        misfit = scale * (output + b2_ref[...] - rad_ref[m, :].astype(jnp.float32))
        alive = lax.broadcasted_iota(jnp.int32, (ROWS, 1), 0) + n * ROWS < count_ref[0]
        rad_ref[m, :] = jnp.where(alive, misfit, 0.0).astype(jnp.bfloat16)
    for i in range(hid // CHUNK):
        part = pl.ds(i * CHUNK, CHUNK)
        for m in blocks:
            back = lax.dot_general(
                rad_ref[m, :], w2_ref[part, :], NT, preferred_element_type=jnp.float32
            )
            hidden_ref[m, part] = (back * factor_ref[m, part]).astype(jnp.bfloat16)
    for m in blocks:
        grads = lax.dot_general(
            hidden_ref[m, :], w1_ref[...], NT, preferred_element_type=jnp.float32
        )
        prof_ref[m, :] = grads.astype(jnp.bfloat16)
    grads = prof_ref[...]
    wide = ROWS // pool
    sent = []
    for n in range(inner // wide):
        placed = jnp.dot(
            placing[n * ROWS : (n + 1) * ROWS], grads, preferred_element_type=jnp.float32
        ).astype(jnp.bfloat16)
        some = pl.ds(n * wide, wide)
        for k in range(parts):
            out_ref[some, k * pool : (k + 1) * pool, :] = placed[
                :, k * LANES : (k + 1) * LANES
            ].reshape(wide, pool, LANES)
        sent.append(pltpu.make_async_copy(out_ref.at[some], out_hbm.at[some], out_sems.at[n]))
        sent[-1].start()
    for copy in sent:
        copy.wait()


def blocks_kernel(tiles, most, me_ref, got_ref, own_ref, other_ref):
    inner = got_ref.shape[0]
    outer = tiles // inner
    pool = outer * most
    group = LANES // pool
    parts = own_ref.shape[1] // LANES
    marks = got_ref[:, parts * pool :, :].astype(jnp.float32)[:, 0, :]
    index = lax.broadcasted_iota(jnp.int32, (outer * COL_DEV, LANES), 0)
    lane = lax.broadcasted_iota(jnp.int32, (1, LANES), 1) & (pool - 1)
    turn = lax.shift_right_arithmetic(lane, most.bit_length() - 1) ^ (
        lax.shift_right_arithmetic(me_ref[0], inner.bit_length() - 1)
    )
    chosen = []
    for g in range(inner // group):
        label = jnp.sum(marks[g * group : (g + 1) * group], axis=0, keepdims=True)
        label = label.astype(jnp.int32)
        code = jnp.where(label > 0, turn * COL_DEV + label - 1, -1)
        chosen.append(as_bf16(index == code))
    chosen = jnp.concatenate(chosen, axis=1)
    for k in range(parts):
        block = got_ref[:, k * pool : (k + 1) * pool, :].reshape(inner * pool, LANES)
        total = jnp.dot(chosen, block, preferred_element_type=jnp.float32)
        own_ref[:, k * LANES : (k + 1) * LANES] = total[:COL_DEV]
        other_ref[:, k * LANES : (k + 1) * LANES] = total[COL_DEV:].astype(jnp.bfloat16)


def per_device(
    profiles,
    radiances,
    inner_weight,
    inner_bias,
    outer_weight,
    outer_bias,
    channel_weight,
    counts,
    owner,
    column,
):
    tiles = lax.axis_size("tile")
    rows, width = profiles.shape
    hid = inner_weight.shape[1]
    chan = radiances.shape[1]
    most = max(2, 2 * rows // tiles)
    inner = tiles // OUTER
    pool = OUTER * most
    high = width // LANES * pool + LABEL_ROWS
    me = lax.axis_index("tile").astype(jnp.int32).reshape(1)
    vmem = pl.BlockSpec(memory_space=pltpu.VMEM)
    smem = pl.BlockSpec(memory_space=pltpu.SMEM)
    anywhere = pl.BlockSpec(memory_space=pl.ANY)
    bucket = pl.pallas_call(
        functools.partial(rows_kernel, tiles, most),
        out_shape=jax.ShapeDtypeStruct((inner, high, LANES), jnp.bfloat16),
        in_specs=[smem, smem, vmem, vmem] + [anywhere] * 7,
        out_specs=anywhere,
        scratch_shapes=[
            pltpu.VMEM((rows, width), jnp.bfloat16),
            pltpu.VMEM((rows, chan), jnp.bfloat16),
            pltpu.VMEM((width, hid), jnp.bfloat16),
            pltpu.VMEM((1, hid), jnp.float32),
            pltpu.VMEM((hid, chan), jnp.bfloat16),
            pltpu.VMEM((1, chan), jnp.float32),
            pltpu.VMEM((1, chan), jnp.float32),
            pltpu.VMEM((rows, hid), jnp.bfloat16),
            pltpu.VMEM((rows, hid), jnp.float32),
            pltpu.VMEM((inner, high, LANES), jnp.bfloat16),
            pltpu.SemaphoreType.DMA((8,)),
            pltpu.SemaphoreType.DMA((inner * pool // ROWS,)),
        ],
        compiler_params=pltpu.CompilerParams(vmem_limit_bytes=60 * 1024 * 1024),
        name="rows_kernel",
    )(
        me,
        counts,
        owner.reshape(1, rows),
        column.reshape(1, rows),
        profiles,
        radiances,
        inner_weight,
        inner_bias.reshape(1, hid),
        outer_weight,
        outer_bias.reshape(1, chan),
        channel_weight.reshape(1, chan),
    )
    halves = [[o * inner + i for i in range(inner)] for o in range(OUTER)]
    got = lax.all_to_all(
        bucket, "tile", split_axis=0, concat_axis=0, axis_index_groups=halves, tiled=True
    )
    own, other = pl.pallas_call(
        functools.partial(blocks_kernel, tiles, most),
        out_shape=[
            jax.ShapeDtypeStruct((COL_DEV, width), jnp.float32),
            jax.ShapeDtypeStruct((COL_DEV, width), jnp.bfloat16),
        ],
        in_specs=[smem, vmem],
        out_specs=[vmem, vmem],
        compiler_params=pltpu.CompilerParams(vmem_limit_bytes=24 * 1024 * 1024),
        name="blocks_kernel",
    )(me, got)
    pairs = [(t, (t + inner) % tiles) for t in range(tiles)]
    return own + lax.ppermute(other, "tile", pairs).astype(jnp.float32)


def solution(mesh):
    placed = (
        P(("group", "tile"), None),
        P(("group", "tile"), None),
        P(),
        P(),
        P(),
        P(),
        P(),
        P(("group", "tile")),
        P(("group", "tile"), None),
        P(("group", "tile")),
    )
    return jax.shard_map(
        per_device,
        mesh=mesh,
        in_specs=placed,
        out_specs=P(("group", "tile"), None),
        check_vma=False,
    )
```

```python
import functools

import jax
import jax.numpy as jnp
from jax import lax
from jax.experimental import pallas as pl
from jax.experimental.pallas import tpu as pltpu
from jax.sharding import PartitionSpec as P

COL_DEV = 128
CHUNK = 256
LANES = 128
LABEL_ROWS = 8
OUTER = 2
ROWS = 256
NT = (((1,), (1,)), ((), ()))


def as_bf16(mask):
    return mask.astype(jnp.float32).astype(jnp.bfloat16)


def rows_kernel(
    tiles,
    most,
    me_ref,
    count_ref,
    owner_ref,
    column_ref,
    prof_hbm,
    rad_hbm,
    w1_hbm,
    b1_hbm,
    w2_hbm,
    b2_hbm,
    cw_hbm,
    out_hbm,
    prof_ref,
    half_ref,
    rad_ref,
    w1_ref,
    b1_ref,
    w2_ref,
    b2_ref,
    cw_ref,
    hidden_ref,
    factor_ref,
    out_ref,
    sems,
    out_sems,
):
    rows, width = prof_ref.shape
    hid = w1_ref.shape[1]
    chan = rad_ref.shape[1]
    starts = [0, hid // 2, hid]
    pieces = [pl.ds(lo, hi - lo) for lo, hi in zip(starts[:-1], starts[1:])]
    pairs = (
        [(prof_hbm, prof_ref), (b1_hbm, b1_ref)]
        + [(w1_hbm.at[:, piece], w1_ref.at[:, piece]) for piece in pieces]
        + [(w2_hbm, w2_ref), (rad_hbm, rad_ref), (b2_hbm, b2_ref), (cw_hbm, cw_ref)]
    )
    copies = [
        pltpu.make_async_copy(src, dst, sems.at[i]) for i, (src, dst) in enumerate(pairs)
    ]
    for copy in copies:
        copy.start()

    inner = out_ref.shape[0]
    live = lax.broadcasted_iota(jnp.int32, (1, rows), 1) < count_ref[0]
    owner = jnp.where(live, owner_ref[...], -1)
    mine = lax.broadcasted_iota(jnp.int32, (tiles, rows), 0) == owner
    one_hot = mine.astype(jnp.float32)
    upper = as_bf16(
        lax.broadcasted_iota(jnp.int32, (rows, rows), 0)
        <= lax.broadcasted_iota(jnp.int32, (rows, rows), 1)
    )
    running = jnp.dot(one_hot.astype(jnp.bfloat16), upper, preferred_element_type=jnp.float32)
    rank = jnp.sum(running * one_hot, axis=0, keepdims=True).astype(jnp.int32) - 1
    pool = tiles // inner * most
    place = owner & (inner - 1)
    order = lax.shift_right_arithmetic(owner, inner.bit_length() - 1) * most + rank
    slot = jnp.where(live, place * pool + order, -1)
    placing = as_bf16(lax.broadcasted_iota(jnp.int32, (inner * pool, rows), 0) == slot)
    lane = order + lax.rem(me_ref[0], LANES // pool) * pool
    lane_hot = as_bf16(lax.broadcasted_iota(jnp.int32, (LANES, rows), 0) == lane)
    here = live & (lax.broadcasted_iota(jnp.int32, (inner, rows), 0) == place)
    marked = jnp.where(here, (column_ref[...] + 1).astype(jnp.float32), 0.0)
    labels = lax.dot_general(
        marked.astype(jnp.bfloat16), lane_hot, NT, preferred_element_type=jnp.float32
    )

    parts = width // LANES
    out_ref[:, parts * pool :, :] = jnp.broadcast_to(
        labels.reshape(inner, 1, LANES), (inner, LABEL_ROWS, LANES)
    ).astype(jnp.bfloat16)

    copies[0].wait()
    copies[1].wait()
    half_ref[...] = (prof_ref[...].astype(jnp.float32) * 0.5).astype(jnp.bfloat16)
    count = hid // CHUNK

    def rows_of(m):
        return pl.ds(m * ROWS, ROWS)

    def enter(m, first, last):
        for i in range(first, last):
            part = pl.ds(i * CHUNK, CHUNK)
            u = jnp.dot(
                half_ref[rows_of(m), :], w1_ref[:, part], preferred_element_type=jnp.float32
            )
            u = u + 0.5 * b1_ref[:, part]
            p = jnp.tanh(u) + 1.0
            hidden = u * p
            hidden_ref[rows_of(m), part] = hidden.astype(jnp.bfloat16)
            factor_ref[rows_of(m), part] = p + hidden * (2.0 - p)

    def leave(m, n):
        part = pl.ds(n * CHUNK, CHUNK)
        output = jnp.dot(
            hidden_ref[rows_of(m), :], w2_ref[:, part], preferred_element_type=jnp.float32
        )
        misfit = output + b2_ref[:, part] - rad_ref[rows_of(m), part].astype(jnp.float32)
        misfit = (0.5 * cw_ref[:, part]) * misfit
        alive = lax.broadcasted_iota(jnp.int32, (ROWS, 1), 0) + m * ROWS < count_ref[0]
        rad_ref[rows_of(m), part] = jnp.where(alive, misfit, 0.0).astype(jnp.bfloat16)

    def enter_back(m, first, last):
        for i in range(first, last):
            part = pl.ds(i * CHUNK, CHUNK)
            back = lax.dot_general(
                rad_ref[rows_of(m), :], w2_ref[part, :], NT, preferred_element_type=jnp.float32
            )
            back = back * factor_ref[rows_of(m), part]
            hidden_ref[rows_of(m), part] = back.astype(jnp.bfloat16)

    def leave_back(m):
        grads = lax.dot_general(
            hidden_ref[rows_of(m), :], w1_ref[...], NT, preferred_element_type=jnp.float32
        )
        prof_ref[rows_of(m), :] = grads.astype(jnp.bfloat16)

    copies[2].wait()
    enter(0, 0, count // 2)
    copies[3].wait()
    enter(0, count // 2, count)
    enter(1, 0, count // 4)
    for copy in copies[2 + len(pieces) :]:
        copy.wait()
    leave(0, 0)
    enter(1, count // 4, count // 2)
    leave(0, 1)
    enter(1, count // 2, count)
    leave(1, 0)
    enter_back(0, 0, count // 2)
    leave(1, 1)
    enter_back(0, count // 2, count)
    leave_back(0)
    enter_back(1, 0, count)
    leave_back(1)
    grads = prof_ref[...]
    wide = ROWS // pool
    sent = []
    for n in range(inner // wide):
        placed = jnp.dot(
            placing[n * ROWS : (n + 1) * ROWS], grads, preferred_element_type=jnp.float32
        ).astype(jnp.bfloat16)
        some = pl.ds(n * wide, wide)
        for k in range(parts):
            out_ref[some, k * pool : (k + 1) * pool, :] = placed[
                :, k * LANES : (k + 1) * LANES
            ].reshape(wide, pool, LANES)
        sent.append(pltpu.make_async_copy(out_ref.at[some], out_hbm.at[some], out_sems.at[n]))
        sent[-1].start()
    for copy in sent:
        copy.wait()


def blocks_kernel(tiles, most, me_ref, got_ref, own_ref, other_ref):
    inner = got_ref.shape[0]
    outer = tiles // inner
    pool = outer * most
    group = LANES // pool
    parts = own_ref.shape[1] // LANES
    marks = got_ref[:, parts * pool :, :].astype(jnp.float32)[:, 0, :]
    index = lax.broadcasted_iota(jnp.int32, (outer * COL_DEV, LANES), 0)
    lane = lax.broadcasted_iota(jnp.int32, (1, LANES), 1) & (pool - 1)
    turn = lax.shift_right_arithmetic(lane, most.bit_length() - 1) ^ (
        lax.shift_right_arithmetic(me_ref[0], inner.bit_length() - 1)
    )
    chosen = []
    for g in range(inner // group):
        label = jnp.sum(marks[g * group : (g + 1) * group], axis=0, keepdims=True)
        label = label.astype(jnp.int32)
        code = jnp.where(label > 0, turn * COL_DEV + label - 1, -1)
        chosen.append(as_bf16(index == code))
    chosen = jnp.concatenate(chosen, axis=1)
    for k in range(parts):
        block = got_ref[:, k * pool : (k + 1) * pool, :].reshape(inner * pool, LANES)
        total = jnp.dot(chosen, block, preferred_element_type=jnp.float32)
        own_ref[:, k * LANES : (k + 1) * LANES] = total[:COL_DEV]
        other_ref[:, k * LANES : (k + 1) * LANES] = total[COL_DEV:].astype(jnp.bfloat16)


def per_device(
    profiles,
    radiances,
    inner_weight,
    inner_bias,
    outer_weight,
    outer_bias,
    channel_weight,
    counts,
    owner,
    column,
):
    tiles = lax.axis_size("tile")
    rows, width = profiles.shape
    hid = inner_weight.shape[1]
    chan = radiances.shape[1]
    most = max(2, 2 * rows // tiles)
    inner = tiles // OUTER
    pool = OUTER * most
    high = width // LANES * pool + LABEL_ROWS
    me = lax.axis_index("tile").astype(jnp.int32).reshape(1)
    vmem = pl.BlockSpec(memory_space=pltpu.VMEM)
    smem = pl.BlockSpec(memory_space=pltpu.SMEM)
    anywhere = pl.BlockSpec(memory_space=pl.ANY)
    bucket = pl.pallas_call(
        functools.partial(rows_kernel, tiles, most),
        out_shape=jax.ShapeDtypeStruct((inner, high, LANES), jnp.bfloat16),
        in_specs=[smem, smem, vmem, vmem] + [anywhere] * 7,
        out_specs=anywhere,
        scratch_shapes=[
            pltpu.VMEM((rows, width), jnp.bfloat16),
            pltpu.VMEM((rows, width), jnp.bfloat16),
            pltpu.VMEM((rows, chan), jnp.bfloat16),
            pltpu.VMEM((width, hid), jnp.bfloat16),
            pltpu.VMEM((1, hid), jnp.float32),
            pltpu.VMEM((hid, chan), jnp.bfloat16),
            pltpu.VMEM((1, chan), jnp.float32),
            pltpu.VMEM((1, chan), jnp.float32),
            pltpu.VMEM((rows, hid), jnp.bfloat16),
            pltpu.VMEM((rows, hid), jnp.float32),
            pltpu.VMEM((inner, high, LANES), jnp.bfloat16),
            pltpu.SemaphoreType.DMA((8,)),
            pltpu.SemaphoreType.DMA((inner * pool // ROWS,)),
        ],
        compiler_params=pltpu.CompilerParams(vmem_limit_bytes=60 * 1024 * 1024),
        name="rows_kernel",
    )(
        me,
        counts,
        owner.reshape(1, rows),
        column.reshape(1, rows),
        profiles,
        radiances,
        inner_weight,
        inner_bias.reshape(1, hid),
        outer_weight,
        outer_bias.reshape(1, chan),
        channel_weight.reshape(1, chan),
    )
    halves = [[o * inner + i for i in range(inner)] for o in range(OUTER)]
    got = lax.all_to_all(
        bucket, "tile", split_axis=0, concat_axis=0, axis_index_groups=halves, tiled=True
    )
    own, other = pl.pallas_call(
        functools.partial(blocks_kernel, tiles, most),
        out_shape=[
            jax.ShapeDtypeStruct((COL_DEV, width), jnp.float32),
            jax.ShapeDtypeStruct((COL_DEV, width), jnp.bfloat16),
        ],
        in_specs=[smem, vmem],
        out_specs=[vmem, vmem],
        compiler_params=pltpu.CompilerParams(vmem_limit_bytes=24 * 1024 * 1024),
        name="blocks_kernel",
    )(me, got)
    pairs = [(t, (t + inner) % tiles) for t in range(tiles)]
    return own + lax.ppermute(other, "tile", pairs).astype(jnp.float32)


def solution(mesh):
    placed = (
        P(("group", "tile"), None),
        P(("group", "tile"), None),
        P(),
        P(),
        P(),
        P(),
        P(),
        P(("group", "tile")),
        P(("group", "tile"), None),
        P(("group", "tile")),
    )
    return jax.shard_map(
        per_device,
        mesh=mesh,
        in_specs=placed,
        out_specs=P(("group", "tile"), None),
        check_vma=False,
    )
```

```python
import functools

import jax
import jax.numpy as jnp
from jax import lax
from jax.experimental import pallas as pl
from jax.experimental.pallas import tpu as pltpu
from jax.sharding import PartitionSpec as P

COL_DEV = 128
CHUNK = 256
LANES = 128
LABEL_ROWS = 8
OUTER = 2
ROWS = 256
NT = (((1,), (1,)), ((), ()))


def as_bf16(mask):
    return mask.astype(jnp.float32).astype(jnp.bfloat16)


def rows_kernel(
    tiles,
    most,
    me_ref,
    count_ref,
    owner_ref,
    column_ref,
    prof_hbm,
    rad_hbm,
    w1_hbm,
    b1_hbm,
    w2_hbm,
    b2_hbm,
    cw_hbm,
    out_hbm,
    prof_ref,
    rad_ref,
    w1_ref,
    b1_ref,
    w2_ref,
    b2_ref,
    cw_ref,
    hidden_ref,
    factor_ref,
    out_ref,
    sems,
    out_sems,
):
    rows, width = prof_ref.shape
    hid = w1_ref.shape[1]
    chan = rad_ref.shape[1]
    starts = [0, hid // 4, hid]
    pieces = [pl.ds(lo, hi - lo) for lo, hi in zip(starts[:-1], starts[1:])]
    pairs = (
        [(prof_hbm, prof_ref), (b1_hbm, b1_ref)]
        + [(w1_hbm.at[:, piece], w1_ref.at[:, piece]) for piece in pieces]
        + [(w2_hbm, w2_ref), (rad_hbm, rad_ref), (b2_hbm, b2_ref), (cw_hbm, cw_ref)]
    )
    copies = [
        pltpu.make_async_copy(src, dst, sems.at[i]) for i, (src, dst) in enumerate(pairs)
    ]
    for copy in copies:
        copy.start()

    inner = out_ref.shape[0]
    live = lax.broadcasted_iota(jnp.int32, (1, rows), 1) < count_ref[0]
    owner = jnp.where(live, owner_ref[...], -1)
    mine = lax.broadcasted_iota(jnp.int32, (tiles, rows), 0) == owner
    one_hot = mine.astype(jnp.float32)
    upper = as_bf16(
        lax.broadcasted_iota(jnp.int32, (rows, rows), 0)
        <= lax.broadcasted_iota(jnp.int32, (rows, rows), 1)
    )
    running = jnp.dot(one_hot.astype(jnp.bfloat16), upper, preferred_element_type=jnp.float32)
    rank = jnp.sum(running * one_hot, axis=0, keepdims=True).astype(jnp.int32) - 1
    pool = tiles // inner * most
    place = owner & (inner - 1)
    order = lax.shift_right_arithmetic(owner, inner.bit_length() - 1) * most + rank
    slot = jnp.where(live, place * pool + order, -1)
    placing = as_bf16(lax.broadcasted_iota(jnp.int32, (inner * pool, rows), 0) == slot)
    lane = order + lax.rem(me_ref[0], LANES // pool) * pool
    lane_hot = as_bf16(lax.broadcasted_iota(jnp.int32, (LANES, rows), 0) == lane)
    here = live & (lax.broadcasted_iota(jnp.int32, (inner, rows), 0) == place)
    marked = jnp.where(here, (column_ref[...] + 1).astype(jnp.float32), 0.0)
    labels = lax.dot_general(
        marked.astype(jnp.bfloat16), lane_hot, NT, preferred_element_type=jnp.float32
    )

    parts = width // LANES
    out_ref[:, parts * pool :, :] = jnp.broadcast_to(
        labels.reshape(inner, 1, LANES), (inner, LABEL_ROWS, LANES)
    ).astype(jnp.bfloat16)

    copies[0].wait()
    copies[1].wait()
    prof_ref[...] = (prof_ref[...].astype(jnp.float32) * 0.5).astype(jnp.bfloat16)
    blocks = [pl.ds(i, ROWS) for i in range(0, rows, ROWS)]
    small = [pl.ds(i, ROWS // 2) for i in range(0, rows, ROWS // 2)]
    for i in range(hid // CHUNK):
        part = pl.ds(i * CHUNK, CHUNK)
        if i * CHUNK in starts:
            copies[2 + starts.index(i * CHUNK)].wait()
        for m in small:
            u = jnp.dot(prof_ref[m, :], w1_ref[:, part], preferred_element_type=jnp.float32)
            u = u + 0.5 * b1_ref[:, part]
            p = jnp.tanh(u) + 1.0
            hidden = u * p
            hidden_ref[m, part] = hidden.astype(jnp.bfloat16)
            factor_ref[m, part] = p + hidden * (2.0 - p)
    for copy in copies[2 + len(pieces) :]:
        copy.wait()
    scale = 0.5 * cw_ref[...]
    for n, m in enumerate(blocks):
        output = jnp.dot(hidden_ref[m, :], w2_ref[...], preferred_element_type=jnp.float32)
        misfit = scale * (output + b2_ref[...] - rad_ref[m, :].astype(jnp.float32))
        alive = lax.broadcasted_iota(jnp.int32, (ROWS, 1), 0) + n * ROWS < count_ref[0]
        rad_ref[m, :] = jnp.where(alive, misfit, 0.0).astype(jnp.bfloat16)
    for i in range(hid // CHUNK):
        part = pl.ds(i * CHUNK, CHUNK)
        for m in small:
            back = lax.dot_general(
                rad_ref[m, :], w2_ref[part, :], NT, preferred_element_type=jnp.float32
            )
            hidden_ref[m, part] = (back * factor_ref[m, part]).astype(jnp.bfloat16)
    for m in blocks:
        grads = lax.dot_general(
            hidden_ref[m, :], w1_ref[...], NT, preferred_element_type=jnp.float32
        )
        prof_ref[m, :] = grads.astype(jnp.bfloat16)
    grads = prof_ref[...]
    wide = ROWS // pool
    sent = []
    for n in range(inner // wide):
        placed = jnp.dot(
            placing[n * ROWS : (n + 1) * ROWS], grads, preferred_element_type=jnp.float32
        ).astype(jnp.bfloat16)
        some = pl.ds(n * wide, wide)
        for k in range(parts):
            out_ref[some, k * pool : (k + 1) * pool, :] = placed[
                :, k * LANES : (k + 1) * LANES
            ].reshape(wide, pool, LANES)
        sent.append(pltpu.make_async_copy(out_ref.at[some], out_hbm.at[some], out_sems.at[n]))
        sent[-1].start()
    for copy in sent:
        copy.wait()


def blocks_kernel(tiles, most, me_ref, got_ref, own_ref, other_ref):
    inner = got_ref.shape[0]
    outer = tiles // inner
    pool = outer * most
    group = LANES // pool
    parts = own_ref.shape[1] // LANES
    marks = got_ref[:, parts * pool :, :].astype(jnp.float32)[:, 0, :]
    index = lax.broadcasted_iota(jnp.int32, (outer * COL_DEV, LANES), 0)
    lane = lax.broadcasted_iota(jnp.int32, (1, LANES), 1) & (pool - 1)
    turn = lax.shift_right_arithmetic(lane, most.bit_length() - 1) ^ (
        lax.shift_right_arithmetic(me_ref[0], inner.bit_length() - 1)
    )
    chosen = []
    for g in range(inner // group):
        label = jnp.sum(marks[g * group : (g + 1) * group], axis=0, keepdims=True)
        label = label.astype(jnp.int32)
        code = jnp.where(label > 0, turn * COL_DEV + label - 1, -1)
        chosen.append(as_bf16(index == code))
    chosen = jnp.concatenate(chosen, axis=1)
    for k in range(parts):
        block = got_ref[:, k * pool : (k + 1) * pool, :].reshape(inner * pool, LANES)
        total = jnp.dot(chosen, block, preferred_element_type=jnp.float32)
        own_ref[:, k * LANES : (k + 1) * LANES] = total[:COL_DEV]
        other_ref[:, k * LANES : (k + 1) * LANES] = total[COL_DEV:].astype(jnp.bfloat16)


def per_device(
    profiles,
    radiances,
    inner_weight,
    inner_bias,
    outer_weight,
    outer_bias,
    channel_weight,
    counts,
    owner,
    column,
):
    tiles = lax.axis_size("tile")
    rows, width = profiles.shape
    hid = inner_weight.shape[1]
    chan = radiances.shape[1]
    most = max(2, 2 * rows // tiles)
    inner = tiles // OUTER
    pool = OUTER * most
    high = width // LANES * pool + LABEL_ROWS
    me = lax.axis_index("tile").astype(jnp.int32).reshape(1)
    vmem = pl.BlockSpec(memory_space=pltpu.VMEM)
    smem = pl.BlockSpec(memory_space=pltpu.SMEM)
    anywhere = pl.BlockSpec(memory_space=pl.ANY)
    bucket = pl.pallas_call(
        functools.partial(rows_kernel, tiles, most),
        out_shape=jax.ShapeDtypeStruct((inner, high, LANES), jnp.bfloat16),
        in_specs=[smem, smem, vmem, vmem] + [anywhere] * 7,
        out_specs=anywhere,
        scratch_shapes=[
            pltpu.VMEM((rows, width), jnp.bfloat16),
            pltpu.VMEM((rows, chan), jnp.bfloat16),
            pltpu.VMEM((width, hid), jnp.bfloat16),
            pltpu.VMEM((1, hid), jnp.float32),
            pltpu.VMEM((hid, chan), jnp.bfloat16),
            pltpu.VMEM((1, chan), jnp.float32),
            pltpu.VMEM((1, chan), jnp.float32),
            pltpu.VMEM((rows, hid), jnp.bfloat16),
            pltpu.VMEM((rows, hid), jnp.float32),
            pltpu.VMEM((inner, high, LANES), jnp.bfloat16),
            pltpu.SemaphoreType.DMA((8,)),
            pltpu.SemaphoreType.DMA((inner * pool // ROWS,)),
        ],
        compiler_params=pltpu.CompilerParams(vmem_limit_bytes=60 * 1024 * 1024),
        name="rows_kernel",
    )(
        me,
        counts,
        owner.reshape(1, rows),
        column.reshape(1, rows),
        profiles,
        radiances,
        inner_weight,
        inner_bias.reshape(1, hid),
        outer_weight,
        outer_bias.reshape(1, chan),
        channel_weight.reshape(1, chan),
    )
    halves = [[o * inner + i for i in range(inner)] for o in range(OUTER)]
    got = lax.all_to_all(
        bucket, "tile", split_axis=0, concat_axis=0, axis_index_groups=halves, tiled=True
    )
    own, other = pl.pallas_call(
        functools.partial(blocks_kernel, tiles, most),
        out_shape=[
            jax.ShapeDtypeStruct((COL_DEV, width), jnp.float32),
            jax.ShapeDtypeStruct((COL_DEV, width), jnp.bfloat16),
        ],
        in_specs=[smem, vmem],
        out_specs=[vmem, vmem],
        compiler_params=pltpu.CompilerParams(vmem_limit_bytes=24 * 1024 * 1024),
        name="blocks_kernel",
    )(me, got)
    pairs = [(t, (t + inner) % tiles) for t in range(tiles)]
    return own + lax.ppermute(other, "tile", pairs).astype(jnp.float32)


def solution(mesh):
    placed = (
        P(("group", "tile"), None),
        P(("group", "tile"), None),
        P(),
        P(),
        P(),
        P(),
        P(),
        P(("group", "tile")),
        P(("group", "tile"), None),
        P(("group", "tile")),
    )
    return jax.shard_map(
        per_device,
        mesh=mesh,
        in_specs=placed,
        out_specs=P(("group", "tile"), None),
        check_vma=False,
    )
```

```python
import functools

import jax
import jax.numpy as jnp
from jax import lax
from jax.experimental import pallas as pl
from jax.experimental.pallas import tpu as pltpu
from jax.sharding import PartitionSpec as P

COL_DEV = 128
CHUNK = 256
LANES = 128
LABEL_ROWS = 8
OUTER = 2
ROWS = 256
NT = (((1,), (1,)), ((), ()))


def as_bf16(mask):
    return mask.astype(jnp.float32).astype(jnp.bfloat16)


def rows_kernel(
    tiles,
    most,
    me_ref,
    count_ref,
    owner_ref,
    column_ref,
    prof_hbm,
    rad_hbm,
    w1_hbm,
    b1_hbm,
    w2_hbm,
    b2_hbm,
    cw_hbm,
    out_hbm,
    prof_ref,
    rad_ref,
    w1_ref,
    b1_ref,
    w2_ref,
    b2_ref,
    cw_ref,
    hidden_ref,
    factor_ref,
    out_ref,
    sems,
    out_sems,
):
    rows, width = prof_ref.shape
    hid = w1_ref.shape[1]
    chan = rad_ref.shape[1]
    starts = [0, hid // 4, hid]
    pieces = [pl.ds(lo, hi - lo) for lo, hi in zip(starts[:-1], starts[1:])]
    pairs = (
        [(prof_hbm, prof_ref), (b1_hbm, b1_ref)]
        + [(w1_hbm.at[:, piece], w1_ref.at[:, piece]) for piece in pieces]
        + [(w2_hbm, w2_ref), (rad_hbm, rad_ref), (b2_hbm, b2_ref), (cw_hbm, cw_ref)]
    )
    copies = [
        pltpu.make_async_copy(src, dst, sems.at[i]) for i, (src, dst) in enumerate(pairs)
    ]
    for copy in copies:
        copy.start()

    inner = out_ref.shape[0]
    live = lax.broadcasted_iota(jnp.int32, (1, rows), 1) < count_ref[0]
    owner = jnp.where(live, owner_ref[...], -1)
    mine = lax.broadcasted_iota(jnp.int32, (tiles, rows), 0) == owner
    one_hot = mine.astype(jnp.float32)
    upper = as_bf16(
        lax.broadcasted_iota(jnp.int32, (rows, rows), 0)
        <= lax.broadcasted_iota(jnp.int32, (rows, rows), 1)
    )
    running = jnp.dot(one_hot.astype(jnp.bfloat16), upper, preferred_element_type=jnp.float32)
    rank = jnp.sum(running * one_hot, axis=0, keepdims=True).astype(jnp.int32) - 1
    pool = tiles // inner * most
    place = owner & (inner - 1)
    order = lax.shift_right_arithmetic(owner, inner.bit_length() - 1) * most + rank
    slot = jnp.where(live, place * pool + order, -1)
    placing = as_bf16(lax.broadcasted_iota(jnp.int32, (inner * pool, rows), 0) == slot)
    lane = order + lax.rem(me_ref[0], LANES // pool) * pool
    lane_hot = as_bf16(lax.broadcasted_iota(jnp.int32, (LANES, rows), 0) == lane)
    here = live & (lax.broadcasted_iota(jnp.int32, (inner, rows), 0) == place)
    marked = jnp.where(here, (column_ref[...] + 1).astype(jnp.float32), 0.0)
    labels = lax.dot_general(
        marked.astype(jnp.bfloat16), lane_hot, NT, preferred_element_type=jnp.float32
    )

    parts = width // LANES
    out_ref[:, parts * pool :, :] = jnp.broadcast_to(
        labels.reshape(inner, 1, LANES), (inner, LABEL_ROWS, LANES)
    ).astype(jnp.bfloat16)

    copies[0].wait()
    copies[1].wait()
    prof_ref[...] = (prof_ref[...].astype(jnp.float32) * 0.5).astype(jnp.bfloat16)
    blocks = [pl.ds(i, ROWS) for i in range(0, rows, ROWS)]
    for i in range(hid // CHUNK):
        part = pl.ds(i * CHUNK, CHUNK)
        if i * CHUNK in starts:
            copies[2 + starts.index(i * CHUNK)].wait()
        for m in [pl.ds(0, rows)]:
            u = jnp.dot(prof_ref[m, :], w1_ref[:, part], preferred_element_type=jnp.float32)
            u = u + 0.5 * b1_ref[:, part]
            p = jnp.tanh(u) + 1.0
            hidden = u * p
            hidden_ref[m, part] = hidden.astype(jnp.bfloat16)
            factor_ref[m, part] = p + hidden * (2.0 - p)
    for copy in copies[2 + len(pieces) :]:
        copy.wait()
    scale = 0.5 * cw_ref[...]
    for n, m in enumerate(blocks):
        output = jnp.dot(hidden_ref[m, :], w2_ref[...], preferred_element_type=jnp.float32)
        misfit = scale * (output + b2_ref[...] - rad_ref[m, :].astype(jnp.float32))
        alive = lax.broadcasted_iota(jnp.int32, (ROWS, 1), 0) + n * ROWS < count_ref[0]
        rad_ref[m, :] = jnp.where(alive, misfit, 0.0).astype(jnp.bfloat16)
    for i in range(hid // CHUNK):
        part = pl.ds(i * CHUNK, CHUNK)
        for m in [pl.ds(0, rows)]:
            back = lax.dot_general(
                rad_ref[m, :], w2_ref[part, :], NT, preferred_element_type=jnp.float32
            )
            hidden_ref[m, part] = (back * factor_ref[m, part]).astype(jnp.bfloat16)
    for m in blocks:
        grads = lax.dot_general(
            hidden_ref[m, :], w1_ref[...], NT, preferred_element_type=jnp.float32
        )
        prof_ref[m, :] = grads.astype(jnp.bfloat16)
    grads = prof_ref[...]
    wide = ROWS // pool
    sent = []
    for n in range(inner // wide):
        placed = jnp.dot(
            placing[n * ROWS : (n + 1) * ROWS], grads, preferred_element_type=jnp.float32
        ).astype(jnp.bfloat16)
        some = pl.ds(n * wide, wide)
        for k in range(parts):
            out_ref[some, k * pool : (k + 1) * pool, :] = placed[
                :, k * LANES : (k + 1) * LANES
            ].reshape(wide, pool, LANES)
        sent.append(pltpu.make_async_copy(out_ref.at[some], out_hbm.at[some], out_sems.at[n]))
        sent[-1].start()
    for copy in sent:
        copy.wait()


def blocks_kernel(tiles, most, me_ref, got_ref, own_ref, other_ref):
    inner = got_ref.shape[0]
    outer = tiles // inner
    pool = outer * most
    group = LANES // pool
    parts = own_ref.shape[1] // LANES
    marks = got_ref[:, parts * pool :, :].astype(jnp.float32)[:, 0, :]
    index = lax.broadcasted_iota(jnp.int32, (outer * COL_DEV, LANES), 0)
    lane = lax.broadcasted_iota(jnp.int32, (1, LANES), 1) & (pool - 1)
    turn = lax.shift_right_arithmetic(lane, most.bit_length() - 1) ^ (
        lax.shift_right_arithmetic(me_ref[0], inner.bit_length() - 1)
    )
    chosen = []
    for g in range(inner // group):
        label = jnp.sum(marks[g * group : (g + 1) * group], axis=0, keepdims=True)
        label = label.astype(jnp.int32)
        code = jnp.where(label > 0, turn * COL_DEV + label - 1, -1)
        chosen.append(as_bf16(index == code))
    chosen = jnp.concatenate(chosen, axis=1)
    for k in range(parts):
        block = got_ref[:, k * pool : (k + 1) * pool, :].reshape(inner * pool, LANES)
        total = jnp.dot(chosen, block, preferred_element_type=jnp.float32)
        own_ref[:, k * LANES : (k + 1) * LANES] = total[:COL_DEV]
        other_ref[:, k * LANES : (k + 1) * LANES] = total[COL_DEV:].astype(jnp.bfloat16)


def per_device(
    profiles,
    radiances,
    inner_weight,
    inner_bias,
    outer_weight,
    outer_bias,
    channel_weight,
    counts,
    owner,
    column,
):
    tiles = lax.axis_size("tile")
    rows, width = profiles.shape
    hid = inner_weight.shape[1]
    chan = radiances.shape[1]
    most = max(2, 2 * rows // tiles)
    inner = tiles // OUTER
    pool = OUTER * most
    high = width // LANES * pool + LABEL_ROWS
    me = lax.axis_index("tile").astype(jnp.int32).reshape(1)
    vmem = pl.BlockSpec(memory_space=pltpu.VMEM)
    smem = pl.BlockSpec(memory_space=pltpu.SMEM)
    anywhere = pl.BlockSpec(memory_space=pl.ANY)
    bucket = pl.pallas_call(
        functools.partial(rows_kernel, tiles, most),
        out_shape=jax.ShapeDtypeStruct((inner, high, LANES), jnp.bfloat16),
        in_specs=[smem, smem, vmem, vmem] + [anywhere] * 7,
        out_specs=anywhere,
        scratch_shapes=[
            pltpu.VMEM((rows, width), jnp.bfloat16),
            pltpu.VMEM((rows, chan), jnp.bfloat16),
            pltpu.VMEM((width, hid), jnp.bfloat16),
            pltpu.VMEM((1, hid), jnp.float32),
            pltpu.VMEM((hid, chan), jnp.bfloat16),
            pltpu.VMEM((1, chan), jnp.float32),
            pltpu.VMEM((1, chan), jnp.float32),
            pltpu.VMEM((rows, hid), jnp.bfloat16),
            pltpu.VMEM((rows, hid), jnp.float32),
            pltpu.VMEM((inner, high, LANES), jnp.bfloat16),
            pltpu.SemaphoreType.DMA((8,)),
            pltpu.SemaphoreType.DMA((inner * pool // ROWS,)),
        ],
        compiler_params=pltpu.CompilerParams(vmem_limit_bytes=60 * 1024 * 1024),
        name="rows_kernel",
    )(
        me,
        counts,
        owner.reshape(1, rows),
        column.reshape(1, rows),
        profiles,
        radiances,
        inner_weight,
        inner_bias.reshape(1, hid),
        outer_weight,
        outer_bias.reshape(1, chan),
        channel_weight.reshape(1, chan),
    )
    halves = [[o * inner + i for i in range(inner)] for o in range(OUTER)]
    got = lax.all_to_all(
        bucket, "tile", split_axis=0, concat_axis=0, axis_index_groups=halves, tiled=True
    )
    own, other = pl.pallas_call(
        functools.partial(blocks_kernel, tiles, most),
        out_shape=[
            jax.ShapeDtypeStruct((COL_DEV, width), jnp.float32),
            jax.ShapeDtypeStruct((COL_DEV, width), jnp.bfloat16),
        ],
        in_specs=[smem, vmem],
        out_specs=[vmem, vmem],
        compiler_params=pltpu.CompilerParams(vmem_limit_bytes=24 * 1024 * 1024),
        name="blocks_kernel",
    )(me, got)
    pairs = [(t, (t + inner) % tiles) for t in range(tiles)]
    return own + lax.ppermute(other, "tile", pairs).astype(jnp.float32)


def solution(mesh):
    placed = (
        P(("group", "tile"), None),
        P(("group", "tile"), None),
        P(),
        P(),
        P(),
        P(),
        P(),
        P(("group", "tile")),
        P(("group", "tile"), None),
        P(("group", "tile")),
    )
    return jax.shard_map(
        per_device,
        mesh=mesh,
        in_specs=placed,
        out_specs=P(("group", "tile"), None),
        check_vma=False,
    )
```

```python
import functools

import jax
import jax.numpy as jnp
from jax import lax
from jax.experimental import pallas as pl
from jax.experimental.pallas import tpu as pltpu
from jax.sharding import PartitionSpec as P

COL_DEV = 128
CHUNK = 256
LANES = 128
LABEL_ROWS = 8
OUTER = 2
ROWS = 256
NT = (((1,), (1,)), ((), ()))


def as_bf16(mask):
    return mask.astype(jnp.float32).astype(jnp.bfloat16)


def rows_kernel(
    tiles,
    most,
    me_ref,
    count_ref,
    owner_ref,
    column_ref,
    prof_hbm,
    rad_hbm,
    w1_hbm,
    b1_hbm,
    w2_hbm,
    b2_hbm,
    cw_hbm,
    out_hbm,
    prof_ref,
    rad_ref,
    w1_ref,
    b1_ref,
    w2_ref,
    b2_ref,
    cw_ref,
    hidden_ref,
    factor_ref,
    out_ref,
    sems,
    out_sems,
):
    rows, width = prof_ref.shape
    hid = w1_ref.shape[1]
    chan = rad_ref.shape[1]
    starts = [0, hid // 4, hid]
    pieces = [pl.ds(lo, hi - lo) for lo, hi in zip(starts[:-1], starts[1:])]
    pairs = (
        [(prof_hbm, prof_ref), (b1_hbm, b1_ref)]
        + [(w1_hbm.at[:, piece], w1_ref.at[:, piece]) for piece in pieces]
        + [(w2_hbm, w2_ref), (rad_hbm, rad_ref), (b2_hbm, b2_ref), (cw_hbm, cw_ref)]
    )
    copies = [
        pltpu.make_async_copy(src, dst, sems.at[i]) for i, (src, dst) in enumerate(pairs)
    ]
    for copy in copies:
        copy.start()

    inner = out_ref.shape[0]
    live = lax.broadcasted_iota(jnp.int32, (1, rows), 1) < count_ref[0]
    owner = jnp.where(live, owner_ref[...], -1)
    mine = lax.broadcasted_iota(jnp.int32, (tiles, rows), 0) == owner
    one_hot = mine.astype(jnp.float32)
    upper = as_bf16(
        lax.broadcasted_iota(jnp.int32, (rows, rows), 0)
        <= lax.broadcasted_iota(jnp.int32, (rows, rows), 1)
    )
    running = jnp.dot(one_hot.astype(jnp.bfloat16), upper, preferred_element_type=jnp.float32)
    rank = jnp.sum(running * one_hot, axis=0, keepdims=True).astype(jnp.int32) - 1
    pool = tiles // inner * most
    place = owner & (inner - 1)
    order = lax.shift_right_arithmetic(owner, inner.bit_length() - 1) * most + rank
    slot = jnp.where(live, place * pool + order, -1)
    placing = as_bf16(lax.broadcasted_iota(jnp.int32, (inner * pool, rows), 0) == slot)
    lane = order + lax.rem(me_ref[0], LANES // pool) * pool
    lane_hot = as_bf16(lax.broadcasted_iota(jnp.int32, (LANES, rows), 0) == lane)
    here = live & (lax.broadcasted_iota(jnp.int32, (inner, rows), 0) == place)
    marked = jnp.where(here, (column_ref[...] + 1).astype(jnp.float32), 0.0)
    labels = lax.dot_general(
        marked.astype(jnp.bfloat16), lane_hot, NT, preferred_element_type=jnp.float32
    )

    parts = width // LANES
    out_ref[:, parts * pool :, :] = jnp.broadcast_to(
        labels.reshape(inner, 1, LANES), (inner, LABEL_ROWS, LANES)
    ).astype(jnp.bfloat16)

    copies[0].wait()
    copies[1].wait()
    prof_ref[...] = (prof_ref[...].astype(jnp.float32) * 0.5).astype(jnp.bfloat16)
    blocks = [pl.ds(i, ROWS) for i in range(0, rows, ROWS)]
    for i in range(hid // CHUNK):
        part = pl.ds(i * CHUNK, CHUNK)
        if i * CHUNK in starts:
            copies[2 + starts.index(i * CHUNK)].wait()
        if i * CHUNK == hid * 5 // 8:
            for copy in copies[2 + len(pieces) :]:
                copy.wait()
        for m in blocks:
            u = jnp.dot(prof_ref[m, :], w1_ref[:, part], preferred_element_type=jnp.float32)
            u = u + 0.5 * b1_ref[:, part]
            p = jnp.tanh(u) + 1.0
            hidden = u * p
            hidden_ref[m, part] = hidden.astype(jnp.bfloat16)
            factor_ref[m, part] = p + hidden * (2.0 - p)
    for n, m in enumerate(blocks):
        alive = lax.broadcasted_iota(jnp.int32, (ROWS, 1), 0) + n * ROWS < count_ref[0]
        for lo in range(0, chan, CHUNK):
            part = pl.ds(lo, CHUNK)
            output = jnp.dot(
                hidden_ref[m, :], w2_ref[:, part], preferred_element_type=jnp.float32
            )
            misfit = output + b2_ref[:, part] - rad_ref[m, part].astype(jnp.float32)
            misfit = (0.5 * cw_ref[:, part]) * misfit
            rad_ref[m, part] = jnp.where(alive, misfit, 0.0).astype(jnp.bfloat16)
    for i in range(hid // CHUNK):
        part = pl.ds(i * CHUNK, CHUNK)
        for m in blocks:
            back = lax.dot_general(
                rad_ref[m, :], w2_ref[part, :], NT, preferred_element_type=jnp.float32
            )
            hidden_ref[m, part] = (back * factor_ref[m, part]).astype(jnp.bfloat16)
    for m in blocks:
        for lo in range(0, width, CHUNK):
            part = pl.ds(lo, min(CHUNK, width - lo))
            grads = lax.dot_general(
                hidden_ref[m, :], w1_ref[part, :], NT, preferred_element_type=jnp.float32
            )
            prof_ref[m, part] = grads.astype(jnp.bfloat16)
    grads = prof_ref[...]
    wide = ROWS // pool
    sent = []
    for n in range(inner // wide):
        placed = jnp.dot(
            placing[n * ROWS : (n + 1) * ROWS], grads, preferred_element_type=jnp.float32
        ).astype(jnp.bfloat16)
        some = pl.ds(n * wide, wide)
        for k in range(parts):
            out_ref[some, k * pool : (k + 1) * pool, :] = placed[
                :, k * LANES : (k + 1) * LANES
            ].reshape(wide, pool, LANES)
        sent.append(pltpu.make_async_copy(out_ref.at[some], out_hbm.at[some], out_sems.at[n]))
        sent[-1].start()
    for copy in sent:
        copy.wait()


def blocks_kernel(tiles, most, me_ref, got_ref, own_ref, other_ref):
    inner = got_ref.shape[0]
    outer = tiles // inner
    pool = outer * most
    group = LANES // pool
    parts = own_ref.shape[1] // LANES
    marks = got_ref[:, parts * pool :, :].astype(jnp.float32)[:, 0, :]
    index = lax.broadcasted_iota(jnp.int32, (outer * COL_DEV, LANES), 0)
    lane = lax.broadcasted_iota(jnp.int32, (1, LANES), 1) & (pool - 1)
    turn = lax.shift_right_arithmetic(lane, most.bit_length() - 1) ^ (
        lax.shift_right_arithmetic(me_ref[0], inner.bit_length() - 1)
    )
    chosen = []
    for g in range(inner // group):
        label = jnp.sum(marks[g * group : (g + 1) * group], axis=0, keepdims=True)
        label = label.astype(jnp.int32)
        code = jnp.where(label > 0, turn * COL_DEV + label - 1, -1)
        chosen.append(as_bf16(index == code))
    chosen = jnp.concatenate(chosen, axis=1)
    for k in range(parts):
        block = got_ref[:, k * pool : (k + 1) * pool, :].reshape(inner * pool, LANES)
        total = jnp.dot(chosen, block, preferred_element_type=jnp.float32)
        own_ref[:, k * LANES : (k + 1) * LANES] = total[:COL_DEV]
        other_ref[:, k * LANES : (k + 1) * LANES] = total[COL_DEV:].astype(jnp.bfloat16)


def per_device(
    profiles,
    radiances,
    inner_weight,
    inner_bias,
    outer_weight,
    outer_bias,
    channel_weight,
    counts,
    owner,
    column,
):
    tiles = lax.axis_size("tile")
    rows, width = profiles.shape
    hid = inner_weight.shape[1]
    chan = radiances.shape[1]
    most = max(2, 2 * rows // tiles)
    inner = tiles // OUTER
    pool = OUTER * most
    high = width // LANES * pool + LABEL_ROWS
    me = lax.axis_index("tile").astype(jnp.int32).reshape(1)
    vmem = pl.BlockSpec(memory_space=pltpu.VMEM)
    smem = pl.BlockSpec(memory_space=pltpu.SMEM)
    anywhere = pl.BlockSpec(memory_space=pl.ANY)
    bucket = pl.pallas_call(
        functools.partial(rows_kernel, tiles, most),
        out_shape=jax.ShapeDtypeStruct((inner, high, LANES), jnp.bfloat16),
        in_specs=[smem, smem, vmem, vmem] + [anywhere] * 7,
        out_specs=anywhere,
        scratch_shapes=[
            pltpu.VMEM((rows, width), jnp.bfloat16),
            pltpu.VMEM((rows, chan), jnp.bfloat16),
            pltpu.VMEM((width, hid), jnp.bfloat16),
            pltpu.VMEM((1, hid), jnp.float32),
            pltpu.VMEM((hid, chan), jnp.bfloat16),
            pltpu.VMEM((1, chan), jnp.float32),
            pltpu.VMEM((1, chan), jnp.float32),
            pltpu.VMEM((rows, hid), jnp.bfloat16),
            pltpu.VMEM((rows, hid), jnp.float32),
            pltpu.VMEM((inner, high, LANES), jnp.bfloat16),
            pltpu.SemaphoreType.DMA((8,)),
            pltpu.SemaphoreType.DMA((inner * pool // ROWS,)),
        ],
        compiler_params=pltpu.CompilerParams(vmem_limit_bytes=60 * 1024 * 1024),
        name="rows_kernel",
    )(
        me,
        counts,
        owner.reshape(1, rows),
        column.reshape(1, rows),
        profiles,
        radiances,
        inner_weight,
        inner_bias.reshape(1, hid),
        outer_weight,
        outer_bias.reshape(1, chan),
        channel_weight.reshape(1, chan),
    )
    halves = [[o * inner + i for i in range(inner)] for o in range(OUTER)]
    got = lax.all_to_all(
        bucket, "tile", split_axis=0, concat_axis=0, axis_index_groups=halves, tiled=True
    )
    own, other = pl.pallas_call(
        functools.partial(blocks_kernel, tiles, most),
        out_shape=[
            jax.ShapeDtypeStruct((COL_DEV, width), jnp.float32),
            jax.ShapeDtypeStruct((COL_DEV, width), jnp.bfloat16),
        ],
        in_specs=[smem, vmem],
        out_specs=[vmem, vmem],
        compiler_params=pltpu.CompilerParams(vmem_limit_bytes=24 * 1024 * 1024),
        name="blocks_kernel",
    )(me, got)
    pairs = [(t, (t + inner) % tiles) for t in range(tiles)]
    return own + lax.ppermute(other, "tile", pairs).astype(jnp.float32)


def solution(mesh):
    placed = (
        P(("group", "tile"), None),
        P(("group", "tile"), None),
        P(),
        P(),
        P(),
        P(),
        P(),
        P(("group", "tile")),
        P(("group", "tile"), None),
        P(("group", "tile")),
    )
    return jax.shard_map(
        per_device,
        mesh=mesh,
        in_specs=placed,
        out_specs=P(("group", "tile"), None),
        check_vma=False,
    )
```

```python
import functools

import jax
import jax.numpy as jnp
from jax import lax
from jax.experimental import pallas as pl
from jax.experimental.pallas import tpu as pltpu
from jax.sharding import PartitionSpec as P

COL_DEV = 128
CHUNK = 256
LANES = 128
LABEL_ROWS = 8
OUTER = 2
ROWS = 256
NT = (((1,), (1,)), ((), ()))


def as_bf16(mask):
    return mask.astype(jnp.float32).astype(jnp.bfloat16)


def rows_kernel(
    tiles,
    most,
    me_ref,
    count_ref,
    owner_ref,
    column_ref,
    prof_hbm,
    rad_hbm,
    w1_hbm,
    b1_hbm,
    w2_hbm,
    b2_hbm,
    cw_hbm,
    out_hbm,
    prof_ref,
    rad_ref,
    w1_ref,
    b1_ref,
    w2_ref,
    b2_ref,
    cw_ref,
    hidden_ref,
    factor_ref,
    out_ref,
    sems,
    out_sems,
):
    rows, width = prof_ref.shape
    hid = w1_ref.shape[1]
    chan = rad_ref.shape[1]
    starts = [0, hid // 4, hid]
    pieces = [pl.ds(lo, hi - lo) for lo, hi in zip(starts[:-1], starts[1:])]
    pairs = (
        [(prof_hbm, prof_ref), (b1_hbm, b1_ref)]
        + [(w1_hbm.at[:, piece], w1_ref.at[:, piece]) for piece in pieces]
        + [(w2_hbm, w2_ref), (rad_hbm, rad_ref), (b2_hbm, b2_ref), (cw_hbm, cw_ref)]
    )
    copies = [
        pltpu.make_async_copy(src, dst, sems.at[i]) for i, (src, dst) in enumerate(pairs)
    ]
    for copy in copies:
        copy.start()

    inner = out_ref.shape[0]
    live = lax.broadcasted_iota(jnp.int32, (1, rows), 1) < count_ref[0]
    owner = jnp.where(live, owner_ref[...], -1)
    mine = lax.broadcasted_iota(jnp.int32, (tiles, rows), 0) == owner
    one_hot = mine.astype(jnp.float32)
    upper = as_bf16(
        lax.broadcasted_iota(jnp.int32, (rows, rows), 0)
        <= lax.broadcasted_iota(jnp.int32, (rows, rows), 1)
    )
    running = jnp.dot(one_hot.astype(jnp.bfloat16), upper, preferred_element_type=jnp.float32)
    rank = jnp.sum(running * one_hot, axis=0, keepdims=True).astype(jnp.int32) - 1
    pool = tiles // inner * most
    place = owner & (inner - 1)
    order = lax.shift_right_arithmetic(owner, inner.bit_length() - 1) * most + rank
    slot = jnp.where(live, place * pool + order, -1)
    placing = as_bf16(lax.broadcasted_iota(jnp.int32, (inner * pool, rows), 0) == slot)
    lane = order + lax.rem(me_ref[0], LANES // pool) * pool
    lane_hot = as_bf16(lax.broadcasted_iota(jnp.int32, (LANES, rows), 0) == lane)
    here = live & (lax.broadcasted_iota(jnp.int32, (inner, rows), 0) == place)
    marked = jnp.where(here, (column_ref[...] + 1).astype(jnp.float32), 0.0)
    labels = lax.dot_general(
        marked.astype(jnp.bfloat16), lane_hot, NT, preferred_element_type=jnp.float32
    )

    parts = width // LANES
    out_ref[:, parts * pool :, :] = jnp.broadcast_to(
        labels.reshape(inner, 1, LANES), (inner, LABEL_ROWS, LANES)
    ).astype(jnp.bfloat16)

    copies[0].wait()
    copies[1].wait()
    prof_ref[...] = (prof_ref[...].astype(jnp.float32) * 0.5).astype(jnp.bfloat16)
    blocks = [pl.ds(i, ROWS) for i in range(0, rows, ROWS)]
    for i in range(hid // CHUNK):
        part = pl.ds(i * CHUNK, CHUNK)
        if i * CHUNK in starts:
            copies[2 + starts.index(i * CHUNK)].wait()
        for m in blocks:
            u = jnp.dot(prof_ref[m, :], w1_ref[:, part], preferred_element_type=jnp.float32)
            u = u + 0.5 * b1_ref[:, part]
            p = jnp.tanh(u) + 1.0
            hidden = u * p
            hidden_ref[m, part] = hidden.astype(jnp.bfloat16)
            factor_ref[m, part] = p + hidden * (2.0 - p)
    for copy in copies[2 + len(pieces) :]:
        copy.wait()
    alive = lax.broadcasted_iota(jnp.int32, (rows, 1), 0) < count_ref[0]
    for lo in range(0, chan, CHUNK):
        part = pl.ds(lo, CHUNK)
        output = jnp.dot(hidden_ref[...], w2_ref[:, part], preferred_element_type=jnp.float32)
        misfit = output + b2_ref[:, part] - rad_ref[:, part].astype(jnp.float32)
        misfit = (0.5 * cw_ref[:, part]) * misfit
        rad_ref[:, part] = jnp.where(alive, misfit, 0.0).astype(jnp.bfloat16)
    for i in range(hid // CHUNK):
        part = pl.ds(i * CHUNK, CHUNK)
        for m in blocks:
            back = lax.dot_general(
                rad_ref[m, :], w2_ref[part, :], NT, preferred_element_type=jnp.float32
            )
            hidden_ref[m, part] = (back * factor_ref[m, part]).astype(jnp.bfloat16)
    for lo in range(0, width, CHUNK):
        part = pl.ds(lo, min(CHUNK, width - lo))
        grads = lax.dot_general(
            hidden_ref[...], w1_ref[part, :], NT, preferred_element_type=jnp.float32
        )
        prof_ref[:, part] = grads.astype(jnp.bfloat16)
    grads = prof_ref[...]
    wide = ROWS // pool
    sent = []
    for n in range(inner // wide):
        placed = jnp.dot(
            placing[n * ROWS : (n + 1) * ROWS], grads, preferred_element_type=jnp.float32
        ).astype(jnp.bfloat16)
        some = pl.ds(n * wide, wide)
        for k in range(parts):
            out_ref[some, k * pool : (k + 1) * pool, :] = placed[
                :, k * LANES : (k + 1) * LANES
            ].reshape(wide, pool, LANES)
        sent.append(pltpu.make_async_copy(out_ref.at[some], out_hbm.at[some], out_sems.at[n]))
        sent[-1].start()
    for copy in sent:
        copy.wait()


def blocks_kernel(tiles, most, me_ref, got_ref, own_ref, other_ref):
    inner = got_ref.shape[0]
    outer = tiles // inner
    pool = outer * most
    group = LANES // pool
    parts = own_ref.shape[1] // LANES
    marks = got_ref[:, parts * pool :, :].astype(jnp.float32)[:, 0, :]
    index = lax.broadcasted_iota(jnp.int32, (outer * COL_DEV, LANES), 0)
    lane = lax.broadcasted_iota(jnp.int32, (1, LANES), 1) & (pool - 1)
    turn = lax.shift_right_arithmetic(lane, most.bit_length() - 1) ^ (
        lax.shift_right_arithmetic(me_ref[0], inner.bit_length() - 1)
    )
    chosen = []
    for g in range(inner // group):
        label = jnp.sum(marks[g * group : (g + 1) * group], axis=0, keepdims=True)
        label = label.astype(jnp.int32)
        code = jnp.where(label > 0, turn * COL_DEV + label - 1, -1)
        chosen.append(as_bf16(index == code))
    chosen = jnp.concatenate(chosen, axis=1)
    for k in range(parts):
        block = got_ref[:, k * pool : (k + 1) * pool, :].reshape(inner * pool, LANES)
        total = jnp.dot(chosen, block, preferred_element_type=jnp.float32)
        own_ref[:, k * LANES : (k + 1) * LANES] = total[:COL_DEV]
        other_ref[:, k * LANES : (k + 1) * LANES] = total[COL_DEV:].astype(jnp.bfloat16)


def per_device(
    profiles,
    radiances,
    inner_weight,
    inner_bias,
    outer_weight,
    outer_bias,
    channel_weight,
    counts,
    owner,
    column,
):
    tiles = lax.axis_size("tile")
    rows, width = profiles.shape
    hid = inner_weight.shape[1]
    chan = radiances.shape[1]
    most = max(2, 2 * rows // tiles)
    inner = tiles // OUTER
    pool = OUTER * most
    high = width // LANES * pool + LABEL_ROWS
    me = lax.axis_index("tile").astype(jnp.int32).reshape(1)
    vmem = pl.BlockSpec(memory_space=pltpu.VMEM)
    smem = pl.BlockSpec(memory_space=pltpu.SMEM)
    anywhere = pl.BlockSpec(memory_space=pl.ANY)
    bucket = pl.pallas_call(
        functools.partial(rows_kernel, tiles, most),
        out_shape=jax.ShapeDtypeStruct((inner, high, LANES), jnp.bfloat16),
        in_specs=[smem, smem, vmem, vmem] + [anywhere] * 7,
        out_specs=anywhere,
        scratch_shapes=[
            pltpu.VMEM((rows, width), jnp.bfloat16),
            pltpu.VMEM((rows, chan), jnp.bfloat16),
            pltpu.VMEM((width, hid), jnp.bfloat16),
            pltpu.VMEM((1, hid), jnp.float32),
            pltpu.VMEM((hid, chan), jnp.bfloat16),
            pltpu.VMEM((1, chan), jnp.float32),
            pltpu.VMEM((1, chan), jnp.float32),
            pltpu.VMEM((rows, hid), jnp.bfloat16),
            pltpu.VMEM((rows, hid), jnp.float32),
            pltpu.VMEM((inner, high, LANES), jnp.bfloat16),
            pltpu.SemaphoreType.DMA((8,)),
            pltpu.SemaphoreType.DMA((inner * pool // ROWS,)),
        ],
        compiler_params=pltpu.CompilerParams(vmem_limit_bytes=60 * 1024 * 1024),
        name="rows_kernel",
    )(
        me,
        counts,
        owner.reshape(1, rows),
        column.reshape(1, rows),
        profiles,
        radiances,
        inner_weight,
        inner_bias.reshape(1, hid),
        outer_weight,
        outer_bias.reshape(1, chan),
        channel_weight.reshape(1, chan),
    )
    halves = [[o * inner + i for i in range(inner)] for o in range(OUTER)]
    got = lax.all_to_all(
        bucket, "tile", split_axis=0, concat_axis=0, axis_index_groups=halves, tiled=True
    )
    own, other = pl.pallas_call(
        functools.partial(blocks_kernel, tiles, most),
        out_shape=[
            jax.ShapeDtypeStruct((COL_DEV, width), jnp.float32),
            jax.ShapeDtypeStruct((COL_DEV, width), jnp.bfloat16),
        ],
        in_specs=[smem, vmem],
        out_specs=[vmem, vmem],
        compiler_params=pltpu.CompilerParams(vmem_limit_bytes=24 * 1024 * 1024),
        name="blocks_kernel",
    )(me, got)
    pairs = [(t, (t + inner) % tiles) for t in range(tiles)]
    return own + lax.ppermute(other, "tile", pairs).astype(jnp.float32)


def solution(mesh):
    placed = (
        P(("group", "tile"), None),
        P(("group", "tile"), None),
        P(),
        P(),
        P(),
        P(),
        P(),
        P(("group", "tile")),
        P(("group", "tile"), None),
        P(("group", "tile")),
    )
    return jax.shard_map(
        per_device,
        mesh=mesh,
        in_specs=placed,
        out_specs=P(("group", "tile"), None),
        check_vma=False,
    )
```

```python
import functools

import jax
import jax.numpy as jnp
from jax import lax
from jax.experimental import pallas as pl
from jax.experimental.pallas import tpu as pltpu
from jax.sharding import PartitionSpec as P

COL_DEV = 128
CHUNK = 256
LANES = 128
LABEL_ROWS = 8
OUTER = 2
ROWS = 256
NT = (((1,), (1,)), ((), ()))


def as_bf16(mask):
    return mask.astype(jnp.float32).astype(jnp.bfloat16)


def rows_kernel(
    tiles,
    most,
    me_ref,
    count_hbm,
    owner_hbm,
    column_hbm,
    prof_hbm,
    rad_hbm,
    w1_hbm,
    b1_hbm,
    w2_hbm,
    b2_hbm,
    cw_hbm,
    out_hbm,
    count_ref,
    owner_ref,
    column_ref,
    prof_ref,
    rad_ref,
    w1_ref,
    b1_ref,
    w2_ref,
    b2_ref,
    cw_ref,
    hidden_ref,
    factor_ref,
    out_ref,
    early_sems,
    sems,
    out_sems,
):
    rows, width = prof_ref.shape
    hid = w1_ref.shape[1]
    chan = rad_ref.shape[1]
    starts = [0, hid // 4, hid]
    pieces = [pl.ds(lo, hi - lo) for lo, hi in zip(starts[:-1], starts[1:])]
    pairs = (
        [(prof_hbm, prof_ref), (b1_hbm, b1_ref)]
        + [(w1_hbm.at[:, piece], w1_ref.at[:, piece]) for piece in pieces]
        + [(w2_hbm, w2_ref), (rad_hbm, rad_ref), (b2_hbm, b2_ref), (cw_hbm, cw_ref)]
    )
    copies = [
        pltpu.make_async_copy(src, dst, sems.at[i]) for i, (src, dst) in enumerate(pairs)
    ]
    early = [
        pltpu.make_async_copy(src, dst, early_sems.at[i])
        for i, (src, dst) in enumerate(
            ((owner_hbm, owner_ref), (column_hbm, column_ref), (count_hbm, count_ref))
        )
    ]
    for copy in early + copies:
        copy.start()
    for copy in early:
        copy.wait()

    inner = out_ref.shape[0]
    live = lax.broadcasted_iota(jnp.int32, (1, rows), 1) < count_ref[0]
    owner = jnp.where(live, owner_ref[...], -1)
    mine = lax.broadcasted_iota(jnp.int32, (tiles, rows), 0) == owner
    one_hot = mine.astype(jnp.float32)
    upper = as_bf16(
        lax.broadcasted_iota(jnp.int32, (rows, rows), 0)
        <= lax.broadcasted_iota(jnp.int32, (rows, rows), 1)
    )
    running = jnp.dot(one_hot.astype(jnp.bfloat16), upper, preferred_element_type=jnp.float32)
    rank = jnp.sum(running * one_hot, axis=0, keepdims=True).astype(jnp.int32) - 1
    pool = tiles // inner * most
    place = owner & (inner - 1)
    order = lax.shift_right_arithmetic(owner, inner.bit_length() - 1) * most + rank
    slot = jnp.where(live, place * pool + order, -1)
    placing = as_bf16(lax.broadcasted_iota(jnp.int32, (inner * pool, rows), 0) == slot)
    lane = order + lax.rem(me_ref[0], LANES // pool) * pool
    lane_hot = as_bf16(lax.broadcasted_iota(jnp.int32, (LANES, rows), 0) == lane)
    here = live & (lax.broadcasted_iota(jnp.int32, (inner, rows), 0) == place)
    marked = jnp.where(here, (column_ref[...] + 1).astype(jnp.float32), 0.0)
    labels = lax.dot_general(
        marked.astype(jnp.bfloat16), lane_hot, NT, preferred_element_type=jnp.float32
    )

    parts = width // LANES
    out_ref[:, parts * pool :, :] = jnp.broadcast_to(
        labels.reshape(inner, 1, LANES), (inner, LABEL_ROWS, LANES)
    ).astype(jnp.bfloat16)

    copies[0].wait()
    copies[1].wait()
    prof_ref[...] = (prof_ref[...].astype(jnp.float32) * 0.5).astype(jnp.bfloat16)
    blocks = [pl.ds(i, ROWS) for i in range(0, rows, ROWS)]
    for i in range(hid // CHUNK):
        part = pl.ds(i * CHUNK, CHUNK)
        if i * CHUNK in starts:
            copies[2 + starts.index(i * CHUNK)].wait()
        for m in blocks:
            u = jnp.dot(prof_ref[m, :], w1_ref[:, part], preferred_element_type=jnp.float32)
            u = u + 0.5 * b1_ref[:, part]
            p = jnp.tanh(u) + 1.0
            hidden = u * p
            hidden_ref[m, part] = hidden.astype(jnp.bfloat16)
            factor_ref[m, part] = p + hidden * (2.0 - p)
    for copy in copies[2 + len(pieces) :]:
        copy.wait()
    alive = lax.broadcasted_iota(jnp.int32, (rows, 1), 0) < count_ref[0]
    for lo in range(0, chan, CHUNK):
        part = pl.ds(lo, CHUNK)
        output = jnp.dot(hidden_ref[...], w2_ref[:, part], preferred_element_type=jnp.float32)
        misfit = output + b2_ref[:, part] - rad_ref[:, part].astype(jnp.float32)
        misfit = (0.5 * cw_ref[:, part]) * misfit
        rad_ref[:, part] = jnp.where(alive, misfit, 0.0).astype(jnp.bfloat16)
    for i in range(hid // CHUNK):
        part = pl.ds(i * CHUNK, CHUNK)
        for m in blocks:
            back = lax.dot_general(
                rad_ref[m, :], w2_ref[part, :], NT, preferred_element_type=jnp.float32
            )
            hidden_ref[m, part] = (back * factor_ref[m, part]).astype(jnp.bfloat16)
    for lo in range(0, width, CHUNK):
        part = pl.ds(lo, min(CHUNK, width - lo))
        grads = lax.dot_general(
            hidden_ref[...], w1_ref[part, :], NT, preferred_element_type=jnp.float32
        )
        prof_ref[:, part] = grads.astype(jnp.bfloat16)
    grads = prof_ref[...]
    wide = ROWS // pool
    sent = []
    for n in range(inner // wide):
        placed = jnp.dot(
            placing[n * ROWS : (n + 1) * ROWS], grads, preferred_element_type=jnp.float32
        ).astype(jnp.bfloat16)
        some = pl.ds(n * wide, wide)
        for k in range(parts):
            out_ref[some, k * pool : (k + 1) * pool, :] = placed[
                :, k * LANES : (k + 1) * LANES
            ].reshape(wide, pool, LANES)
        sent.append(pltpu.make_async_copy(out_ref.at[some], out_hbm.at[some], out_sems.at[n]))
        sent[-1].start()
    for copy in sent:
        copy.wait()


def blocks_kernel(tiles, most, me_ref, got_ref, own_ref, other_ref):
    inner = got_ref.shape[0]
    outer = tiles // inner
    pool = outer * most
    group = LANES // pool
    parts = own_ref.shape[1] // LANES
    marks = got_ref[:, parts * pool :, :].astype(jnp.float32)[:, 0, :]
    index = lax.broadcasted_iota(jnp.int32, (outer * COL_DEV, LANES), 0)
    lane = lax.broadcasted_iota(jnp.int32, (1, LANES), 1) & (pool - 1)
    turn = lax.shift_right_arithmetic(lane, most.bit_length() - 1) ^ (
        lax.shift_right_arithmetic(me_ref[0], inner.bit_length() - 1)
    )
    chosen = []
    for g in range(inner // group):
        label = jnp.sum(marks[g * group : (g + 1) * group], axis=0, keepdims=True)
        label = label.astype(jnp.int32)
        code = jnp.where(label > 0, turn * COL_DEV + label - 1, -1)
        chosen.append(as_bf16(index == code))
    chosen = jnp.concatenate(chosen, axis=1)
    for k in range(parts):
        block = got_ref[:, k * pool : (k + 1) * pool, :].reshape(inner * pool, LANES)
        total = jnp.dot(chosen, block, preferred_element_type=jnp.float32)
        own_ref[:, k * LANES : (k + 1) * LANES] = total[:COL_DEV]
        other_ref[:, k * LANES : (k + 1) * LANES] = total[COL_DEV:].astype(jnp.bfloat16)


def per_device(
    profiles,
    radiances,
    inner_weight,
    inner_bias,
    outer_weight,
    outer_bias,
    channel_weight,
    counts,
    owner,
    column,
):
    tiles = lax.axis_size("tile")
    rows, width = profiles.shape
    hid = inner_weight.shape[1]
    chan = radiances.shape[1]
    most = max(2, 2 * rows // tiles)
    inner = tiles // OUTER
    pool = OUTER * most
    high = width // LANES * pool + LABEL_ROWS
    me = lax.axis_index("tile").astype(jnp.int32).reshape(1)
    vmem = pl.BlockSpec(memory_space=pltpu.VMEM)
    smem = pl.BlockSpec(memory_space=pltpu.SMEM)
    anywhere = pl.BlockSpec(memory_space=pl.ANY)
    bucket = pl.pallas_call(
        functools.partial(rows_kernel, tiles, most),
        out_shape=jax.ShapeDtypeStruct((inner, high, LANES), jnp.bfloat16),
        in_specs=[smem] + [anywhere] * 10,
        out_specs=anywhere,
        scratch_shapes=[
            pltpu.SMEM((1,), jnp.int32),
            pltpu.VMEM((1, rows), jnp.int32),
            pltpu.VMEM((1, rows), jnp.int32),
            pltpu.VMEM((rows, width), jnp.bfloat16),
            pltpu.VMEM((rows, chan), jnp.bfloat16),
            pltpu.VMEM((width, hid), jnp.bfloat16),
            pltpu.VMEM((1, hid), jnp.float32),
            pltpu.VMEM((hid, chan), jnp.bfloat16),
            pltpu.VMEM((1, chan), jnp.float32),
            pltpu.VMEM((1, chan), jnp.float32),
            pltpu.VMEM((rows, hid), jnp.bfloat16),
            pltpu.VMEM((rows, hid), jnp.float32),
            pltpu.VMEM((inner, high, LANES), jnp.bfloat16),
            pltpu.SemaphoreType.DMA((3,)),
            pltpu.SemaphoreType.DMA((8,)),
            pltpu.SemaphoreType.DMA((inner * pool // ROWS,)),
        ],
        compiler_params=pltpu.CompilerParams(vmem_limit_bytes=60 * 1024 * 1024),
        name="rows_kernel",
    )(
        me,
        counts,
        owner.reshape(1, rows),
        column.reshape(1, rows),
        profiles,
        radiances,
        inner_weight,
        inner_bias.reshape(1, hid),
        outer_weight,
        outer_bias.reshape(1, chan),
        channel_weight.reshape(1, chan),
    )
    halves = [[o * inner + i for i in range(inner)] for o in range(OUTER)]
    got = lax.all_to_all(
        bucket, "tile", split_axis=0, concat_axis=0, axis_index_groups=halves, tiled=True
    )
    own, other = pl.pallas_call(
        functools.partial(blocks_kernel, tiles, most),
        out_shape=[
            jax.ShapeDtypeStruct((COL_DEV, width), jnp.float32),
            jax.ShapeDtypeStruct((COL_DEV, width), jnp.bfloat16),
        ],
        in_specs=[smem, vmem],
        out_specs=[vmem, vmem],
        compiler_params=pltpu.CompilerParams(vmem_limit_bytes=24 * 1024 * 1024),
        name="blocks_kernel",
    )(me, got)
    pairs = [(t, (t + inner) % tiles) for t in range(tiles)]
    return own + lax.ppermute(other, "tile", pairs).astype(jnp.float32)


def solution(mesh):
    placed = (
        P(("group", "tile"), None),
        P(("group", "tile"), None),
        P(),
        P(),
        P(),
        P(),
        P(),
        P(("group", "tile")),
        P(("group", "tile"), None),
        P(("group", "tile")),
    )
    return jax.shard_map(
        per_device,
        mesh=mesh,
        in_specs=placed,
        out_specs=P(("group", "tile"), None),
        check_vma=False,
    )
```

```python
import functools

import jax
import jax.numpy as jnp
from jax import lax
from jax.experimental import pallas as pl
from jax.experimental.pallas import tpu as pltpu
from jax.sharding import PartitionSpec as P

COL_DEV = 128
CHUNK = 256
LANES = 128
LABEL_ROWS = 8
OUTER = 2
ROWS = 256
NT = (((1,), (1,)), ((), ()))


def as_bf16(mask):
    return mask.astype(jnp.float32).astype(jnp.bfloat16)


def rows_kernel(
    tiles,
    most,
    me_ref,
    count_ref,
    owner_ref,
    column_ref,
    prof_hbm,
    rad_hbm,
    w1_hbm,
    b1_hbm,
    w2_hbm,
    b2_hbm,
    cw_hbm,
    out_hbm,
    prof_ref,
    rad_ref,
    w1_ref,
    b1_ref,
    w2_ref,
    b2_ref,
    cw_ref,
    hidden_ref,
    factor_ref,
    out_ref,
    sems,
    out_sems,
):
    rows, width = prof_ref.shape
    hid = w1_ref.shape[1]
    chan = rad_ref.shape[1]
    starts = [0, hid // 4, hid]
    pieces = [pl.ds(lo, hi - lo) for lo, hi in zip(starts[:-1], starts[1:])]
    pairs = (
        [(prof_hbm, prof_ref), (b1_hbm, b1_ref)]
        + [(w1_hbm.at[:, piece], w1_ref.at[:, piece]) for piece in pieces]
        + [(w2_hbm, w2_ref), (rad_hbm, rad_ref), (b2_hbm, b2_ref), (cw_hbm, cw_ref)]
    )
    copies = [
        pltpu.make_async_copy(src, dst, sems.at[i]) for i, (src, dst) in enumerate(pairs)
    ]
    for copy in copies:
        copy.start()

    inner = out_ref.shape[0]
    live = lax.broadcasted_iota(jnp.int32, (1, rows), 1) < count_ref[...]
    owner = jnp.where(live, owner_ref[...], -1)
    mine = lax.broadcasted_iota(jnp.int32, (tiles, rows), 0) == owner
    one_hot = mine.astype(jnp.float32)
    upper = as_bf16(
        lax.broadcasted_iota(jnp.int32, (rows, rows), 0)
        <= lax.broadcasted_iota(jnp.int32, (rows, rows), 1)
    )
    running = jnp.dot(one_hot.astype(jnp.bfloat16), upper, preferred_element_type=jnp.float32)
    rank = jnp.sum(running * one_hot, axis=0, keepdims=True).astype(jnp.int32) - 1
    pool = tiles // inner * most
    place = owner & (inner - 1)
    order = lax.shift_right_arithmetic(owner, inner.bit_length() - 1) * most + rank
    slot = jnp.where(live, place * pool + order, -1)
    lane = order + lax.rem(me_ref[0], LANES // pool) * pool
    lane_hot = as_bf16(lax.broadcasted_iota(jnp.int32, (LANES, rows), 0) == lane)
    here = live & (lax.broadcasted_iota(jnp.int32, (inner, rows), 0) == place)
    marked = jnp.where(here, (column_ref[...] + 1).astype(jnp.float32), 0.0)
    labels = lax.dot_general(
        marked.astype(jnp.bfloat16), lane_hot, NT, preferred_element_type=jnp.float32
    )

    parts = width // LANES
    out_ref[:, parts * pool :, :] = jnp.broadcast_to(
        labels.reshape(inner, 1, LANES), (inner, LABEL_ROWS, LANES)
    ).astype(jnp.bfloat16)

    copies[0].wait()
    copies[1].wait()
    prof_ref[...] = (prof_ref[...].astype(jnp.float32) * 0.5).astype(jnp.bfloat16)
    blocks = [pl.ds(i, ROWS) for i in range(0, rows, ROWS)]
    for i in range(hid // CHUNK):
        part = pl.ds(i * CHUNK, CHUNK)
        if i * CHUNK in starts:
            copies[2 + starts.index(i * CHUNK)].wait()
        for m in blocks:
            u = jnp.dot(prof_ref[m, :], w1_ref[:, part], preferred_element_type=jnp.float32)
            u = u + 0.5 * b1_ref[:, part]
            p = jnp.tanh(u) + 1.0
            hidden = u * p
            hidden_ref[m, part] = hidden.astype(jnp.bfloat16)
            factor_ref[m, part] = p + hidden * (2.0 - p)
    for copy in copies[2 + len(pieces) :]:
        copy.wait()
    scale = 0.5 * cw_ref[...]
    for n, m in enumerate(blocks):
        output = jnp.dot(hidden_ref[m, :], w2_ref[...], preferred_element_type=jnp.float32)
        misfit = scale * (output + b2_ref[...] - rad_ref[m, :].astype(jnp.float32))
        alive = lax.broadcasted_iota(jnp.int32, (ROWS, 1), 0) + n * ROWS < count_ref[...]
        rad_ref[m, :] = jnp.where(alive, misfit, 0.0).astype(jnp.bfloat16)
    for i in range(hid // CHUNK):
        part = pl.ds(i * CHUNK, CHUNK)
        for m in blocks:
            back = lax.dot_general(
                rad_ref[m, :], w2_ref[part, :], NT, preferred_element_type=jnp.float32
            )
            hidden_ref[m, part] = (back * factor_ref[m, part]).astype(jnp.bfloat16)
    for m in blocks:
        grads = lax.dot_general(
            hidden_ref[m, :], w1_ref[...], NT, preferred_element_type=jnp.float32
        )
        prof_ref[m, :] = grads.astype(jnp.bfloat16)
    grads = prof_ref[...]
    wide = ROWS // pool
    sent = []
    for n in range(inner // wide):
        placing = as_bf16(
            lax.broadcasted_iota(jnp.int32, (ROWS, rows), 0) + n * ROWS == slot
        )
        placed = jnp.dot(placing, grads, preferred_element_type=jnp.float32).astype(jnp.bfloat16)
        some = pl.ds(n * wide, wide)
        for k in range(parts):
            out_ref[some, k * pool : (k + 1) * pool, :] = placed[
                :, k * LANES : (k + 1) * LANES
            ].reshape(wide, pool, LANES)
        sent.append(pltpu.make_async_copy(out_ref.at[some], out_hbm.at[some], out_sems.at[n]))
        sent[-1].start()
    for copy in sent:
        copy.wait()


def blocks_kernel(tiles, most, me_ref, got_ref, own_ref, other_ref):
    inner = got_ref.shape[0]
    outer = tiles // inner
    pool = outer * most
    group = LANES // pool
    parts = own_ref.shape[1] // LANES
    marks = got_ref[:, parts * pool :, :].astype(jnp.float32)[:, 0, :]
    index = lax.broadcasted_iota(jnp.int32, (outer * COL_DEV, LANES), 0)
    lane = lax.broadcasted_iota(jnp.int32, (1, LANES), 1) & (pool - 1)
    turn = lax.shift_right_arithmetic(lane, most.bit_length() - 1) ^ (
        lax.shift_right_arithmetic(me_ref[0], inner.bit_length() - 1)
    )
    chosen = []
    for g in range(inner // group):
        label = jnp.sum(marks[g * group : (g + 1) * group], axis=0, keepdims=True)
        label = label.astype(jnp.int32)
        code = jnp.where(label > 0, turn * COL_DEV + label - 1, -1)
        chosen.append(as_bf16(index == code))
    chosen = jnp.concatenate(chosen, axis=1)
    for k in range(parts):
        block = got_ref[:, k * pool : (k + 1) * pool, :].reshape(inner * pool, LANES)
        total = jnp.dot(chosen, block, preferred_element_type=jnp.float32)
        own_ref[:, k * LANES : (k + 1) * LANES] = total[:COL_DEV]
        other_ref[:, k * LANES : (k + 1) * LANES] = total[COL_DEV:].astype(jnp.bfloat16)


def per_device(
    profiles,
    radiances,
    inner_weight,
    inner_bias,
    outer_weight,
    outer_bias,
    channel_weight,
    counts,
    owner,
    column,
):
    tiles = lax.axis_size("tile")
    rows, width = profiles.shape
    hid = inner_weight.shape[1]
    chan = radiances.shape[1]
    most = max(2, 2 * rows // tiles)
    inner = tiles // OUTER
    pool = OUTER * most
    high = width // LANES * pool + LABEL_ROWS
    me = lax.axis_index("tile").astype(jnp.int32).reshape(1)
    vmem = pl.BlockSpec(memory_space=pltpu.VMEM)
    smem = pl.BlockSpec(memory_space=pltpu.SMEM)
    anywhere = pl.BlockSpec(memory_space=pl.ANY)
    bucket = pl.pallas_call(
        functools.partial(rows_kernel, tiles, most),
        out_shape=jax.ShapeDtypeStruct((inner, high, LANES), jnp.bfloat16),
        in_specs=[smem, vmem, vmem, vmem] + [anywhere] * 7,
        out_specs=anywhere,
        scratch_shapes=[
            pltpu.VMEM((rows, width), jnp.bfloat16),
            pltpu.VMEM((rows, chan), jnp.bfloat16),
            pltpu.VMEM((width, hid), jnp.bfloat16),
            pltpu.VMEM((1, hid), jnp.float32),
            pltpu.VMEM((hid, chan), jnp.bfloat16),
            pltpu.VMEM((1, chan), jnp.float32),
            pltpu.VMEM((1, chan), jnp.float32),
            pltpu.VMEM((rows, hid), jnp.bfloat16),
            pltpu.VMEM((rows, hid), jnp.float32),
            pltpu.VMEM((inner, high, LANES), jnp.bfloat16),
            pltpu.SemaphoreType.DMA((8,)),
            pltpu.SemaphoreType.DMA((inner * pool // ROWS,)),
        ],
        compiler_params=pltpu.CompilerParams(vmem_limit_bytes=60 * 1024 * 1024),
        name="rows_kernel",
    )(
        me,
        counts.reshape(1, 1),
        owner.reshape(1, rows),
        column.reshape(1, rows),
        profiles,
        radiances,
        inner_weight,
        inner_bias.reshape(1, hid),
        outer_weight,
        outer_bias.reshape(1, chan),
        channel_weight.reshape(1, chan),
    )
    halves = [[o * inner + i for i in range(inner)] for o in range(OUTER)]
    got = lax.all_to_all(
        bucket, "tile", split_axis=0, concat_axis=0, axis_index_groups=halves, tiled=True
    )
    own, other = pl.pallas_call(
        functools.partial(blocks_kernel, tiles, most),
        out_shape=[
            jax.ShapeDtypeStruct((COL_DEV, width), jnp.float32),
            jax.ShapeDtypeStruct((COL_DEV, width), jnp.bfloat16),
        ],
        in_specs=[smem, vmem],
        out_specs=[vmem, vmem],
        compiler_params=pltpu.CompilerParams(vmem_limit_bytes=24 * 1024 * 1024),
        name="blocks_kernel",
    )(me, got)
    pairs = [(t, (t + inner) % tiles) for t in range(tiles)]
    return own + lax.ppermute(other, "tile", pairs).astype(jnp.float32)


def solution(mesh):
    placed = (
        P(("group", "tile"), None),
        P(("group", "tile"), None),
        P(),
        P(),
        P(),
        P(),
        P(),
        P(("group", "tile")),
        P(("group", "tile"), None),
        P(("group", "tile")),
    )
    return jax.shard_map(
        per_device,
        mesh=mesh,
        in_specs=placed,
        out_specs=P(("group", "tile"), None),
        check_vma=False,
    )
```

```python
import functools

import jax
import jax.numpy as jnp
from jax import lax
from jax.experimental import pallas as pl
from jax.experimental.pallas import tpu as pltpu
from jax.sharding import PartitionSpec as P

COL_DEV = 128
CHUNK = 256
LANES = 128
LABEL_ROWS = 8
ROWS = 256
NT = (((1,), (1,)), ((), ()))


def as_bf16(mask):
    return mask.astype(jnp.float32).astype(jnp.bfloat16)


def rows_kernel(
    tiles,
    most,
    me_ref,
    count_ref,
    owner_ref,
    column_ref,
    prof_hbm,
    rad_hbm,
    w1_hbm,
    b1_hbm,
    w2_hbm,
    b2_hbm,
    cw_hbm,
    *refs,
):
    (
        prof_ref,
        rad_ref,
        w1_ref,
        b1_ref,
        w2_ref,
        b2_ref,
        cw_ref,
        hidden_ref,
        factor_ref,
        far_ref,
        near_ref,
        sems,
        out_sems,
    ) = refs[-13:]
    far_hbm, near_hbms = refs[0], refs[1:-13]
    rows, width = prof_ref.shape
    hid = w1_ref.shape[1]
    chan = rad_ref.shape[1]
    starts = [0, hid // 4, hid]
    pieces = [pl.ds(lo, hi - lo) for lo, hi in zip(starts[:-1], starts[1:])]
    pairs = (
        [(prof_hbm, prof_ref), (b1_hbm, b1_ref)]
        + [(w1_hbm.at[:, piece], w1_ref.at[:, piece]) for piece in pieces]
        + [(w2_hbm, w2_ref), (rad_hbm, rad_ref), (b2_hbm, b2_ref), (cw_hbm, cw_ref)]
    )
    copies = [
        pltpu.make_async_copy(src, dst, sems.at[i]) for i, (src, dst) in enumerate(pairs)
    ]
    for copy in copies:
        copy.start()

    inner, chips = far_ref.shape[0], near_ref.shape[0]
    me = me_ref[0]
    live = lax.broadcasted_iota(jnp.int32, (1, rows), 1) < count_ref[0]
    owner = jnp.where(live, owner_ref[...], -1)
    mine = lax.broadcasted_iota(jnp.int32, (tiles, rows), 0) == owner
    one_hot = mine.astype(jnp.float32)
    upper = as_bf16(
        lax.broadcasted_iota(jnp.int32, (rows, rows), 0)
        <= lax.broadcasted_iota(jnp.int32, (rows, rows), 1)
    )
    running = jnp.dot(one_hot.astype(jnp.bfloat16), upper, preferred_element_type=jnp.float32)
    rank = jnp.sum(running * one_hot, axis=0, keepdims=True).astype(jnp.int32) - 1
    pool = 2 * most
    place = owner & (inner - 1)
    near = (owner & inner) == (me & inner)
    chip = lax.shift_right_arithmetic(place, 1) ^ (
        lax.shift_right_arithmetic(me, 1) & (chips - 1)
    )
    order = (owner & 1) * most + rank
    slot = jnp.where(near, inner * most + chip * pool + order, place * most + rank)
    slot = jnp.where(live, slot, -1)
    slots = inner * most + chips * pool
    placing = as_bf16(lax.broadcasted_iota(jnp.int32, (slots, rows), 0) == slot)
    lane = jnp.where(
        near,
        (chip & (LANES // pool - 1)) * pool + order,
        (me & (LANES // most - 1)) * most + rank,
    )
    lane_hot = as_bf16(lax.broadcasted_iota(jnp.int32, (LANES, rows), 0) == lane)
    block = jnp.where(live, jnp.where(near, inner + chip, place), -1)
    here = lax.broadcasted_iota(jnp.int32, (inner + chips, rows), 0) == block
    marked = jnp.where(here, (column_ref[...] + 1).astype(jnp.float32), 0.0)
    labels = lax.dot_general(
        marked.astype(jnp.bfloat16), lane_hot, NT, preferred_element_type=jnp.float32
    )
    parts = width // LANES
    far_ref[:, parts * most :, :] = jnp.broadcast_to(
        labels[:inner].reshape(inner, 1, LANES), (inner, LABEL_ROWS, LANES)
    ).astype(jnp.bfloat16)
    near_ref[:, parts * pool :, :] = jnp.broadcast_to(
        labels[inner:].reshape(chips, 1, LANES), (chips, LABEL_ROWS, LANES)
    ).astype(jnp.bfloat16)

    copies[0].wait()
    copies[1].wait()
    prof_ref[...] = (prof_ref[...].astype(jnp.float32) * 0.5).astype(jnp.bfloat16)
    blocks = [pl.ds(i, ROWS) for i in range(0, rows, ROWS)]
    for i in range(hid // CHUNK):
        part = pl.ds(i * CHUNK, CHUNK)
        if i * CHUNK in starts:
            copies[2 + starts.index(i * CHUNK)].wait()
        for m in blocks:
            u = jnp.dot(prof_ref[m, :], w1_ref[:, part], preferred_element_type=jnp.float32)
            u = u + 0.5 * b1_ref[:, part]
            p = jnp.tanh(u) + 1.0
            hidden = u * p
            hidden_ref[m, part] = hidden.astype(jnp.bfloat16)
            factor_ref[m, part] = p + hidden * (2.0 - p)
    for copy in copies[2 + len(pieces) :]:
        copy.wait()
    scale = 0.5 * cw_ref[...]
    for n, m in enumerate(blocks):
        output = jnp.dot(hidden_ref[m, :], w2_ref[...], preferred_element_type=jnp.float32)
        misfit = scale * (output + b2_ref[...] - rad_ref[m, :].astype(jnp.float32))
        alive = lax.broadcasted_iota(jnp.int32, (ROWS, 1), 0) + n * ROWS < count_ref[0]
        rad_ref[m, :] = jnp.where(alive, misfit, 0.0).astype(jnp.bfloat16)
    for i in range(hid // CHUNK):
        part = pl.ds(i * CHUNK, CHUNK)
        for m in blocks:
            back = lax.dot_general(
                rad_ref[m, :], w2_ref[part, :], NT, preferred_element_type=jnp.float32
            )
            hidden_ref[m, part] = (back * factor_ref[m, part]).astype(jnp.bfloat16)
    for m in blocks:
        grads = lax.dot_general(
            hidden_ref[m, :], w1_ref[...], NT, preferred_element_type=jnp.float32
        )
        prof_ref[m, :] = grads.astype(jnp.bfloat16)
    grads = prof_ref[...]
    sent = []
    for n in range(slots // ROWS):
        placed = jnp.dot(
            placing[n * ROWS : (n + 1) * ROWS], grads, preferred_element_type=jnp.float32
        ).astype(jnp.bfloat16)
        far = n * ROWS < inner * most
        high, target_ref = (most, far_ref) if far else (pool, near_ref)
        wide = ROWS // high
        first = n * wide if far else (n * ROWS - inner * most) // high
        for k in range(parts):
            target_ref[first : first + wide, k * high : (k + 1) * high, :] = placed[
                :, k * LANES : (k + 1) * LANES
            ].reshape(wide, high, LANES)
        some = pl.ds(first, wide)
        if far:
            moves = [(far_ref.at[some], far_hbm.at[some])]
        else:
            moves = [(near_ref.at[j], near_hbms[j]) for j in range(first, first + wide)]
        for src, dst in moves:
            sent.append(pltpu.make_async_copy(src, dst, out_sems.at[len(sent)]))
            sent[-1].start()
    for copy in sent:
        copy.wait()


def far_kernel(most, got_ref, out_ref):
    inner = got_ref.shape[0]
    group = LANES // most
    parts = out_ref.shape[1] // LANES
    marks = got_ref[:, parts * most :, :].astype(jnp.float32)[:, 0, :]
    index = lax.broadcasted_iota(jnp.int32, (COL_DEV, LANES), 0) + 1
    chosen = []
    for g in range(inner // group):
        label = jnp.sum(marks[g * group : (g + 1) * group], axis=0, keepdims=True)
        chosen.append(as_bf16(index == label.astype(jnp.int32)))
    chosen = jnp.concatenate(chosen, axis=1)
    for k in range(parts):
        block = got_ref[:, k * most : (k + 1) * most, :].reshape(inner * most, LANES)
        total = jnp.dot(chosen, block, preferred_element_type=jnp.float32)
        out_ref[:, k * LANES : (k + 1) * LANES] = total.astype(jnp.bfloat16)


def near_kernel(most, me_ref, *refs):
    got, (own_ref, other_ref) = refs[:-2], refs[-2:]
    pool = 2 * most
    group = LANES // pool
    parts = own_ref.shape[1] // LANES
    index = lax.broadcasted_iota(jnp.int32, (2 * COL_DEV, LANES), 0)
    lane = lax.broadcasted_iota(jnp.int32, (1, LANES), 1) & (pool - 1)
    turn = lax.shift_right_arithmetic(lane, most.bit_length() - 1) ^ (me_ref[0] & 1)
    chosen = []
    for g in range(len(got) // group):
        label = sum(
            ref[parts * pool :, :].astype(jnp.float32)[:1]
            for ref in got[g * group : (g + 1) * group]
        ).astype(jnp.int32)
        code = jnp.where(label > 0, turn * COL_DEV + label - 1, -1)
        chosen.append(as_bf16(index == code))
    chosen = jnp.concatenate(chosen, axis=1)
    for k in range(parts):
        block = jnp.concatenate([ref[k * pool : (k + 1) * pool, :] for ref in got], axis=0)
        total = jnp.dot(chosen, block, preferred_element_type=jnp.float32)
        own_ref[:, k * LANES : (k + 1) * LANES] = total[:COL_DEV]
        other_ref[:, k * LANES : (k + 1) * LANES] = total[COL_DEV:].astype(jnp.bfloat16)


def per_device(
    profiles,
    radiances,
    inner_weight,
    inner_bias,
    outer_weight,
    outer_bias,
    channel_weight,
    counts,
    owner,
    column,
):
    tiles = lax.axis_size("tile")
    rows, width = profiles.shape
    hid = inner_weight.shape[1]
    chan = radiances.shape[1]
    most = max(2, 2 * rows // tiles)
    inner = tiles // 2
    chips = inner // 2
    far_high = width // LANES * most + LABEL_ROWS
    near_high = width // LANES * 2 * most + LABEL_ROWS
    me = lax.axis_index("tile").astype(jnp.int32).reshape(1)
    vmem = pl.BlockSpec(memory_space=pltpu.VMEM)
    smem = pl.BlockSpec(memory_space=pltpu.SMEM)
    anywhere = pl.BlockSpec(memory_space=pl.ANY)
    far, *near = pl.pallas_call(
        functools.partial(rows_kernel, tiles, most),
        out_shape=[jax.ShapeDtypeStruct((inner, far_high, LANES), jnp.bfloat16)]
        + [jax.ShapeDtypeStruct((near_high, LANES), jnp.bfloat16)] * chips,
        in_specs=[smem, smem, vmem, vmem] + [anywhere] * 7,
        out_specs=[anywhere] * (1 + chips),
        scratch_shapes=[
            pltpu.VMEM((rows, width), jnp.bfloat16),
            pltpu.VMEM((rows, chan), jnp.bfloat16),
            pltpu.VMEM((width, hid), jnp.bfloat16),
            pltpu.VMEM((1, hid), jnp.float32),
            pltpu.VMEM((hid, chan), jnp.bfloat16),
            pltpu.VMEM((1, chan), jnp.float32),
            pltpu.VMEM((1, chan), jnp.float32),
            pltpu.VMEM((rows, hid), jnp.bfloat16),
            pltpu.VMEM((rows, hid), jnp.float32),
            pltpu.VMEM((inner, far_high, LANES), jnp.bfloat16),
            pltpu.VMEM((chips, near_high, LANES), jnp.bfloat16),
            pltpu.SemaphoreType.DMA((8,)),
            pltpu.SemaphoreType.DMA((inner * most // ROWS + chips,)),
        ],
        compiler_params=pltpu.CompilerParams(vmem_limit_bytes=60 * 1024 * 1024),
        name="rows_kernel",
    )(
        me,
        counts,
        owner.reshape(1, rows),
        column.reshape(1, rows),
        profiles,
        radiances,
        inner_weight,
        inner_bias.reshape(1, hid),
        outer_weight,
        outer_bias.reshape(1, chan),
        channel_weight.reshape(1, chan),
    )
    halves = [[o * inner + i for i in range(inner)] for o in range(2)]
    got = lax.all_to_all(
        far, "tile", split_axis=0, concat_axis=0, axis_index_groups=halves, tiled=True
    )

    def swap(block, bits):
        pairs = [(t, t ^ bits) for t in range(tiles)]
        return lax.ppermute(block, "tile", pairs)

    across = pl.pallas_call(
        functools.partial(far_kernel, most),
        out_shape=jax.ShapeDtypeStruct((COL_DEV, width), jnp.bfloat16),
        in_specs=[vmem],
        out_specs=vmem,
        compiler_params=pltpu.CompilerParams(vmem_limit_bytes=16 * 1024 * 1024),
        name="far_kernel",
    )(got)
    from_half = swap(across, inner)
    came = [near[0]] + [swap(near[j], 2 * j) for j in range(1, chips)]
    own, other = pl.pallas_call(
        functools.partial(near_kernel, most),
        out_shape=[
            jax.ShapeDtypeStruct((COL_DEV, width), jnp.float32),
            jax.ShapeDtypeStruct((COL_DEV, width), jnp.bfloat16),
        ],
        in_specs=[smem] + [vmem] * chips,
        out_specs=[vmem, vmem],
        compiler_params=pltpu.CompilerParams(vmem_limit_bytes=24 * 1024 * 1024),
        name="near_kernel",
    )(me, *came)
    from_core = swap(other, 1)
    return own + from_core.astype(jnp.float32) + from_half.astype(jnp.float32)


def solution(mesh):
    placed = (
        P(("group", "tile"), None),
        P(("group", "tile"), None),
        P(),
        P(),
        P(),
        P(),
        P(),
        P(("group", "tile")),
        P(("group", "tile"), None),
        P(("group", "tile")),
    )
    return jax.shard_map(
        per_device,
        mesh=mesh,
        in_specs=placed,
        out_specs=P(("group", "tile"), None),
        check_vma=False,
    )
```

```python
import functools

import jax
import jax.numpy as jnp
from jax import lax
from jax.experimental import pallas as pl
from jax.experimental.pallas import tpu as pltpu
from jax.sharding import PartitionSpec as P

COL_DEV = 128
CHUNK = 256
LANES = 128
LABEL_ROWS = 8
OUTER = 2
ROWS = 256
NT = (((1,), (1,)), ((), ()))


def as_bf16(mask):
    return mask.astype(jnp.float32).astype(jnp.bfloat16)


def rows_kernel(
    tiles,
    most,
    me_ref,
    count_ref,
    owner_ref,
    column_ref,
    prof_hbm,
    rad_hbm,
    w1_hbm,
    b1_hbm,
    w2_hbm,
    b2_hbm,
    cw_hbm,
    out_ref,
    prof_ref,
    rad_ref,
    w1_ref,
    b1_ref,
    w2_ref,
    b2_ref,
    cw_ref,
    hidden_ref,
    factor_ref,
    sems,
):
    rows, width = prof_ref.shape
    hid = w1_ref.shape[1]
    chan = rad_ref.shape[1]
    starts = [0, hid // 4, hid]
    pieces = [pl.ds(lo, hi - lo) for lo, hi in zip(starts[:-1], starts[1:])]
    pairs = (
        [(prof_hbm, prof_ref), (b1_hbm, b1_ref)]
        + [(w1_hbm.at[:, piece], w1_ref.at[:, piece]) for piece in pieces]
        + [(w2_hbm, w2_ref), (rad_hbm, rad_ref), (b2_hbm, b2_ref), (cw_hbm, cw_ref)]
    )
    copies = [
        pltpu.make_async_copy(src, dst, sems.at[i]) for i, (src, dst) in enumerate(pairs)
    ]
    for copy in copies:
        copy.start()

    inner = out_ref.shape[0]
    live = lax.broadcasted_iota(jnp.int32, (1, rows), 1) < count_ref[0]
    owner = jnp.where(live, owner_ref[...], -1)
    mine = lax.broadcasted_iota(jnp.int32, (tiles, rows), 0) == owner
    one_hot = mine.astype(jnp.float32)
    upper = as_bf16(
        lax.broadcasted_iota(jnp.int32, (rows, rows), 0)
        <= lax.broadcasted_iota(jnp.int32, (rows, rows), 1)
    )
    running = jnp.dot(one_hot.astype(jnp.bfloat16), upper, preferred_element_type=jnp.float32)
    rank = jnp.sum(running * one_hot, axis=0, keepdims=True).astype(jnp.int32) - 1
    pool = tiles // inner * most
    place = owner & (inner - 1)
    order = lax.shift_right_arithmetic(owner, inner.bit_length() - 1) * most + rank
    slot = jnp.where(live, place * pool + order, -1)
    placing = as_bf16(lax.broadcasted_iota(jnp.int32, (inner * pool, rows), 0) == slot)
    lane = order + lax.rem(me_ref[0], LANES // pool) * pool
    lane_hot = as_bf16(lax.broadcasted_iota(jnp.int32, (LANES, rows), 0) == lane)
    here = live & (lax.broadcasted_iota(jnp.int32, (inner, rows), 0) == place)
    marked = jnp.where(here, (column_ref[...] + 1).astype(jnp.float32), 0.0)
    labels = lax.dot_general(
        marked.astype(jnp.bfloat16), lane_hot, NT, preferred_element_type=jnp.float32
    )

    parts = width // LANES
    out_ref[:, parts * pool :, :] = jnp.broadcast_to(
        labels.reshape(inner, 1, LANES), (inner, LABEL_ROWS, LANES)
    ).astype(jnp.bfloat16)

    copies[0].wait()
    copies[1].wait()
    prof_ref[...] = (prof_ref[...].astype(jnp.float32) * 0.5).astype(jnp.bfloat16)
    blocks = [pl.ds(i, ROWS) for i in range(0, rows, ROWS)]
    for i in range(hid // CHUNK):
        part = pl.ds(i * CHUNK, CHUNK)
        if i * CHUNK in starts:
            copies[2 + starts.index(i * CHUNK)].wait()
        for m in blocks:
            u = jnp.dot(prof_ref[m, :], w1_ref[:, part], preferred_element_type=jnp.float32)
            u = u + 0.5 * b1_ref[:, part]
            p = jnp.tanh(u) + 1.0
            hidden = u * p
            hidden_ref[m, part] = hidden.astype(jnp.bfloat16)
            factor_ref[m, part] = p + hidden * (2.0 - p)
    for copy in copies[2 + len(pieces) :]:
        copy.wait()
    scale = 0.5 * cw_ref[...]
    for n, m in enumerate(blocks):
        output = jnp.dot(hidden_ref[m, :], w2_ref[...], preferred_element_type=jnp.float32)
        misfit = scale * (output + b2_ref[...] - rad_ref[m, :].astype(jnp.float32))
        alive = lax.broadcasted_iota(jnp.int32, (ROWS, 1), 0) + n * ROWS < count_ref[0]
        rad_ref[m, :] = jnp.where(alive, misfit, 0.0).astype(jnp.bfloat16)
    for i in range(hid // CHUNK):
        part = pl.ds(i * CHUNK, CHUNK)
        for m in blocks:
            back = lax.dot_general(
                rad_ref[m, :], w2_ref[part, :], NT, preferred_element_type=jnp.float32
            )
            hidden_ref[m, part] = (back * factor_ref[m, part]).astype(jnp.bfloat16)
    for m in blocks:
        grads = lax.dot_general(
            hidden_ref[m, :], w1_ref[...], NT, preferred_element_type=jnp.float32
        )
        prof_ref[m, :] = grads.astype(jnp.bfloat16)
    grads = prof_ref[...]
    wide = ROWS // pool
    for n in range(inner // wide):
        placed = jnp.dot(
            placing[n * ROWS : (n + 1) * ROWS], grads, preferred_element_type=jnp.float32
        ).astype(jnp.bfloat16)
        some = pl.ds(n * wide, wide)
        for k in range(parts):
            out_ref[some, k * pool : (k + 1) * pool, :] = placed[
                :, k * LANES : (k + 1) * LANES
            ].reshape(wide, pool, LANES)


def blocks_kernel(tiles, most, me_ref, got_ref, own_ref, other_ref):
    inner = got_ref.shape[0]
    outer = tiles // inner
    pool = outer * most
    group = LANES // pool
    parts = own_ref.shape[1] // LANES
    marks = got_ref[:, parts * pool :, :].astype(jnp.float32)[:, 0, :]
    index = lax.broadcasted_iota(jnp.int32, (outer * COL_DEV, LANES), 0)
    lane = lax.broadcasted_iota(jnp.int32, (1, LANES), 1) & (pool - 1)
    turn = lax.shift_right_arithmetic(lane, most.bit_length() - 1) ^ (
        lax.shift_right_arithmetic(me_ref[0], inner.bit_length() - 1)
    )
    chosen = []
    for g in range(inner // group):
        label = jnp.sum(marks[g * group : (g + 1) * group], axis=0, keepdims=True)
        label = label.astype(jnp.int32)
        code = jnp.where(label > 0, turn * COL_DEV + label - 1, -1)
        chosen.append(as_bf16(index == code))
    chosen = jnp.concatenate(chosen, axis=1)
    for k in range(parts):
        block = got_ref[:, k * pool : (k + 1) * pool, :].reshape(inner * pool, LANES)
        total = jnp.dot(chosen, block, preferred_element_type=jnp.float32)
        own_ref[:, k * LANES : (k + 1) * LANES] = total[:COL_DEV]
        other_ref[:, k * LANES : (k + 1) * LANES] = total[COL_DEV:].astype(jnp.bfloat16)


def per_device(
    profiles,
    radiances,
    inner_weight,
    inner_bias,
    outer_weight,
    outer_bias,
    channel_weight,
    counts,
    owner,
    column,
):
    tiles = lax.axis_size("tile")
    rows, width = profiles.shape
    hid = inner_weight.shape[1]
    chan = radiances.shape[1]
    most = max(2, 2 * rows // tiles)
    inner = tiles // OUTER
    pool = OUTER * most
    high = width // LANES * pool + LABEL_ROWS
    me = lax.axis_index("tile").astype(jnp.int32).reshape(1)
    vmem = pl.BlockSpec(memory_space=pltpu.VMEM)
    smem = pl.BlockSpec(memory_space=pltpu.SMEM)
    anywhere = pl.BlockSpec(memory_space=pl.ANY)
    bucket = pl.pallas_call(
        functools.partial(rows_kernel, tiles, most),
        out_shape=jax.ShapeDtypeStruct((inner, high, LANES), jnp.bfloat16),
        in_specs=[smem, smem, vmem, vmem] + [anywhere] * 7,
        out_specs=vmem,
        scratch_shapes=[
            pltpu.VMEM((rows, width), jnp.bfloat16),
            pltpu.VMEM((rows, chan), jnp.bfloat16),
            pltpu.VMEM((width, hid), jnp.bfloat16),
            pltpu.VMEM((1, hid), jnp.float32),
            pltpu.VMEM((hid, chan), jnp.bfloat16),
            pltpu.VMEM((1, chan), jnp.float32),
            pltpu.VMEM((1, chan), jnp.float32),
            pltpu.VMEM((rows, hid), jnp.bfloat16),
            pltpu.VMEM((rows, hid), jnp.float32),
            pltpu.SemaphoreType.DMA((8,)),
        ],
        compiler_params=pltpu.CompilerParams(vmem_limit_bytes=40 * 1024 * 1024),
        name="rows_kernel",
    )(
        me,
        counts,
        *[
            pltpu.with_memory_space_constraint(operand, pltpu.HBM)
            for operand in (
                owner.reshape(1, rows),
                column.reshape(1, rows),
                profiles,
                radiances,
                inner_weight,
                inner_bias.reshape(1, hid),
                outer_weight,
                outer_bias.reshape(1, chan),
                channel_weight.reshape(1, chan),
            )
        ],
    )
    halves = [[o * inner + i for i in range(inner)] for o in range(OUTER)]
    got = lax.all_to_all(
        bucket, "tile", split_axis=0, concat_axis=0, axis_index_groups=halves, tiled=True
    )
    own, other = pl.pallas_call(
        functools.partial(blocks_kernel, tiles, most),
        out_shape=[
            jax.ShapeDtypeStruct((COL_DEV, width), jnp.float32),
            jax.ShapeDtypeStruct((COL_DEV, width), jnp.bfloat16),
        ],
        in_specs=[smem, vmem],
        out_specs=[vmem, vmem],
        compiler_params=pltpu.CompilerParams(vmem_limit_bytes=24 * 1024 * 1024),
        name="blocks_kernel",
    )(me, got)
    pairs = [(t, (t + inner) % tiles) for t in range(tiles)]
    return own + lax.ppermute(other, "tile", pairs).astype(jnp.float32)


def solution(mesh):
    placed = (
        P(("group", "tile"), None),
        P(("group", "tile"), None),
        P(),
        P(),
        P(),
        P(),
        P(),
        P(("group", "tile")),
        P(("group", "tile"), None),
        P(("group", "tile")),
    )
    return jax.shard_map(
        per_device,
        mesh=mesh,
        in_specs=placed,
        out_specs=P(("group", "tile"), None),
        check_vma=False,
    )
```

```python
import functools

import jax
import jax.numpy as jnp
from jax import lax
from jax.experimental import pallas as pl
from jax.experimental.pallas import tpu as pltpu
from jax.sharding import PartitionSpec as P

COL_DEV = 128
CHUNK = 256
LANES = 128
LABEL_ROWS = 8
OUTER = 2
ROWS = 256
NT = (((1,), (1,)), ((), ()))


def as_bf16(mask):
    return mask.astype(jnp.float32).astype(jnp.bfloat16)


def rows_kernel(
    tiles,
    most,
    me_ref,
    count_ref,
    owner_hbm,
    column_hbm,
    prof_hbm,
    rad_hbm,
    w1_hbm,
    b1_hbm,
    w2_hbm,
    b2_hbm,
    cw_hbm,
    out_ref,
    owner_ref,
    column_ref,
    prof_ref,
    rad_ref,
    w1_ref,
    b1_ref,
    w2_ref,
    b2_ref,
    cw_ref,
    hidden_ref,
    factor_ref,
    sems,
):
    rows, width = prof_ref.shape
    hid = w1_ref.shape[1]
    chan = rad_ref.shape[1]
    starts = [0, hid // 4, hid]
    pieces = [pl.ds(lo, hi - lo) for lo, hi in zip(starts[:-1], starts[1:])]
    pairs = (
        [(prof_hbm, prof_ref), (b1_hbm, b1_ref)]
        + [(w1_hbm.at[:, piece], w1_ref.at[:, piece]) for piece in pieces]
        + [(w2_hbm, w2_ref), (rad_hbm, rad_ref), (b2_hbm, b2_ref), (cw_hbm, cw_ref)]
        + [(owner_hbm, owner_ref), (column_hbm, column_ref)]
    )
    copies = [
        pltpu.make_async_copy(src, dst, sems.at[i]) for i, (src, dst) in enumerate(pairs)
    ]
    for copy in copies:
        copy.start()

    copies[0].wait()
    copies[1].wait()
    prof_ref[...] = (prof_ref[...].astype(jnp.float32) * 0.5).astype(jnp.bfloat16)
    blocks = [pl.ds(i, ROWS) for i in range(0, rows, ROWS)]
    for i in range(hid // CHUNK):
        part = pl.ds(i * CHUNK, CHUNK)
        if i * CHUNK in starts:
            copies[2 + starts.index(i * CHUNK)].wait()
        for m in blocks:
            u = jnp.dot(prof_ref[m, :], w1_ref[:, part], preferred_element_type=jnp.float32)
            u = u + 0.5 * b1_ref[:, part]
            p = jnp.tanh(u) + 1.0
            hidden = u * p
            hidden_ref[m, part] = hidden.astype(jnp.bfloat16)
            factor_ref[m, part] = p + hidden * (2.0 - p)
    for copy in copies[2 + len(pieces) :]:
        copy.wait()
    inner = out_ref.shape[0]
    live = lax.broadcasted_iota(jnp.int32, (1, rows), 1) < count_ref[0]
    owner = jnp.where(live, owner_ref[...], -1)
    mine = lax.broadcasted_iota(jnp.int32, (tiles, rows), 0) == owner
    one_hot = mine.astype(jnp.float32)
    upper = as_bf16(
        lax.broadcasted_iota(jnp.int32, (rows, rows), 0)
        <= lax.broadcasted_iota(jnp.int32, (rows, rows), 1)
    )
    running = jnp.dot(one_hot.astype(jnp.bfloat16), upper, preferred_element_type=jnp.float32)
    rank = jnp.sum(running * one_hot, axis=0, keepdims=True).astype(jnp.int32) - 1
    pool = tiles // inner * most
    place = owner & (inner - 1)
    order = lax.shift_right_arithmetic(owner, inner.bit_length() - 1) * most + rank
    slot = jnp.where(live, place * pool + order, -1)
    placing = as_bf16(lax.broadcasted_iota(jnp.int32, (inner * pool, rows), 0) == slot)
    lane = order + lax.rem(me_ref[0], LANES // pool) * pool
    lane_hot = as_bf16(lax.broadcasted_iota(jnp.int32, (LANES, rows), 0) == lane)
    here = live & (lax.broadcasted_iota(jnp.int32, (inner, rows), 0) == place)
    marked = jnp.where(here, (column_ref[...] + 1).astype(jnp.float32), 0.0)
    labels = lax.dot_general(
        marked.astype(jnp.bfloat16), lane_hot, NT, preferred_element_type=jnp.float32
    )

    parts = width // LANES
    out_ref[:, parts * pool :, :] = jnp.broadcast_to(
        labels.reshape(inner, 1, LANES), (inner, LABEL_ROWS, LANES)
    ).astype(jnp.bfloat16)

    scale = 0.5 * cw_ref[...]
    for n, m in enumerate(blocks):
        output = jnp.dot(hidden_ref[m, :], w2_ref[...], preferred_element_type=jnp.float32)
        misfit = scale * (output + b2_ref[...] - rad_ref[m, :].astype(jnp.float32))
        alive = lax.broadcasted_iota(jnp.int32, (ROWS, 1), 0) + n * ROWS < count_ref[0]
        rad_ref[m, :] = jnp.where(alive, misfit, 0.0).astype(jnp.bfloat16)
    for i in range(hid // CHUNK):
        part = pl.ds(i * CHUNK, CHUNK)
        for m in blocks:
            back = lax.dot_general(
                rad_ref[m, :], w2_ref[part, :], NT, preferred_element_type=jnp.float32
            )
            hidden_ref[m, part] = (back * factor_ref[m, part]).astype(jnp.bfloat16)
    for m in blocks:
        grads = lax.dot_general(
            hidden_ref[m, :], w1_ref[...], NT, preferred_element_type=jnp.float32
        )
        prof_ref[m, :] = grads.astype(jnp.bfloat16)
    grads = prof_ref[...]
    wide = ROWS // pool
    for n in range(inner // wide):
        placed = jnp.dot(
            placing[n * ROWS : (n + 1) * ROWS], grads, preferred_element_type=jnp.float32
        ).astype(jnp.bfloat16)
        some = pl.ds(n * wide, wide)
        for k in range(parts):
            out_ref[some, k * pool : (k + 1) * pool, :] = placed[
                :, k * LANES : (k + 1) * LANES
            ].reshape(wide, pool, LANES)


def blocks_kernel(tiles, most, me_ref, got_ref, own_ref, other_ref):
    inner = got_ref.shape[0]
    outer = tiles // inner
    pool = outer * most
    group = LANES // pool
    parts = own_ref.shape[1] // LANES
    marks = got_ref[:, parts * pool :, :].astype(jnp.float32)[:, 0, :]
    index = lax.broadcasted_iota(jnp.int32, (outer * COL_DEV, LANES), 0)
    lane = lax.broadcasted_iota(jnp.int32, (1, LANES), 1) & (pool - 1)
    turn = lax.shift_right_arithmetic(lane, most.bit_length() - 1) ^ (
        lax.shift_right_arithmetic(me_ref[0], inner.bit_length() - 1)
    )
    chosen = []
    for g in range(inner // group):
        label = jnp.sum(marks[g * group : (g + 1) * group], axis=0, keepdims=True)
        label = label.astype(jnp.int32)
        code = jnp.where(label > 0, turn * COL_DEV + label - 1, -1)
        chosen.append(as_bf16(index == code))
    chosen = jnp.concatenate(chosen, axis=1)
    for k in range(parts):
        block = got_ref[:, k * pool : (k + 1) * pool, :].reshape(inner * pool, LANES)
        total = jnp.dot(chosen, block, preferred_element_type=jnp.float32)
        own_ref[:, k * LANES : (k + 1) * LANES] = total[:COL_DEV]
        other_ref[:, k * LANES : (k + 1) * LANES] = total[COL_DEV:].astype(jnp.bfloat16)


def per_device(
    profiles,
    radiances,
    inner_weight,
    inner_bias,
    outer_weight,
    outer_bias,
    channel_weight,
    counts,
    owner,
    column,
):
    tiles = lax.axis_size("tile")
    rows, width = profiles.shape
    hid = inner_weight.shape[1]
    chan = radiances.shape[1]
    most = max(2, 2 * rows // tiles)
    inner = tiles // OUTER
    pool = OUTER * most
    high = width // LANES * pool + LABEL_ROWS
    me = lax.axis_index("tile").astype(jnp.int32).reshape(1)
    vmem = pl.BlockSpec(memory_space=pltpu.VMEM)
    smem = pl.BlockSpec(memory_space=pltpu.SMEM)
    anywhere = pl.BlockSpec(memory_space=pl.ANY)
    bucket = pl.pallas_call(
        functools.partial(rows_kernel, tiles, most),
        out_shape=jax.ShapeDtypeStruct((inner, high, LANES), jnp.bfloat16),
        in_specs=[smem, smem] + [anywhere] * 9,
        out_specs=vmem,
        scratch_shapes=[
            pltpu.VMEM((1, rows), jnp.int32),
            pltpu.VMEM((1, rows), jnp.int32),
            pltpu.VMEM((rows, width), jnp.bfloat16),
            pltpu.VMEM((rows, chan), jnp.bfloat16),
            pltpu.VMEM((width, hid), jnp.bfloat16),
            pltpu.VMEM((1, hid), jnp.float32),
            pltpu.VMEM((hid, chan), jnp.bfloat16),
            pltpu.VMEM((1, chan), jnp.float32),
            pltpu.VMEM((1, chan), jnp.float32),
            pltpu.VMEM((rows, hid), jnp.bfloat16),
            pltpu.VMEM((rows, hid), jnp.float32),
            pltpu.SemaphoreType.DMA((10,)),
        ],
        compiler_params=pltpu.CompilerParams(vmem_limit_bytes=40 * 1024 * 1024),
        name="rows_kernel",
    )(
        me,
        counts,
        *[
            pltpu.with_memory_space_constraint(operand, pltpu.HBM)
            for operand in (
                owner.reshape(1, rows),
                column.reshape(1, rows),
                profiles,
                radiances,
                inner_weight,
                inner_bias.reshape(1, hid),
                outer_weight,
                outer_bias.reshape(1, chan),
                channel_weight.reshape(1, chan),
            )
        ],
    )
    halves = [[o * inner + i for i in range(inner)] for o in range(OUTER)]
    got = lax.all_to_all(
        bucket, "tile", split_axis=0, concat_axis=0, axis_index_groups=halves, tiled=True
    )
    own, other = pl.pallas_call(
        functools.partial(blocks_kernel, tiles, most),
        out_shape=[
            jax.ShapeDtypeStruct((COL_DEV, width), jnp.float32),
            jax.ShapeDtypeStruct((COL_DEV, width), jnp.bfloat16),
        ],
        in_specs=[smem, vmem],
        out_specs=[vmem, vmem],
        compiler_params=pltpu.CompilerParams(vmem_limit_bytes=24 * 1024 * 1024),
        name="blocks_kernel",
    )(me, got)
    pairs = [(t, (t + inner) % tiles) for t in range(tiles)]
    return own + lax.ppermute(other, "tile", pairs).astype(jnp.float32)


def solution(mesh):
    placed = (
        P(("group", "tile"), None),
        P(("group", "tile"), None),
        P(),
        P(),
        P(),
        P(),
        P(),
        P(("group", "tile")),
        P(("group", "tile"), None),
        P(("group", "tile")),
    )
    return jax.shard_map(
        per_device,
        mesh=mesh,
        in_specs=placed,
        out_specs=P(("group", "tile"), None),
        check_vma=False,
    )
```

```python
import functools

import jax
import jax.numpy as jnp
from jax import lax
from jax.experimental import pallas as pl
from jax.experimental.pallas import tpu as pltpu
from jax.sharding import PartitionSpec as P

COL_DEV = 128
CHUNK = 256
LANES = 128
LABEL_ROWS = 8
OUTER = 2
ROWS = 256
NT = (((1,), (1,)), ((), ()))


def as_bf16(mask):
    return mask.astype(jnp.float32).astype(jnp.bfloat16)


def rows_kernel(
    tiles,
    most,
    me_ref,
    count_ref,
    owner_hbm,
    column_hbm,
    prof_hbm,
    rad_hbm,
    w1_hbm,
    b1_hbm,
    w2_hbm,
    b2_hbm,
    cw_hbm,
    out_ref,
    owner_ref,
    column_ref,
    prof_ref,
    rad_ref,
    w1_ref,
    b1_ref,
    w2_ref,
    b2_ref,
    cw_ref,
    hidden_ref,
    factor_ref,
    sems,
):
    rows, width = prof_ref.shape
    hid = w1_ref.shape[1]
    chan = rad_ref.shape[1]
    starts = [0, hid // 4, hid]
    pieces = [pl.ds(lo, hi - lo) for lo, hi in zip(starts[:-1], starts[1:])]
    pairs = (
        [(prof_hbm, prof_ref), (b1_hbm, b1_ref)]
        + [(w1_hbm.at[:, piece], w1_ref.at[:, piece]) for piece in pieces]
        + [(w2_hbm, w2_ref), (rad_hbm, rad_ref), (b2_hbm, b2_ref), (cw_hbm, cw_ref)]
        + [(owner_hbm, owner_ref), (column_hbm, column_ref)]
    )
    copies = [
        pltpu.make_async_copy(src, dst, sems.at[i]) for i, (src, dst) in enumerate(pairs)
    ]
    for copy in copies:
        copy.start()

    copies[0].wait()
    copies[1].wait()
    prof_ref[...] = (prof_ref[...].astype(jnp.float32) * 0.5).astype(jnp.bfloat16)
    blocks = [pl.ds(i, ROWS) for i in range(0, rows, ROWS)]
    for i in range(hid // CHUNK):
        part = pl.ds(i * CHUNK, CHUNK)
        if i * CHUNK in starts:
            copies[2 + starts.index(i * CHUNK)].wait()
        for m in blocks:
            u = jnp.dot(prof_ref[m, :], w1_ref[:, part], preferred_element_type=jnp.float32)
            u = u + 0.5 * b1_ref[:, part]
            p = jnp.tanh(u) + 1.0
            hidden = u * p
            hidden_ref[m, part] = hidden.astype(jnp.bfloat16)
            factor_ref[m, part] = p
    for copy in copies[2 + len(pieces) :]:
        copy.wait()
    inner = out_ref.shape[0]
    live = lax.broadcasted_iota(jnp.int32, (1, rows), 1) < count_ref[0]
    owner = jnp.where(live, owner_ref[...], -1)
    mine = lax.broadcasted_iota(jnp.int32, (tiles, rows), 0) == owner
    one_hot = mine.astype(jnp.float32)
    upper = as_bf16(
        lax.broadcasted_iota(jnp.int32, (rows, rows), 0)
        <= lax.broadcasted_iota(jnp.int32, (rows, rows), 1)
    )
    running = jnp.dot(one_hot.astype(jnp.bfloat16), upper, preferred_element_type=jnp.float32)
    rank = jnp.sum(running * one_hot, axis=0, keepdims=True).astype(jnp.int32) - 1
    pool = tiles // inner * most
    place = owner & (inner - 1)
    order = lax.shift_right_arithmetic(owner, inner.bit_length() - 1) * most + rank
    slot = jnp.where(live, place * pool + order, -1)
    placing = as_bf16(lax.broadcasted_iota(jnp.int32, (inner * pool, rows), 0) == slot)
    lane = order + lax.rem(me_ref[0], LANES // pool) * pool
    lane_hot = as_bf16(lax.broadcasted_iota(jnp.int32, (LANES, rows), 0) == lane)
    here = live & (lax.broadcasted_iota(jnp.int32, (inner, rows), 0) == place)
    marked = jnp.where(here, (column_ref[...] + 1).astype(jnp.float32), 0.0)
    labels = lax.dot_general(
        marked.astype(jnp.bfloat16), lane_hot, NT, preferred_element_type=jnp.float32
    )

    parts = width // LANES
    out_ref[:, parts * pool :, :] = jnp.broadcast_to(
        labels.reshape(inner, 1, LANES), (inner, LABEL_ROWS, LANES)
    ).astype(jnp.bfloat16)

    scale = 0.5 * cw_ref[...]
    for n, m in enumerate(blocks):
        output = jnp.dot(hidden_ref[m, :], w2_ref[...], preferred_element_type=jnp.float32)
        misfit = scale * (output + b2_ref[...] - rad_ref[m, :].astype(jnp.float32))
        alive = lax.broadcasted_iota(jnp.int32, (ROWS, 1), 0) + n * ROWS < count_ref[0]
        rad_ref[m, :] = jnp.where(alive, misfit, 0.0).astype(jnp.bfloat16)
    for i in range(hid // CHUNK):
        part = pl.ds(i * CHUNK, CHUNK)
        for m in blocks:
            back = lax.dot_general(
                rad_ref[m, :], w2_ref[part, :], NT, preferred_element_type=jnp.float32
            )
            p = factor_ref[m, part]
            factor = p + hidden_ref[m, part].astype(jnp.float32) * (2.0 - p)
            hidden_ref[m, part] = (back * factor).astype(jnp.bfloat16)
    for m in blocks:
        grads = lax.dot_general(
            hidden_ref[m, :], w1_ref[...], NT, preferred_element_type=jnp.float32
        )
        prof_ref[m, :] = grads.astype(jnp.bfloat16)
    grads = prof_ref[...]
    wide = ROWS // pool
    for n in range(inner // wide):
        placed = jnp.dot(
            placing[n * ROWS : (n + 1) * ROWS], grads, preferred_element_type=jnp.float32
        ).astype(jnp.bfloat16)
        some = pl.ds(n * wide, wide)
        for k in range(parts):
            out_ref[some, k * pool : (k + 1) * pool, :] = placed[
                :, k * LANES : (k + 1) * LANES
            ].reshape(wide, pool, LANES)


def blocks_kernel(tiles, most, me_ref, got_ref, own_ref, other_ref):
    inner = got_ref.shape[0]
    outer = tiles // inner
    pool = outer * most
    group = LANES // pool
    parts = own_ref.shape[1] // LANES
    marks = got_ref[:, parts * pool :, :].astype(jnp.float32)[:, 0, :]
    index = lax.broadcasted_iota(jnp.int32, (outer * COL_DEV, LANES), 0)
    lane = lax.broadcasted_iota(jnp.int32, (1, LANES), 1) & (pool - 1)
    turn = lax.shift_right_arithmetic(lane, most.bit_length() - 1) ^ (
        lax.shift_right_arithmetic(me_ref[0], inner.bit_length() - 1)
    )
    chosen = []
    for g in range(inner // group):
        label = jnp.sum(marks[g * group : (g + 1) * group], axis=0, keepdims=True)
        label = label.astype(jnp.int32)
        code = jnp.where(label > 0, turn * COL_DEV + label - 1, -1)
        chosen.append(as_bf16(index == code))
    chosen = jnp.concatenate(chosen, axis=1)
    for k in range(parts):
        block = got_ref[:, k * pool : (k + 1) * pool, :].reshape(inner * pool, LANES)
        total = jnp.dot(chosen, block, preferred_element_type=jnp.float32)
        own_ref[:, k * LANES : (k + 1) * LANES] = total[:COL_DEV]
        other_ref[:, k * LANES : (k + 1) * LANES] = total[COL_DEV:].astype(jnp.bfloat16)


def per_device(
    profiles,
    radiances,
    inner_weight,
    inner_bias,
    outer_weight,
    outer_bias,
    channel_weight,
    counts,
    owner,
    column,
):
    tiles = lax.axis_size("tile")
    rows, width = profiles.shape
    hid = inner_weight.shape[1]
    chan = radiances.shape[1]
    most = max(2, 2 * rows // tiles)
    inner = tiles // OUTER
    pool = OUTER * most
    high = width // LANES * pool + LABEL_ROWS
    me = lax.axis_index("tile").astype(jnp.int32).reshape(1)
    vmem = pl.BlockSpec(memory_space=pltpu.VMEM)
    smem = pl.BlockSpec(memory_space=pltpu.SMEM)
    anywhere = pl.BlockSpec(memory_space=pl.ANY)
    bucket = pl.pallas_call(
        functools.partial(rows_kernel, tiles, most),
        out_shape=jax.ShapeDtypeStruct((inner, high, LANES), jnp.bfloat16),
        in_specs=[smem, smem] + [anywhere] * 9,
        out_specs=vmem,
        scratch_shapes=[
            pltpu.VMEM((1, rows), jnp.int32),
            pltpu.VMEM((1, rows), jnp.int32),
            pltpu.VMEM((rows, width), jnp.bfloat16),
            pltpu.VMEM((rows, chan), jnp.bfloat16),
            pltpu.VMEM((width, hid), jnp.bfloat16),
            pltpu.VMEM((1, hid), jnp.float32),
            pltpu.VMEM((hid, chan), jnp.bfloat16),
            pltpu.VMEM((1, chan), jnp.float32),
            pltpu.VMEM((1, chan), jnp.float32),
            pltpu.VMEM((rows, hid), jnp.bfloat16),
            pltpu.VMEM((rows, hid), jnp.float32),
            pltpu.SemaphoreType.DMA((10,)),
        ],
        compiler_params=pltpu.CompilerParams(vmem_limit_bytes=40 * 1024 * 1024),
        name="rows_kernel",
    )(
        me,
        counts,
        *[
            pltpu.with_memory_space_constraint(operand, pltpu.HBM)
            for operand in (
                owner.reshape(1, rows),
                column.reshape(1, rows),
                profiles,
                radiances,
                inner_weight,
                inner_bias.reshape(1, hid),
                outer_weight,
                outer_bias.reshape(1, chan),
                channel_weight.reshape(1, chan),
            )
        ],
    )
    halves = [[o * inner + i for i in range(inner)] for o in range(OUTER)]
    got = lax.all_to_all(
        bucket, "tile", split_axis=0, concat_axis=0, axis_index_groups=halves, tiled=True
    )
    own, other = pl.pallas_call(
        functools.partial(blocks_kernel, tiles, most),
        out_shape=[
            jax.ShapeDtypeStruct((COL_DEV, width), jnp.float32),
            jax.ShapeDtypeStruct((COL_DEV, width), jnp.bfloat16),
        ],
        in_specs=[smem, vmem],
        out_specs=[vmem, vmem],
        compiler_params=pltpu.CompilerParams(vmem_limit_bytes=24 * 1024 * 1024),
        name="blocks_kernel",
    )(me, got)
    pairs = [(t, (t + inner) % tiles) for t in range(tiles)]
    return own + lax.ppermute(other, "tile", pairs).astype(jnp.float32)


def solution(mesh):
    placed = (
        P(("group", "tile"), None),
        P(("group", "tile"), None),
        P(),
        P(),
        P(),
        P(),
        P(),
        P(("group", "tile")),
        P(("group", "tile"), None),
        P(("group", "tile")),
    )
    return jax.shard_map(
        per_device,
        mesh=mesh,
        in_specs=placed,
        out_specs=P(("group", "tile"), None),
        check_vma=False,
    )
```

```python
import functools

import jax
import jax.numpy as jnp
from jax import lax
from jax.experimental import pallas as pl
from jax.experimental.pallas import tpu as pltpu
from jax.sharding import PartitionSpec as P

COL_DEV = 128
CHUNK = 256
LANES = 128
LABEL_ROWS = 8
OUTER = 2
ROWS = 256
NT = (((1,), (1,)), ((), ()))


def as_bf16(mask):
    return mask.astype(jnp.float32).astype(jnp.bfloat16)


def rows_kernel(
    tiles,
    most,
    me_ref,
    count_ref,
    owner_hbm,
    column_hbm,
    prof_hbm,
    rad_hbm,
    w1_hbm,
    b1_hbm,
    w2_hbm,
    b2_hbm,
    cw_hbm,
    out_ref,
    owner_ref,
    column_ref,
    prof_ref,
    rad_ref,
    w1_ref,
    b1_ref,
    w2_ref,
    b2_ref,
    cw_ref,
    hidden_ref,
    factor_ref,
    grads_ref,
    sems,
):
    rows, width = prof_ref.shape
    hid = w1_ref.shape[1]
    chan = rad_ref.shape[1]
    starts = [0, hid // 4, hid]
    pieces = [pl.ds(lo, hi - lo) for lo, hi in zip(starts[:-1], starts[1:])]
    pairs = (
        [(prof_hbm, prof_ref), (b1_hbm, b1_ref)]
        + [(w1_hbm.at[:, piece], w1_ref.at[:, piece]) for piece in pieces]
        + [(w2_hbm, w2_ref), (rad_hbm, rad_ref), (b2_hbm, b2_ref), (cw_hbm, cw_ref)]
        + [(owner_hbm, owner_ref), (column_hbm, column_ref)]
    )
    copies = [
        pltpu.make_async_copy(src, dst, sems.at[i]) for i, (src, dst) in enumerate(pairs)
    ]
    for copy in copies:
        copy.start()

    copies[0].wait()
    copies[1].wait()
    prof_ref[...] = (prof_ref[...].astype(jnp.float32) * 0.5).astype(jnp.bfloat16)
    blocks = [pl.ds(i, ROWS) for i in range(0, rows, ROWS)]
    for i in range(hid // CHUNK):
        part = pl.ds(i * CHUNK, CHUNK)
        if i * CHUNK in starts:
            copies[2 + starts.index(i * CHUNK)].wait()
        for m in blocks:
            u = jnp.dot(prof_ref[m, :], w1_ref[:, part], preferred_element_type=jnp.float32)
            u = u + 0.5 * b1_ref[:, part]
            p = jnp.tanh(u) + 1.0
            hidden = u * p
            hidden_ref[m, part] = hidden.astype(jnp.bfloat16)
            factor_ref[m, part] = p + hidden * (2.0 - p)
    for copy in copies[2 + len(pieces) :]:
        copy.wait()
    inner = out_ref.shape[0]
    live = lax.broadcasted_iota(jnp.int32, (1, rows), 1) < count_ref[0]
    owner = jnp.where(live, owner_ref[...], -1)
    mine = lax.broadcasted_iota(jnp.int32, (tiles, rows), 0) == owner
    one_hot = mine.astype(jnp.float32)
    upper = as_bf16(
        lax.broadcasted_iota(jnp.int32, (rows, rows), 0)
        <= lax.broadcasted_iota(jnp.int32, (rows, rows), 1)
    )
    running = jnp.dot(one_hot.astype(jnp.bfloat16), upper, preferred_element_type=jnp.float32)
    rank = jnp.sum(running * one_hot, axis=0, keepdims=True).astype(jnp.int32) - 1
    pool = tiles // inner * most
    place = owner & (inner - 1)
    order = lax.shift_right_arithmetic(owner, inner.bit_length() - 1) * most + rank
    slot = jnp.where(live, place * pool + order, -1)
    placing = as_bf16(lax.broadcasted_iota(jnp.int32, (inner * pool, rows), 0) == slot)
    lane = order + lax.rem(me_ref[0], LANES // pool) * pool
    lane_hot = as_bf16(lax.broadcasted_iota(jnp.int32, (LANES, rows), 0) == lane)
    here = live & (lax.broadcasted_iota(jnp.int32, (inner, rows), 0) == place)
    marked = jnp.where(here, (column_ref[...] + 1).astype(jnp.float32), 0.0)
    labels = lax.dot_general(
        marked.astype(jnp.bfloat16), lane_hot, NT, preferred_element_type=jnp.float32
    )

    parts = width // LANES
    out_ref[:, parts * pool :, :] = jnp.broadcast_to(
        labels.reshape(inner, 1, LANES), (inner, LABEL_ROWS, LANES)
    ).astype(jnp.bfloat16)

    scale = 0.5 * cw_ref[...]
    for n, m in enumerate(blocks):
        output = jnp.dot(hidden_ref[m, :], w2_ref[...], preferred_element_type=jnp.float32)
        misfit = scale * (output + b2_ref[...] - rad_ref[m, :].astype(jnp.float32))
        alive = lax.broadcasted_iota(jnp.int32, (ROWS, 1), 0) + n * ROWS < count_ref[0]
        rad_ref[m, :] = jnp.where(alive, misfit, 0.0).astype(jnp.bfloat16)
    for i in range(hid // CHUNK):
        part = pl.ds(i * CHUNK, CHUNK)
        for m in blocks:
            back = lax.dot_general(
                rad_ref[m, :], w2_ref[part, :], NT, preferred_element_type=jnp.float32
            )
            hidden_ref[m, part] = (back * factor_ref[m, part]).astype(jnp.bfloat16)
    for m in blocks:
        grads = lax.dot_general(
            w1_ref[...], hidden_ref[m, :], NT, preferred_element_type=jnp.float32
        )
        grads_ref[:, m] = grads.astype(jnp.bfloat16)
    wide = ROWS // pool
    for n in range(inner // wide):
        placed = lax.dot_general(
            placing[n * ROWS : (n + 1) * ROWS],
            grads_ref[...],
            NT,
            preferred_element_type=jnp.float32,
        ).astype(jnp.bfloat16)
        some = pl.ds(n * wide, wide)
        for k in range(parts):
            out_ref[some, k * pool : (k + 1) * pool, :] = placed[
                :, k * LANES : (k + 1) * LANES
            ].reshape(wide, pool, LANES)


def blocks_kernel(tiles, most, me_ref, got_ref, own_ref, other_ref):
    inner = got_ref.shape[0]
    outer = tiles // inner
    pool = outer * most
    group = LANES // pool
    parts = own_ref.shape[1] // LANES
    marks = got_ref[:, parts * pool :, :].astype(jnp.float32)[:, 0, :]
    index = lax.broadcasted_iota(jnp.int32, (outer * COL_DEV, LANES), 0)
    lane = lax.broadcasted_iota(jnp.int32, (1, LANES), 1) & (pool - 1)
    turn = lax.shift_right_arithmetic(lane, most.bit_length() - 1) ^ (
        lax.shift_right_arithmetic(me_ref[0], inner.bit_length() - 1)
    )
    chosen = []
    for g in range(inner // group):
        label = jnp.sum(marks[g * group : (g + 1) * group], axis=0, keepdims=True)
        label = label.astype(jnp.int32)
        code = jnp.where(label > 0, turn * COL_DEV + label - 1, -1)
        chosen.append(as_bf16(index == code))
    chosen = jnp.concatenate(chosen, axis=1)
    for k in range(parts):
        block = got_ref[:, k * pool : (k + 1) * pool, :].reshape(inner * pool, LANES)
        total = jnp.dot(chosen, block, preferred_element_type=jnp.float32)
        own_ref[:, k * LANES : (k + 1) * LANES] = total[:COL_DEV]
        other_ref[:, k * LANES : (k + 1) * LANES] = total[COL_DEV:].astype(jnp.bfloat16)


def per_device(
    profiles,
    radiances,
    inner_weight,
    inner_bias,
    outer_weight,
    outer_bias,
    channel_weight,
    counts,
    owner,
    column,
):
    tiles = lax.axis_size("tile")
    rows, width = profiles.shape
    hid = inner_weight.shape[1]
    chan = radiances.shape[1]
    most = max(2, 2 * rows // tiles)
    inner = tiles // OUTER
    pool = OUTER * most
    high = width // LANES * pool + LABEL_ROWS
    me = lax.axis_index("tile").astype(jnp.int32).reshape(1)
    vmem = pl.BlockSpec(memory_space=pltpu.VMEM)
    smem = pl.BlockSpec(memory_space=pltpu.SMEM)
    anywhere = pl.BlockSpec(memory_space=pl.ANY)
    bucket = pl.pallas_call(
        functools.partial(rows_kernel, tiles, most),
        out_shape=jax.ShapeDtypeStruct((inner, high, LANES), jnp.bfloat16),
        in_specs=[smem, smem] + [anywhere] * 9,
        out_specs=vmem,
        scratch_shapes=[
            pltpu.VMEM((1, rows), jnp.int32),
            pltpu.VMEM((1, rows), jnp.int32),
            pltpu.VMEM((rows, width), jnp.bfloat16),
            pltpu.VMEM((rows, chan), jnp.bfloat16),
            pltpu.VMEM((width, hid), jnp.bfloat16),
            pltpu.VMEM((1, hid), jnp.float32),
            pltpu.VMEM((hid, chan), jnp.bfloat16),
            pltpu.VMEM((1, chan), jnp.float32),
            pltpu.VMEM((1, chan), jnp.float32),
            pltpu.VMEM((rows, hid), jnp.bfloat16),
            pltpu.VMEM((rows, hid), jnp.float32),
            pltpu.VMEM((width, rows), jnp.bfloat16),
            pltpu.SemaphoreType.DMA((10,)),
        ],
        compiler_params=pltpu.CompilerParams(vmem_limit_bytes=40 * 1024 * 1024),
        name="rows_kernel",
    )(
        me,
        counts,
        *[
            pltpu.with_memory_space_constraint(operand, pltpu.HBM)
            for operand in (
                owner.reshape(1, rows),
                column.reshape(1, rows),
                profiles,
                radiances,
                inner_weight,
                inner_bias.reshape(1, hid),
                outer_weight,
                outer_bias.reshape(1, chan),
                channel_weight.reshape(1, chan),
            )
        ],
    )
    halves = [[o * inner + i for i in range(inner)] for o in range(OUTER)]
    got = lax.all_to_all(
        bucket, "tile", split_axis=0, concat_axis=0, axis_index_groups=halves, tiled=True
    )
    own, other = pl.pallas_call(
        functools.partial(blocks_kernel, tiles, most),
        out_shape=[
            jax.ShapeDtypeStruct((COL_DEV, width), jnp.float32),
            jax.ShapeDtypeStruct((COL_DEV, width), jnp.bfloat16),
        ],
        in_specs=[smem, vmem],
        out_specs=[vmem, vmem],
        compiler_params=pltpu.CompilerParams(vmem_limit_bytes=24 * 1024 * 1024),
        name="blocks_kernel",
    )(me, got)
    pairs = [(t, (t + inner) % tiles) for t in range(tiles)]
    return own + lax.ppermute(other, "tile", pairs).astype(jnp.float32)


def solution(mesh):
    placed = (
        P(("group", "tile"), None),
        P(("group", "tile"), None),
        P(),
        P(),
        P(),
        P(),
        P(),
        P(("group", "tile")),
        P(("group", "tile"), None),
        P(("group", "tile")),
    )
    return jax.shard_map(
        per_device,
        mesh=mesh,
        in_specs=placed,
        out_specs=P(("group", "tile"), None),
        check_vma=False,
    )
```

```python
import functools

import jax
import jax.numpy as jnp
from jax import lax
from jax.experimental import pallas as pl
from jax.experimental.pallas import tpu as pltpu
from jax.sharding import PartitionSpec as P

COL_DEV = 128
CHUNK = 256
LANES = 128
LABEL_ROWS = 8
OUTER = 2
ROWS = 256
NT = (((1,), (1,)), ((), ()))


def as_bf16(mask):
    return mask.astype(jnp.float32).astype(jnp.bfloat16)


def rows_kernel(
    tiles,
    most,
    me_ref,
    count_ref,
    owner_hbm,
    column_hbm,
    prof_hbm,
    rad_hbm,
    w1_hbm,
    b1_hbm,
    w2_hbm,
    b2_hbm,
    cw_hbm,
    out_ref,
    owner_ref,
    column_ref,
    prof_ref,
    rad_ref,
    w1_ref,
    b1_ref,
    w2_ref,
    b2_ref,
    cw_ref,
    hidden_ref,
    factor_ref,
    grads_ref,
    sems,
):
    rows, width = prof_ref.shape
    hid = w1_ref.shape[1]
    chan = rad_ref.shape[1]
    starts = [0, hid // 4, hid]
    pieces = [pl.ds(lo, hi - lo) for lo, hi in zip(starts[:-1], starts[1:])]
    pairs = (
        [(prof_hbm, prof_ref), (b1_hbm, b1_ref)]
        + [(w1_hbm.at[:, piece], w1_ref.at[:, piece]) for piece in pieces]
        + [(w2_hbm, w2_ref), (rad_hbm, rad_ref), (b2_hbm, b2_ref), (cw_hbm, cw_ref)]
        + [(owner_hbm, owner_ref), (column_hbm, column_ref)]
    )
    copies = [
        pltpu.make_async_copy(src, dst, sems.at[i]) for i, (src, dst) in enumerate(pairs)
    ]
    for copy in copies:
        copy.start()

    upper = as_bf16(
        lax.broadcasted_iota(jnp.int32, (rows, rows), 0)
        <= lax.broadcasted_iota(jnp.int32, (rows, rows), 1)
    )
    copies[0].wait()
    copies[1].wait()
    prof_ref[...] = (prof_ref[...].astype(jnp.float32) * 0.5).astype(jnp.bfloat16)
    blocks = [pl.ds(i, ROWS) for i in range(0, rows, ROWS)]
    for i in range(hid // CHUNK):
        part = pl.ds(i * CHUNK, CHUNK)
        if i * CHUNK in starts:
            copies[2 + starts.index(i * CHUNK)].wait()
        if i * CHUNK == hid * 7 // 8:
            for copy in copies[2 + len(pieces) :]:
                copy.wait()
        for m in blocks:
            u = jnp.dot(prof_ref[m, :], w1_ref[:, part], preferred_element_type=jnp.float32)
            u = u + 0.5 * b1_ref[:, part]
            p = jnp.tanh(u) + 1.0
            hidden = u * p
            hidden_ref[m, part] = hidden.astype(jnp.bfloat16)
            factor_ref[m, part] = p + hidden * (2.0 - p)
    inner = out_ref.shape[0]
    live = lax.broadcasted_iota(jnp.int32, (1, rows), 1) < count_ref[0]
    owner = jnp.where(live, owner_ref[...], -1)
    mine = lax.broadcasted_iota(jnp.int32, (tiles, rows), 0) == owner
    one_hot = mine.astype(jnp.float32)
    running = jnp.dot(one_hot.astype(jnp.bfloat16), upper, preferred_element_type=jnp.float32)
    rank = jnp.sum(running * one_hot, axis=0, keepdims=True).astype(jnp.int32) - 1
    pool = tiles // inner * most
    place = owner & (inner - 1)
    order = lax.shift_right_arithmetic(owner, inner.bit_length() - 1) * most + rank
    slot = jnp.where(live, place * pool + order, -1)
    placing = as_bf16(lax.broadcasted_iota(jnp.int32, (inner * pool, rows), 0) == slot)
    lane = order + lax.rem(me_ref[0], LANES // pool) * pool
    lane_hot = as_bf16(lax.broadcasted_iota(jnp.int32, (LANES, rows), 0) == lane)
    here = live & (lax.broadcasted_iota(jnp.int32, (inner, rows), 0) == place)
    marked = jnp.where(here, (column_ref[...] + 1).astype(jnp.float32), 0.0)
    labels = lax.dot_general(
        marked.astype(jnp.bfloat16), lane_hot, NT, preferred_element_type=jnp.float32
    )

    parts = width // LANES
    out_ref[:, parts * pool :, :] = jnp.broadcast_to(
        labels.reshape(inner, 1, LANES), (inner, LABEL_ROWS, LANES)
    ).astype(jnp.bfloat16)

    scale = 0.5 * cw_ref[...]
    for n, m in enumerate(blocks):
        output = jnp.dot(hidden_ref[m, :], w2_ref[...], preferred_element_type=jnp.float32)
        misfit = scale * (output + b2_ref[...] - rad_ref[m, :].astype(jnp.float32))
        alive = lax.broadcasted_iota(jnp.int32, (ROWS, 1), 0) + n * ROWS < count_ref[0]
        rad_ref[m, :] = jnp.where(alive, misfit, 0.0).astype(jnp.bfloat16)
    for i in range(hid // CHUNK):
        part = pl.ds(i * CHUNK, CHUNK)
        for m in blocks:
            back = lax.dot_general(
                rad_ref[m, :], w2_ref[part, :], NT, preferred_element_type=jnp.float32
            )
            hidden_ref[m, part] = (back * factor_ref[m, part]).astype(jnp.bfloat16)
    for m in blocks:
        grads = lax.dot_general(
            w1_ref[...], hidden_ref[m, :], NT, preferred_element_type=jnp.float32
        )
        grads_ref[:, m] = grads.astype(jnp.bfloat16)
    wide = ROWS // pool
    for n in range(inner // wide):
        placed = lax.dot_general(
            placing[n * ROWS : (n + 1) * ROWS],
            grads_ref[...],
            NT,
            preferred_element_type=jnp.float32,
        ).astype(jnp.bfloat16)
        some = pl.ds(n * wide, wide)
        for k in range(parts):
            out_ref[some, k * pool : (k + 1) * pool, :] = placed[
                :, k * LANES : (k + 1) * LANES
            ].reshape(wide, pool, LANES)


def blocks_kernel(tiles, most, me_ref, got_ref, own_ref, other_ref):
    inner = got_ref.shape[0]
    outer = tiles // inner
    pool = outer * most
    group = LANES // pool
    parts = own_ref.shape[1] // LANES
    marks = got_ref[:, parts * pool :, :].astype(jnp.float32)[:, 0, :]
    index = lax.broadcasted_iota(jnp.int32, (outer * COL_DEV, LANES), 0)
    lane = lax.broadcasted_iota(jnp.int32, (1, LANES), 1) & (pool - 1)
    turn = lax.shift_right_arithmetic(lane, most.bit_length() - 1) ^ (
        lax.shift_right_arithmetic(me_ref[0], inner.bit_length() - 1)
    )
    chosen = []
    for g in range(inner // group):
        label = jnp.sum(marks[g * group : (g + 1) * group], axis=0, keepdims=True)
        label = label.astype(jnp.int32)
        code = jnp.where(label > 0, turn * COL_DEV + label - 1, -1)
        chosen.append(as_bf16(index == code))
    chosen = jnp.concatenate(chosen, axis=1)
    for k in range(parts):
        block = got_ref[:, k * pool : (k + 1) * pool, :].reshape(inner * pool, LANES)
        total = jnp.dot(chosen, block, preferred_element_type=jnp.float32)
        own_ref[:, k * LANES : (k + 1) * LANES] = total[:COL_DEV]
        other_ref[:, k * LANES : (k + 1) * LANES] = total[COL_DEV:].astype(jnp.bfloat16)


def per_device(
    profiles,
    radiances,
    inner_weight,
    inner_bias,
    outer_weight,
    outer_bias,
    channel_weight,
    counts,
    owner,
    column,
):
    tiles = lax.axis_size("tile")
    rows, width = profiles.shape
    hid = inner_weight.shape[1]
    chan = radiances.shape[1]
    most = max(2, 2 * rows // tiles)
    inner = tiles // OUTER
    pool = OUTER * most
    high = width // LANES * pool + LABEL_ROWS
    me = lax.axis_index("tile").astype(jnp.int32).reshape(1)
    vmem = pl.BlockSpec(memory_space=pltpu.VMEM)
    smem = pl.BlockSpec(memory_space=pltpu.SMEM)
    anywhere = pl.BlockSpec(memory_space=pl.ANY)
    bucket = pl.pallas_call(
        functools.partial(rows_kernel, tiles, most),
        out_shape=jax.ShapeDtypeStruct((inner, high, LANES), jnp.bfloat16),
        in_specs=[smem, smem] + [anywhere] * 9,
        out_specs=vmem,
        scratch_shapes=[
            pltpu.VMEM((1, rows), jnp.int32),
            pltpu.VMEM((1, rows), jnp.int32),
            pltpu.VMEM((rows, width), jnp.bfloat16),
            pltpu.VMEM((rows, chan), jnp.bfloat16),
            pltpu.VMEM((width, hid), jnp.bfloat16),
            pltpu.VMEM((1, hid), jnp.float32),
            pltpu.VMEM((hid, chan), jnp.bfloat16),
            pltpu.VMEM((1, chan), jnp.float32),
            pltpu.VMEM((1, chan), jnp.float32),
            pltpu.VMEM((rows, hid), jnp.bfloat16),
            pltpu.VMEM((rows, hid), jnp.float32),
            pltpu.VMEM((width, rows), jnp.bfloat16),
            pltpu.SemaphoreType.DMA((10,)),
        ],
        compiler_params=pltpu.CompilerParams(vmem_limit_bytes=40 * 1024 * 1024),
        name="rows_kernel",
    )(
        me,
        counts,
        *[
            pltpu.with_memory_space_constraint(operand, pltpu.HBM)
            for operand in (
                owner.reshape(1, rows),
                column.reshape(1, rows),
                profiles,
                radiances,
                inner_weight,
                inner_bias.reshape(1, hid),
                outer_weight,
                outer_bias.reshape(1, chan),
                channel_weight.reshape(1, chan),
            )
        ],
    )
    halves = [[o * inner + i for i in range(inner)] for o in range(OUTER)]
    got = lax.all_to_all(
        bucket, "tile", split_axis=0, concat_axis=0, axis_index_groups=halves, tiled=True
    )
    own, other = pl.pallas_call(
        functools.partial(blocks_kernel, tiles, most),
        out_shape=[
            jax.ShapeDtypeStruct((COL_DEV, width), jnp.float32),
            jax.ShapeDtypeStruct((COL_DEV, width), jnp.bfloat16),
        ],
        in_specs=[smem, vmem],
        out_specs=[vmem, vmem],
        compiler_params=pltpu.CompilerParams(vmem_limit_bytes=24 * 1024 * 1024),
        name="blocks_kernel",
    )(me, got)
    pairs = [(t, (t + inner) % tiles) for t in range(tiles)]
    return own + lax.ppermute(other, "tile", pairs).astype(jnp.float32)


def solution(mesh):
    placed = (
        P(("group", "tile"), None),
        P(("group", "tile"), None),
        P(),
        P(),
        P(),
        P(),
        P(),
        P(("group", "tile")),
        P(("group", "tile"), None),
        P(("group", "tile")),
    )
    return jax.shard_map(
        per_device,
        mesh=mesh,
        in_specs=placed,
        out_specs=P(("group", "tile"), None),
        check_vma=False,
    )
```

```python
import functools

import jax
import jax.numpy as jnp
from jax import lax
from jax.experimental import pallas as pl
from jax.experimental.pallas import tpu as pltpu
from jax.sharding import PartitionSpec as P

COL_DEV = 128
CHUNK = 256
LANES = 128
LABEL_ROWS = 8
OUTER = 2
ROWS = 256
NT = (((1,), (1,)), ((), ()))


def as_bf16(mask):
    return mask.astype(jnp.float32).astype(jnp.bfloat16)


def rows_kernel(
    tiles,
    most,
    me_ref,
    count_ref,
    owner_hbm,
    column_hbm,
    prof_hbm,
    rad_hbm,
    w1_hbm,
    b1_hbm,
    w2_hbm,
    b2_hbm,
    cw_hbm,
    out_ref,
    owner_ref,
    column_ref,
    prof_ref,
    rad_ref,
    w1_ref,
    b1_ref,
    w2_ref,
    b2_ref,
    cw_ref,
    hidden_ref,
    factor_ref,
    grads_ref,
    half_ref,
    sems,
):
    rows, width = prof_ref.shape
    depth, hid = w1_ref.shape
    chan = rad_ref.shape[1]
    starts = [0, hid // 4, hid]
    pieces = [pl.ds(lo, hi - lo) for lo, hi in zip(starts[:-1], starts[1:])]
    pairs = (
        [(prof_hbm, prof_ref), (b1_hbm, b1_ref)]
        + [(w1_hbm.at[:, piece], w1_ref.at[pl.ds(0, width), piece]) for piece in pieces]
        + [(w2_hbm, w2_ref), (rad_hbm, rad_ref), (b2_hbm, b2_ref), (cw_hbm, cw_ref)]
        + [(owner_hbm, owner_ref), (column_hbm, column_ref)]
    )
    copies = [
        pltpu.make_async_copy(src, dst, sems.at[i]) for i, (src, dst) in enumerate(pairs)
    ]
    for copy in copies:
        copy.start()

    upper = as_bf16(
        lax.broadcasted_iota(jnp.int32, (rows, rows), 0)
        <= lax.broadcasted_iota(jnp.int32, (rows, rows), 1)
    )
    ones = lax.broadcasted_iota(jnp.int32, (rows, depth - width), 1) < 3
    half_ref[:, width:] = as_bf16(ones)
    w1_ref[width + 16 :, :] = jnp.zeros((depth - width - 16, hid), jnp.bfloat16)
    copies[0].wait()
    copies[1].wait()
    half_ref[:, :width] = (prof_ref[...].astype(jnp.float32) * 0.5).astype(jnp.bfloat16)
    bias = 0.5 * b1_ref[...]
    high = bias.astype(jnp.bfloat16).astype(jnp.float32)
    low = (bias - high).astype(jnp.bfloat16).astype(jnp.float32)
    line = lax.broadcasted_iota(jnp.int32, (16, hid), 0)
    terms = jnp.where(line == 0, high, jnp.where(line == 1, low, bias - high - low))
    w1_ref[width : width + 16, :] = jnp.where(line < 3, terms, 0.0).astype(jnp.bfloat16)
    blocks = [pl.ds(i, ROWS) for i in range(0, rows, ROWS)]
    for i in range(hid // CHUNK):
        part = pl.ds(i * CHUNK, CHUNK)
        if i * CHUNK in starts:
            copies[2 + starts.index(i * CHUNK)].wait()
        if i * CHUNK == hid * 7 // 8:
            for copy in copies[2 + len(pieces) :]:
                copy.wait()
        for m in blocks:
            u = jnp.dot(half_ref[m, :], w1_ref[:, part], preferred_element_type=jnp.float32)
            p = jnp.tanh(u) + 1.0
            hidden = u * p
            hidden_ref[m, part] = hidden.astype(jnp.bfloat16)
            factor_ref[m, part] = p + hidden * (2.0 - p)
    inner = out_ref.shape[0]
    live = lax.broadcasted_iota(jnp.int32, (1, rows), 1) < count_ref[0]
    owner = jnp.where(live, owner_ref[...], -1)
    mine = lax.broadcasted_iota(jnp.int32, (tiles, rows), 0) == owner
    one_hot = mine.astype(jnp.float32)
    running = jnp.dot(one_hot.astype(jnp.bfloat16), upper, preferred_element_type=jnp.float32)
    rank = jnp.sum(running * one_hot, axis=0, keepdims=True).astype(jnp.int32) - 1
    pool = tiles // inner * most
    place = owner & (inner - 1)
    order = lax.shift_right_arithmetic(owner, inner.bit_length() - 1) * most + rank
    slot = jnp.where(live, place * pool + order, -1)
    placing = as_bf16(lax.broadcasted_iota(jnp.int32, (inner * pool, rows), 0) == slot)
    lane = order + lax.rem(me_ref[0], LANES // pool) * pool
    lane_hot = as_bf16(lax.broadcasted_iota(jnp.int32, (LANES, rows), 0) == lane)
    here = live & (lax.broadcasted_iota(jnp.int32, (inner, rows), 0) == place)
    marked = jnp.where(here, (column_ref[...] + 1).astype(jnp.float32), 0.0)
    labels = lax.dot_general(
        marked.astype(jnp.bfloat16), lane_hot, NT, preferred_element_type=jnp.float32
    )

    parts = width // LANES
    out_ref[:, parts * pool :, :] = jnp.broadcast_to(
        labels.reshape(inner, 1, LANES), (inner, LABEL_ROWS, LANES)
    ).astype(jnp.bfloat16)

    scale = 0.5 * cw_ref[...]
    for n, m in enumerate(blocks):
        output = jnp.dot(hidden_ref[m, :], w2_ref[...], preferred_element_type=jnp.float32)
        misfit = scale * (output + b2_ref[...] - rad_ref[m, :].astype(jnp.float32))
        alive = lax.broadcasted_iota(jnp.int32, (ROWS, 1), 0) + n * ROWS < count_ref[0]
        rad_ref[m, :] = jnp.where(alive, misfit, 0.0).astype(jnp.bfloat16)
    for i in range(hid // CHUNK):
        part = pl.ds(i * CHUNK, CHUNK)
        for m in blocks:
            back = lax.dot_general(
                rad_ref[m, :], w2_ref[part, :], NT, preferred_element_type=jnp.float32
            )
            hidden_ref[m, part] = (back * factor_ref[m, part]).astype(jnp.bfloat16)
    for m in blocks:
        grads = lax.dot_general(
            w1_ref[:width, :], hidden_ref[m, :], NT, preferred_element_type=jnp.float32
        )
        grads_ref[:, m] = grads.astype(jnp.bfloat16)
    wide = ROWS // pool
    for n in range(inner // wide):
        placed = lax.dot_general(
            placing[n * ROWS : (n + 1) * ROWS],
            grads_ref[...],
            NT,
            preferred_element_type=jnp.float32,
        ).astype(jnp.bfloat16)
        some = pl.ds(n * wide, wide)
        for k in range(parts):
            out_ref[some, k * pool : (k + 1) * pool, :] = placed[
                :, k * LANES : (k + 1) * LANES
            ].reshape(wide, pool, LANES)


def blocks_kernel(tiles, most, me_ref, got_ref, own_ref, other_ref):
    inner = got_ref.shape[0]
    outer = tiles // inner
    pool = outer * most
    group = LANES // pool
    parts = own_ref.shape[1] // LANES
    marks = got_ref[:, parts * pool :, :].astype(jnp.float32)[:, 0, :]
    index = lax.broadcasted_iota(jnp.int32, (outer * COL_DEV, LANES), 0)
    lane = lax.broadcasted_iota(jnp.int32, (1, LANES), 1) & (pool - 1)
    turn = lax.shift_right_arithmetic(lane, most.bit_length() - 1) ^ (
        lax.shift_right_arithmetic(me_ref[0], inner.bit_length() - 1)
    )
    chosen = []
    for g in range(inner // group):
        label = jnp.sum(marks[g * group : (g + 1) * group], axis=0, keepdims=True)
        label = label.astype(jnp.int32)
        code = jnp.where(label > 0, turn * COL_DEV + label - 1, -1)
        chosen.append(as_bf16(index == code))
    chosen = jnp.concatenate(chosen, axis=1)
    for k in range(parts):
        block = got_ref[:, k * pool : (k + 1) * pool, :].reshape(inner * pool, LANES)
        total = jnp.dot(chosen, block, preferred_element_type=jnp.float32)
        own_ref[:, k * LANES : (k + 1) * LANES] = total[:COL_DEV]
        other_ref[:, k * LANES : (k + 1) * LANES] = total[COL_DEV:].astype(jnp.bfloat16)


def per_device(
    profiles,
    radiances,
    inner_weight,
    inner_bias,
    outer_weight,
    outer_bias,
    channel_weight,
    counts,
    owner,
    column,
):
    tiles = lax.axis_size("tile")
    rows, width = profiles.shape
    hid = inner_weight.shape[1]
    chan = radiances.shape[1]
    most = max(2, 2 * rows // tiles)
    depth = width + LANES
    inner = tiles // OUTER
    pool = OUTER * most
    high = width // LANES * pool + LABEL_ROWS
    me = lax.axis_index("tile").astype(jnp.int32).reshape(1)
    vmem = pl.BlockSpec(memory_space=pltpu.VMEM)
    smem = pl.BlockSpec(memory_space=pltpu.SMEM)
    anywhere = pl.BlockSpec(memory_space=pl.ANY)
    bucket = pl.pallas_call(
        functools.partial(rows_kernel, tiles, most),
        out_shape=jax.ShapeDtypeStruct((inner, high, LANES), jnp.bfloat16),
        in_specs=[smem, smem] + [anywhere] * 9,
        out_specs=vmem,
        scratch_shapes=[
            pltpu.VMEM((1, rows), jnp.int32),
            pltpu.VMEM((1, rows), jnp.int32),
            pltpu.VMEM((rows, width), jnp.bfloat16),
            pltpu.VMEM((rows, chan), jnp.bfloat16),
            pltpu.VMEM((depth, hid), jnp.bfloat16),
            pltpu.VMEM((1, hid), jnp.float32),
            pltpu.VMEM((hid, chan), jnp.bfloat16),
            pltpu.VMEM((1, chan), jnp.float32),
            pltpu.VMEM((1, chan), jnp.float32),
            pltpu.VMEM((rows, hid), jnp.bfloat16),
            pltpu.VMEM((rows, hid), jnp.float32),
            pltpu.VMEM((width, rows), jnp.bfloat16),
            pltpu.VMEM((rows, depth), jnp.bfloat16),
            pltpu.SemaphoreType.DMA((10,)),
        ],
        compiler_params=pltpu.CompilerParams(vmem_limit_bytes=40 * 1024 * 1024),
        name="rows_kernel",
    )(
        me,
        counts,
        *[
            pltpu.with_memory_space_constraint(operand, pltpu.HBM)
            for operand in (
                owner.reshape(1, rows),
                column.reshape(1, rows),
                profiles,
                radiances,
                inner_weight,
                inner_bias.reshape(1, hid),
                outer_weight,
                outer_bias.reshape(1, chan),
                channel_weight.reshape(1, chan),
            )
        ],
    )
    halves = [[o * inner + i for i in range(inner)] for o in range(OUTER)]
    got = lax.all_to_all(
        bucket, "tile", split_axis=0, concat_axis=0, axis_index_groups=halves, tiled=True
    )
    own, other = pl.pallas_call(
        functools.partial(blocks_kernel, tiles, most),
        out_shape=[
            jax.ShapeDtypeStruct((COL_DEV, width), jnp.float32),
            jax.ShapeDtypeStruct((COL_DEV, width), jnp.bfloat16),
        ],
        in_specs=[smem, vmem],
        out_specs=[vmem, vmem],
        compiler_params=pltpu.CompilerParams(vmem_limit_bytes=24 * 1024 * 1024),
        name="blocks_kernel",
    )(me, got)
    pairs = [(t, (t + inner) % tiles) for t in range(tiles)]
    return own + lax.ppermute(other, "tile", pairs).astype(jnp.float32)


def solution(mesh):
    placed = (
        P(("group", "tile"), None),
        P(("group", "tile"), None),
        P(),
        P(),
        P(),
        P(),
        P(),
        P(("group", "tile")),
        P(("group", "tile"), None),
        P(("group", "tile")),
    )
    return jax.shard_map(
        per_device,
        mesh=mesh,
        in_specs=placed,
        out_specs=P(("group", "tile"), None),
        check_vma=False,
    )
```

```python
import functools

import jax
import jax.numpy as jnp
from jax import lax
from jax.experimental import pallas as pl
from jax.experimental.pallas import tpu as pltpu
from jax.sharding import PartitionSpec as P

COL_DEV = 128
CHUNK = 256
LANES = 128
LABEL_ROWS = 8
OUTER = 2
ROWS = 256
NT = (((1,), (1,)), ((), ()))


def as_bf16(mask):
    return mask.astype(jnp.float32).astype(jnp.bfloat16)


def reversed_bits(value, count):
    bits = count.bit_length() - 1
    total = 0
    for i in range(bits):
        total = total | (((value >> i) & 1) << (bits - 1 - i))
    return total


def rows_kernel(
    tiles,
    most,
    me_ref,
    count_ref,
    owner_hbm,
    column_hbm,
    prof_hbm,
    rad_hbm,
    w1_hbm,
    b1_hbm,
    w2_hbm,
    b2_hbm,
    cw_hbm,
    out_ref,
    owner_ref,
    column_ref,
    prof_ref,
    rad_ref,
    w1_ref,
    b1_ref,
    w2_ref,
    b2_ref,
    cw_ref,
    hidden_ref,
    factor_ref,
    grads_ref,
    sems,
):
    rows, width = prof_ref.shape
    hid = w1_ref.shape[1]
    chan = rad_ref.shape[1]
    starts = [0, hid // 4, hid]
    pieces = [pl.ds(lo, hi - lo) for lo, hi in zip(starts[:-1], starts[1:])]
    pairs = (
        [(prof_hbm, prof_ref), (b1_hbm, b1_ref)]
        + [(w1_hbm.at[:, piece], w1_ref.at[:, piece]) for piece in pieces]
        + [(w2_hbm, w2_ref), (rad_hbm, rad_ref), (b2_hbm, b2_ref), (cw_hbm, cw_ref)]
        + [(owner_hbm, owner_ref), (column_hbm, column_ref)]
    )
    copies = [
        pltpu.make_async_copy(src, dst, sems.at[i]) for i, (src, dst) in enumerate(pairs)
    ]
    for copy in copies:
        copy.start()

    upper = as_bf16(
        lax.broadcasted_iota(jnp.int32, (rows, rows), 0)
        <= lax.broadcasted_iota(jnp.int32, (rows, rows), 1)
    )
    copies[0].wait()
    copies[1].wait()
    prof_ref[...] = (prof_ref[...].astype(jnp.float32) * 0.5).astype(jnp.bfloat16)
    blocks = [pl.ds(i, ROWS) for i in range(0, rows, ROWS)]
    for i in range(hid // CHUNK):
        part = pl.ds(i * CHUNK, CHUNK)
        if i * CHUNK in starts:
            copies[2 + starts.index(i * CHUNK)].wait()
        if i * CHUNK == hid * 7 // 8:
            for copy in copies[2 + len(pieces) :]:
                copy.wait()
        for m in blocks:
            u = jnp.dot(prof_ref[m, :], w1_ref[:, part], preferred_element_type=jnp.float32)
            u = u + 0.5 * b1_ref[:, part]
            p = jnp.tanh(u) + 1.0
            hidden = u * p
            hidden_ref[m, part] = hidden.astype(jnp.bfloat16)
            factor_ref[m, part] = p + hidden * (2.0 - p)
    inner = out_ref.shape[0]
    live = lax.broadcasted_iota(jnp.int32, (1, rows), 1) < count_ref[0]
    owner = jnp.where(live, owner_ref[...], -1)
    mine = lax.broadcasted_iota(jnp.int32, (tiles, rows), 0) == owner
    one_hot = mine.astype(jnp.float32)
    running = jnp.dot(one_hot.astype(jnp.bfloat16), upper, preferred_element_type=jnp.float32)
    rank = jnp.sum(running * one_hot, axis=0, keepdims=True).astype(jnp.int32) - 1
    pool = tiles // inner * most
    place = reversed_bits(owner, inner)
    order = lax.shift_right_arithmetic(owner, inner.bit_length() - 1) * most + rank
    slot = jnp.where(live, place * pool + order, -1)
    placing = as_bf16(lax.broadcasted_iota(jnp.int32, (inner * pool, rows), 0) == slot)
    mine_at = reversed_bits(me_ref[0], inner)
    lane = order + (mine_at & (LANES // pool - 1)) * pool
    lane_hot = as_bf16(lax.broadcasted_iota(jnp.int32, (LANES, rows), 0) == lane)
    here = live & (lax.broadcasted_iota(jnp.int32, (inner, rows), 0) == place)
    marked = jnp.where(here, (column_ref[...] + 1).astype(jnp.float32), 0.0)
    labels = lax.dot_general(
        marked.astype(jnp.bfloat16), lane_hot, NT, preferred_element_type=jnp.float32
    )

    parts = width // LANES
    out_ref[:, parts * pool :, :] = jnp.broadcast_to(
        labels.reshape(inner, 1, LANES), (inner, LABEL_ROWS, LANES)
    ).astype(jnp.bfloat16)

    scale = 0.5 * cw_ref[...]
    for n, m in enumerate(blocks):
        output = jnp.dot(hidden_ref[m, :], w2_ref[...], preferred_element_type=jnp.float32)
        misfit = scale * (output + b2_ref[...] - rad_ref[m, :].astype(jnp.float32))
        alive = lax.broadcasted_iota(jnp.int32, (ROWS, 1), 0) + n * ROWS < count_ref[0]
        rad_ref[m, :] = jnp.where(alive, misfit, 0.0).astype(jnp.bfloat16)
    for i in range(hid // CHUNK):
        part = pl.ds(i * CHUNK, CHUNK)
        for m in blocks:
            back = lax.dot_general(
                rad_ref[m, :], w2_ref[part, :], NT, preferred_element_type=jnp.float32
            )
            hidden_ref[m, part] = (back * factor_ref[m, part]).astype(jnp.bfloat16)
    for m in blocks:
        grads = lax.dot_general(
            w1_ref[...], hidden_ref[m, :], NT, preferred_element_type=jnp.float32
        )
        grads_ref[:, m] = grads.astype(jnp.bfloat16)
    wide = ROWS // pool
    for n in range(inner // wide):
        placed = lax.dot_general(
            placing[n * ROWS : (n + 1) * ROWS],
            grads_ref[...],
            NT,
            preferred_element_type=jnp.float32,
        ).astype(jnp.bfloat16)
        some = pl.ds(n * wide, wide)
        for k in range(parts):
            out_ref[some, k * pool : (k + 1) * pool, :] = placed[
                :, k * LANES : (k + 1) * LANES
            ].reshape(wide, pool, LANES)


def blocks_kernel(tiles, most, me_ref, got_ref, own_ref, other_ref):
    inner = got_ref.shape[0]
    outer = tiles // inner
    pool = outer * most
    group = LANES // pool
    parts = own_ref.shape[1] // LANES
    marks = got_ref[:, parts * pool :, :].astype(jnp.float32)[:, 0, :]
    index = lax.broadcasted_iota(jnp.int32, (outer * COL_DEV, LANES), 0)
    lane = lax.broadcasted_iota(jnp.int32, (1, LANES), 1) & (pool - 1)
    turn = lax.shift_right_arithmetic(lane, most.bit_length() - 1) ^ (
        lax.shift_right_arithmetic(me_ref[0], inner.bit_length() - 1)
    )
    chosen = []
    for g in range(inner // group):
        label = jnp.sum(marks[g * group : (g + 1) * group], axis=0, keepdims=True)
        label = label.astype(jnp.int32)
        code = jnp.where(label > 0, turn * COL_DEV + label - 1, -1)
        chosen.append(as_bf16(index == code))
    chosen = jnp.concatenate(chosen, axis=1)
    block = jnp.concatenate(
        [
            got_ref[:, k * pool : (k + 1) * pool, :].reshape(inner * pool, LANES)
            for k in range(parts)
        ],
        axis=1,
    )
    total = jnp.dot(chosen, block, preferred_element_type=jnp.float32)
    own_ref[...] = total[:COL_DEV]
    other_ref[...] = total[COL_DEV:].astype(jnp.bfloat16)


def per_device(
    profiles,
    radiances,
    inner_weight,
    inner_bias,
    outer_weight,
    outer_bias,
    channel_weight,
    counts,
    owner,
    column,
):
    tiles = lax.axis_size("tile")
    rows, width = profiles.shape
    hid = inner_weight.shape[1]
    chan = radiances.shape[1]
    most = max(2, 2 * rows // tiles)
    inner = tiles // OUTER
    pool = OUTER * most
    high = width // LANES * pool + LABEL_ROWS
    me = lax.axis_index("tile").astype(jnp.int32).reshape(1)
    vmem = pl.BlockSpec(memory_space=pltpu.VMEM)
    smem = pl.BlockSpec(memory_space=pltpu.SMEM)
    anywhere = pl.BlockSpec(memory_space=pl.ANY)
    bucket = pl.pallas_call(
        functools.partial(rows_kernel, tiles, most),
        out_shape=jax.ShapeDtypeStruct((inner, high, LANES), jnp.bfloat16),
        in_specs=[smem, smem] + [anywhere] * 9,
        out_specs=vmem,
        scratch_shapes=[
            pltpu.VMEM((1, rows), jnp.int32),
            pltpu.VMEM((1, rows), jnp.int32),
            pltpu.VMEM((rows, width), jnp.bfloat16),
            pltpu.VMEM((rows, chan), jnp.bfloat16),
            pltpu.VMEM((width, hid), jnp.bfloat16),
            pltpu.VMEM((1, hid), jnp.float32),
            pltpu.VMEM((hid, chan), jnp.bfloat16),
            pltpu.VMEM((1, chan), jnp.float32),
            pltpu.VMEM((1, chan), jnp.float32),
            pltpu.VMEM((rows, hid), jnp.bfloat16),
            pltpu.VMEM((rows, hid), jnp.float32),
            pltpu.VMEM((width, rows), jnp.bfloat16),
            pltpu.SemaphoreType.DMA((10,)),
        ],
        compiler_params=pltpu.CompilerParams(vmem_limit_bytes=40 * 1024 * 1024),
        name="rows_kernel",
    )(
        me,
        counts,
        *[
            pltpu.with_memory_space_constraint(operand, pltpu.HBM)
            for operand in (
                owner.reshape(1, rows),
                column.reshape(1, rows),
                profiles,
                radiances,
                inner_weight,
                inner_bias.reshape(1, hid),
                outer_weight,
                outer_bias.reshape(1, chan),
                channel_weight.reshape(1, chan),
            )
        ],
    )
    halves = [
        [o * inner + reversed_bits(i, inner) for i in range(inner)] for o in range(OUTER)
    ]
    got = lax.all_to_all(
        bucket, "tile", split_axis=0, concat_axis=0, axis_index_groups=halves, tiled=True
    )
    own, other = pl.pallas_call(
        functools.partial(blocks_kernel, tiles, most),
        out_shape=[
            jax.ShapeDtypeStruct((COL_DEV, width), jnp.float32),
            jax.ShapeDtypeStruct((COL_DEV, width), jnp.bfloat16),
        ],
        in_specs=[smem, vmem],
        out_specs=[vmem, vmem],
        compiler_params=pltpu.CompilerParams(vmem_limit_bytes=24 * 1024 * 1024),
        name="blocks_kernel",
    )(me, got)
    pairs = [(t, (t + inner) % tiles) for t in range(tiles)]
    return own + lax.ppermute(other, "tile", pairs).astype(jnp.float32)


def solution(mesh):
    placed = (
        P(("group", "tile"), None),
        P(("group", "tile"), None),
        P(),
        P(),
        P(),
        P(),
        P(),
        P(("group", "tile")),
        P(("group", "tile"), None),
        P(("group", "tile")),
    )
    return jax.shard_map(
        per_device,
        mesh=mesh,
        in_specs=placed,
        out_specs=P(("group", "tile"), None),
        check_vma=False,
    )
```

```python
import functools

import jax
import jax.numpy as jnp
from jax import lax
from jax.experimental import pallas as pl
from jax.experimental.pallas import tpu as pltpu
from jax.sharding import PartitionSpec as P

COL_DEV = 128
CHUNK = 256
LANES = 128
LABEL_ROWS = 8
OUTER = 2
ROWS = 256
NT = (((1,), (1,)), ((), ()))


def as_bf16(mask):
    return mask.astype(jnp.float32).astype(jnp.bfloat16)


def reversed_bits(value, count):
    bits = count.bit_length() - 1
    total = 0
    for i in range(bits):
        total = total | (((value >> i) & 1) << (bits - 1 - i))
    return total


def rank_of(device, count):
    code = reversed_bits(device, count)
    rank, shift = code, 1
    while 1 << shift < count:
        rank = rank ^ (code >> shift)
        shift += 1
    return rank


def device_at(rank, count):
    return reversed_bits(rank ^ (rank >> 1), count)


def rows_kernel(
    tiles,
    most,
    me_ref,
    count_ref,
    owner_hbm,
    column_hbm,
    prof_hbm,
    rad_hbm,
    w1_hbm,
    b1_hbm,
    w2_hbm,
    b2_hbm,
    cw_hbm,
    out_ref,
    owner_ref,
    column_ref,
    prof_ref,
    rad_ref,
    w1_ref,
    b1_ref,
    w2_ref,
    b2_ref,
    cw_ref,
    hidden_ref,
    factor_ref,
    grads_ref,
    sems,
):
    rows, width = prof_ref.shape
    hid = w1_ref.shape[1]
    chan = rad_ref.shape[1]
    starts = [0, hid // 4, hid]
    pieces = [pl.ds(lo, hi - lo) for lo, hi in zip(starts[:-1], starts[1:])]
    pairs = (
        [(prof_hbm, prof_ref), (b1_hbm, b1_ref)]
        + [(w1_hbm.at[:, piece], w1_ref.at[:, piece]) for piece in pieces]
        + [(w2_hbm, w2_ref), (rad_hbm, rad_ref), (b2_hbm, b2_ref), (cw_hbm, cw_ref)]
        + [(owner_hbm, owner_ref), (column_hbm, column_ref)]
    )
    copies = [
        pltpu.make_async_copy(src, dst, sems.at[i]) for i, (src, dst) in enumerate(pairs)
    ]
    for copy in copies:
        copy.start()

    upper = as_bf16(
        lax.broadcasted_iota(jnp.int32, (rows, rows), 0)
        <= lax.broadcasted_iota(jnp.int32, (rows, rows), 1)
    )
    copies[0].wait()
    copies[1].wait()
    prof_ref[...] = (prof_ref[...].astype(jnp.float32) * 0.5).astype(jnp.bfloat16)
    blocks = [pl.ds(i, ROWS) for i in range(0, rows, ROWS)]
    for i in range(hid // CHUNK):
        part = pl.ds(i * CHUNK, CHUNK)
        if i * CHUNK in starts:
            copies[2 + starts.index(i * CHUNK)].wait()
        if i * CHUNK == hid * 7 // 8:
            for copy in copies[2 + len(pieces) :]:
                copy.wait()
        for m in blocks:
            u = jnp.dot(prof_ref[m, :], w1_ref[:, part], preferred_element_type=jnp.float32)
            u = u + 0.5 * b1_ref[:, part]
            p = jnp.tanh(u) + 1.0
            hidden = u * p
            hidden_ref[m, part] = hidden.astype(jnp.bfloat16)
            factor_ref[m, part] = p + hidden * (2.0 - p)
    inner = out_ref.shape[0]
    live = lax.broadcasted_iota(jnp.int32, (1, rows), 1) < count_ref[0]
    owner = jnp.where(live, owner_ref[...], -1)
    mine = lax.broadcasted_iota(jnp.int32, (tiles, rows), 0) == owner
    one_hot = mine.astype(jnp.float32)
    running = jnp.dot(one_hot.astype(jnp.bfloat16), upper, preferred_element_type=jnp.float32)
    rank = jnp.sum(running * one_hot, axis=0, keepdims=True).astype(jnp.int32) - 1
    pool = tiles // inner * most
    place = rank_of(owner, inner)
    order = lax.shift_right_arithmetic(owner, inner.bit_length() - 1) * most + rank
    slot = jnp.where(live, place * pool + order, -1)
    placing = as_bf16(lax.broadcasted_iota(jnp.int32, (inner * pool, rows), 0) == slot)
    mine_at = rank_of(me_ref[0], inner)
    lane = order + (mine_at & (LANES // pool - 1)) * pool
    lane_hot = as_bf16(lax.broadcasted_iota(jnp.int32, (LANES, rows), 0) == lane)
    here = live & (lax.broadcasted_iota(jnp.int32, (inner, rows), 0) == place)
    marked = jnp.where(here, (column_ref[...] + 1).astype(jnp.float32), 0.0)
    labels = lax.dot_general(
        marked.astype(jnp.bfloat16), lane_hot, NT, preferred_element_type=jnp.float32
    )

    parts = width // LANES
    out_ref[:, parts * pool :, :] = jnp.broadcast_to(
        labels.reshape(inner, 1, LANES), (inner, LABEL_ROWS, LANES)
    ).astype(jnp.bfloat16)

    scale = 0.5 * cw_ref[...]
    for n, m in enumerate(blocks):
        output = jnp.dot(hidden_ref[m, :], w2_ref[...], preferred_element_type=jnp.float32)
        misfit = scale * (output + b2_ref[...] - rad_ref[m, :].astype(jnp.float32))
        alive = lax.broadcasted_iota(jnp.int32, (ROWS, 1), 0) + n * ROWS < count_ref[0]
        rad_ref[m, :] = jnp.where(alive, misfit, 0.0).astype(jnp.bfloat16)
    for i in range(hid // CHUNK):
        part = pl.ds(i * CHUNK, CHUNK)
        for m in blocks:
            back = lax.dot_general(
                rad_ref[m, :], w2_ref[part, :], NT, preferred_element_type=jnp.float32
            )
            hidden_ref[m, part] = (back * factor_ref[m, part]).astype(jnp.bfloat16)
    for m in blocks:
        grads = lax.dot_general(
            w1_ref[...], hidden_ref[m, :], NT, preferred_element_type=jnp.float32
        )
        grads_ref[:, m] = grads.astype(jnp.bfloat16)
    wide = ROWS // pool
    for n in range(inner // wide):
        placed = lax.dot_general(
            placing[n * ROWS : (n + 1) * ROWS],
            grads_ref[...],
            NT,
            preferred_element_type=jnp.float32,
        ).astype(jnp.bfloat16)
        some = pl.ds(n * wide, wide)
        for k in range(parts):
            out_ref[some, k * pool : (k + 1) * pool, :] = placed[
                :, k * LANES : (k + 1) * LANES
            ].reshape(wide, pool, LANES)


def blocks_kernel(tiles, most, me_ref, got_ref, own_ref, other_ref):
    inner = got_ref.shape[0]
    outer = tiles // inner
    pool = outer * most
    group = LANES // pool
    parts = own_ref.shape[1] // LANES
    marks = got_ref[:, parts * pool :, :].astype(jnp.float32)[:, 0, :]
    index = lax.broadcasted_iota(jnp.int32, (outer * COL_DEV, LANES), 0)
    lane = lax.broadcasted_iota(jnp.int32, (1, LANES), 1) & (pool - 1)
    turn = lax.shift_right_arithmetic(lane, most.bit_length() - 1) ^ (
        lax.shift_right_arithmetic(me_ref[0], inner.bit_length() - 1)
    )
    chosen = []
    for g in range(inner // group):
        label = jnp.sum(marks[g * group : (g + 1) * group], axis=0, keepdims=True)
        label = label.astype(jnp.int32)
        code = jnp.where(label > 0, turn * COL_DEV + label - 1, -1)
        chosen.append(as_bf16(index == code))
    chosen = jnp.concatenate(chosen, axis=1)
    block = jnp.concatenate(
        [
            got_ref[:, k * pool : (k + 1) * pool, :].reshape(inner * pool, LANES)
            for k in range(parts)
        ],
        axis=1,
    )
    total = jnp.dot(chosen, block, preferred_element_type=jnp.float32)
    own_ref[...] = total[:COL_DEV]
    other_ref[...] = total[COL_DEV:].astype(jnp.bfloat16)


def per_device(
    profiles,
    radiances,
    inner_weight,
    inner_bias,
    outer_weight,
    outer_bias,
    channel_weight,
    counts,
    owner,
    column,
):
    tiles = lax.axis_size("tile")
    rows, width = profiles.shape
    hid = inner_weight.shape[1]
    chan = radiances.shape[1]
    most = max(2, 2 * rows // tiles)
    inner = tiles // OUTER
    pool = OUTER * most
    high = width // LANES * pool + LABEL_ROWS
    me = lax.axis_index("tile").astype(jnp.int32).reshape(1)
    vmem = pl.BlockSpec(memory_space=pltpu.VMEM)
    smem = pl.BlockSpec(memory_space=pltpu.SMEM)
    anywhere = pl.BlockSpec(memory_space=pl.ANY)
    bucket = pl.pallas_call(
        functools.partial(rows_kernel, tiles, most),
        out_shape=jax.ShapeDtypeStruct((inner, high, LANES), jnp.bfloat16),
        in_specs=[smem, smem] + [anywhere] * 9,
        out_specs=vmem,
        scratch_shapes=[
            pltpu.VMEM((1, rows), jnp.int32),
            pltpu.VMEM((1, rows), jnp.int32),
            pltpu.VMEM((rows, width), jnp.bfloat16),
            pltpu.VMEM((rows, chan), jnp.bfloat16),
            pltpu.VMEM((width, hid), jnp.bfloat16),
            pltpu.VMEM((1, hid), jnp.float32),
            pltpu.VMEM((hid, chan), jnp.bfloat16),
            pltpu.VMEM((1, chan), jnp.float32),
            pltpu.VMEM((1, chan), jnp.float32),
            pltpu.VMEM((rows, hid), jnp.bfloat16),
            pltpu.VMEM((rows, hid), jnp.float32),
            pltpu.VMEM((width, rows), jnp.bfloat16),
            pltpu.SemaphoreType.DMA((10,)),
        ],
        compiler_params=pltpu.CompilerParams(vmem_limit_bytes=40 * 1024 * 1024),
        name="rows_kernel",
    )(
        me,
        counts,
        *[
            pltpu.with_memory_space_constraint(operand, pltpu.HBM)
            for operand in (
                owner.reshape(1, rows),
                column.reshape(1, rows),
                profiles,
                radiances,
                inner_weight,
                inner_bias.reshape(1, hid),
                outer_weight,
                outer_bias.reshape(1, chan),
                channel_weight.reshape(1, chan),
            )
        ],
    )
    halves = [
        [o * inner + device_at(i, inner) for i in range(inner)] for o in range(OUTER)
    ]
    got = lax.all_to_all(
        bucket, "tile", split_axis=0, concat_axis=0, axis_index_groups=halves, tiled=True
    )
    own, other = pl.pallas_call(
        functools.partial(blocks_kernel, tiles, most),
        out_shape=[
            jax.ShapeDtypeStruct((COL_DEV, width), jnp.float32),
            jax.ShapeDtypeStruct((COL_DEV, width), jnp.bfloat16),
        ],
        in_specs=[smem, vmem],
        out_specs=[vmem, vmem],
        compiler_params=pltpu.CompilerParams(vmem_limit_bytes=24 * 1024 * 1024),
        name="blocks_kernel",
    )(me, got)
    pairs = [(t, (t + inner) % tiles) for t in range(tiles)]
    return own + lax.ppermute(other, "tile", pairs).astype(jnp.float32)


def solution(mesh):
    placed = (
        P(("group", "tile"), None),
        P(("group", "tile"), None),
        P(),
        P(),
        P(),
        P(),
        P(),
        P(("group", "tile")),
        P(("group", "tile"), None),
        P(("group", "tile")),
    )
    return jax.shard_map(
        per_device,
        mesh=mesh,
        in_specs=placed,
        out_specs=P(("group", "tile"), None),
        check_vma=False,
    )
```

```python
import functools

import jax
import jax.numpy as jnp
from jax import lax
from jax.experimental import pallas as pl
from jax.experimental.pallas import tpu as pltpu
from jax.sharding import PartitionSpec as P

COL_DEV = 128
CHUNK = 256
LANES = 128
LABEL_ROWS = 8
OUTER = 2
ROWS = 256
NT = (((1,), (1,)), ((), ()))


def as_bf16(mask):
    return mask.astype(jnp.float32).astype(jnp.bfloat16)


def reversed_bits(value, count):
    bits = count.bit_length() - 1
    total = 0
    for i in range(bits):
        total = total | (((value >> i) & 1) << (bits - 1 - i))
    return total


def rank_of(device, count):
    code = reversed_bits(device, count)
    rank, shift = code, 1
    while 1 << shift < count:
        rank = rank ^ (code >> shift)
        shift += 1
    return rank


def device_at(rank, count):
    return reversed_bits(rank ^ (rank >> 1), count)


def rows_kernel(
    tiles,
    most,
    me_ref,
    count_ref,
    owner_hbm,
    column_hbm,
    prof_hbm,
    rad_hbm,
    w1_hbm,
    b1_hbm,
    w2_hbm,
    b2_hbm,
    cw_hbm,
    out_ref,
    owner_ref,
    column_ref,
    prof_ref,
    rad_ref,
    w1_ref,
    b1_ref,
    w2_ref,
    b2_ref,
    cw_ref,
    hidden_ref,
    factor_ref,
    grads_ref,
    sems,
):
    rows, width = prof_ref.shape
    hid = w1_ref.shape[1]
    chan = rad_ref.shape[1]
    starts = [0, hid // 4, hid]
    pieces = [pl.ds(lo, hi - lo) for lo, hi in zip(starts[:-1], starts[1:])]
    pairs = (
        [(prof_hbm, prof_ref), (b1_hbm, b1_ref)]
        + [(w1_hbm.at[:, piece], w1_ref.at[:, piece]) for piece in pieces]
        + [(w2_hbm, w2_ref), (rad_hbm, rad_ref), (b2_hbm, b2_ref), (cw_hbm, cw_ref)]
        + [(owner_hbm, owner_ref), (column_hbm, column_ref)]
    )
    copies = [
        pltpu.make_async_copy(src, dst, sems.at[i]) for i, (src, dst) in enumerate(pairs)
    ]
    for copy in copies:
        copy.start()

    upper = as_bf16(
        lax.broadcasted_iota(jnp.int32, (rows, rows), 0)
        <= lax.broadcasted_iota(jnp.int32, (rows, rows), 1)
    )
    copies[0].wait()
    copies[1].wait()
    prof_ref[...] = (prof_ref[...].astype(jnp.float32) * 0.5).astype(jnp.bfloat16)
    blocks = [pl.ds(i, ROWS) for i in range(0, rows, ROWS)]
    for i in range(hid // CHUNK):
        part = pl.ds(i * CHUNK, CHUNK)
        if i * CHUNK in starts:
            copies[2 + starts.index(i * CHUNK)].wait()
        if i * CHUNK == hid * 7 // 8:
            for copy in copies[2 + len(pieces) :]:
                copy.wait()
        for m in blocks:
            u = jnp.dot(prof_ref[m, :], w1_ref[:, part], preferred_element_type=jnp.float32)
            u = u + 0.5 * b1_ref[:, part]
            p = jnp.tanh(u) + 1.0
            hidden = u * p
            hidden_ref[m, part] = hidden.astype(jnp.bfloat16)
            factor_ref[m, part] = p + hidden * (2.0 - p)
    inner = out_ref.shape[0]
    live = lax.broadcasted_iota(jnp.int32, (1, rows), 1) < count_ref[0]
    owner = jnp.where(live, owner_ref[...], -1)
    mine = lax.broadcasted_iota(jnp.int32, (tiles, rows), 0) == owner
    one_hot = mine.astype(jnp.float32)
    running = jnp.dot(one_hot.astype(jnp.bfloat16), upper, preferred_element_type=jnp.float32)
    rank = jnp.sum(running * one_hot, axis=0, keepdims=True).astype(jnp.int32) - 1
    pool = tiles // inner * most
    place = rank_of(owner, inner)
    order = lax.shift_right_arithmetic(owner, inner.bit_length() - 1) * most + rank
    slot = jnp.where(live, place * pool + order, -1)
    placing = as_bf16(lax.broadcasted_iota(jnp.int32, (inner * pool, rows), 0) == slot)
    mine_at = rank_of(me_ref[0], inner)
    lane = order + (mine_at & (LANES // pool - 1)) * pool
    lane_hot = as_bf16(lax.broadcasted_iota(jnp.int32, (LANES, rows), 0) == lane)
    here = live & (lax.broadcasted_iota(jnp.int32, (inner, rows), 0) == place)
    marked = jnp.where(here, (column_ref[...] + 1).astype(jnp.float32), 0.0)
    labels = lax.dot_general(
        marked.astype(jnp.bfloat16), lane_hot, NT, preferred_element_type=jnp.float32
    )

    parts = width // LANES
    out_ref[:, parts * pool :, :] = jnp.broadcast_to(
        labels.reshape(inner, 1, LANES), (inner, LABEL_ROWS, LANES)
    ).astype(jnp.bfloat16)

    scale = 0.5 * cw_ref[...]
    for n, m in enumerate(blocks):
        output = jnp.dot(hidden_ref[m, :], w2_ref[...], preferred_element_type=jnp.float32)
        misfit = scale * (output + b2_ref[...] - rad_ref[m, :].astype(jnp.float32))
        alive = lax.broadcasted_iota(jnp.int32, (ROWS, 1), 0) + n * ROWS < count_ref[0]
        rad_ref[m, :] = jnp.where(alive, misfit, 0.0).astype(jnp.bfloat16)
    for i in range(hid // CHUNK):
        part = pl.ds(i * CHUNK, CHUNK)
        for m in [pl.ds(0, rows)]:
            back = lax.dot_general(
                rad_ref[m, :], w2_ref[part, :], NT, preferred_element_type=jnp.float32
            )
            hidden_ref[m, part] = (back * factor_ref[m, part]).astype(jnp.bfloat16)
    for m in blocks:
        grads = lax.dot_general(
            w1_ref[...], hidden_ref[m, :], NT, preferred_element_type=jnp.float32
        )
        grads_ref[:, m] = grads.astype(jnp.bfloat16)
    wide = ROWS // pool
    for n in range(inner // wide):
        placed = lax.dot_general(
            placing[n * ROWS : (n + 1) * ROWS],
            grads_ref[...],
            NT,
            preferred_element_type=jnp.float32,
        ).astype(jnp.bfloat16)
        some = pl.ds(n * wide, wide)
        for k in range(parts):
            out_ref[some, k * pool : (k + 1) * pool, :] = placed[
                :, k * LANES : (k + 1) * LANES
            ].reshape(wide, pool, LANES)


def blocks_kernel(tiles, most, me_ref, got_ref, own_ref, other_ref):
    inner = got_ref.shape[0]
    outer = tiles // inner
    pool = outer * most
    group = LANES // pool
    parts = own_ref.shape[1] // LANES
    marks = got_ref[:, parts * pool :, :].astype(jnp.float32)[:, 0, :]
    index = lax.broadcasted_iota(jnp.int32, (outer * COL_DEV, LANES), 0)
    lane = lax.broadcasted_iota(jnp.int32, (1, LANES), 1) & (pool - 1)
    turn = lax.shift_right_arithmetic(lane, most.bit_length() - 1) ^ (
        lax.shift_right_arithmetic(me_ref[0], inner.bit_length() - 1)
    )
    chosen = []
    for g in range(inner // group):
        label = jnp.sum(marks[g * group : (g + 1) * group], axis=0, keepdims=True)
        label = label.astype(jnp.int32)
        code = jnp.where(label > 0, turn * COL_DEV + label - 1, -1)
        chosen.append(as_bf16(index == code))
    chosen = jnp.concatenate(chosen, axis=1)
    block = jnp.concatenate(
        [
            got_ref[:, k * pool : (k + 1) * pool, :].reshape(inner * pool, LANES)
            for k in range(parts)
        ],
        axis=1,
    )
    total = jnp.dot(chosen, block, preferred_element_type=jnp.float32)
    own_ref[...] = total[:COL_DEV]
    other_ref[...] = total[COL_DEV:].astype(jnp.bfloat16)


def per_device(
    profiles,
    radiances,
    inner_weight,
    inner_bias,
    outer_weight,
    outer_bias,
    channel_weight,
    counts,
    owner,
    column,
):
    tiles = lax.axis_size("tile")
    rows, width = profiles.shape
    hid = inner_weight.shape[1]
    chan = radiances.shape[1]
    most = max(2, 2 * rows // tiles)
    inner = tiles // OUTER
    pool = OUTER * most
    high = width // LANES * pool + LABEL_ROWS
    me = lax.axis_index("tile").astype(jnp.int32).reshape(1)
    vmem = pl.BlockSpec(memory_space=pltpu.VMEM)
    smem = pl.BlockSpec(memory_space=pltpu.SMEM)
    anywhere = pl.BlockSpec(memory_space=pl.ANY)
    bucket = pl.pallas_call(
        functools.partial(rows_kernel, tiles, most),
        out_shape=jax.ShapeDtypeStruct((inner, high, LANES), jnp.bfloat16),
        in_specs=[smem, smem] + [anywhere] * 9,
        out_specs=vmem,
        scratch_shapes=[
            pltpu.VMEM((1, rows), jnp.int32),
            pltpu.VMEM((1, rows), jnp.int32),
            pltpu.VMEM((rows, width), jnp.bfloat16),
            pltpu.VMEM((rows, chan), jnp.bfloat16),
            pltpu.VMEM((width, hid), jnp.bfloat16),
            pltpu.VMEM((1, hid), jnp.float32),
            pltpu.VMEM((hid, chan), jnp.bfloat16),
            pltpu.VMEM((1, chan), jnp.float32),
            pltpu.VMEM((1, chan), jnp.float32),
            pltpu.VMEM((rows, hid), jnp.bfloat16),
            pltpu.VMEM((rows, hid), jnp.float32),
            pltpu.VMEM((width, rows), jnp.bfloat16),
            pltpu.SemaphoreType.DMA((10,)),
        ],
        compiler_params=pltpu.CompilerParams(vmem_limit_bytes=40 * 1024 * 1024),
        name="rows_kernel",
    )(
        me,
        counts,
        *[
            pltpu.with_memory_space_constraint(operand, pltpu.HBM)
            for operand in (
                owner.reshape(1, rows),
                column.reshape(1, rows),
                profiles,
                radiances,
                inner_weight,
                inner_bias.reshape(1, hid),
                outer_weight,
                outer_bias.reshape(1, chan),
                channel_weight.reshape(1, chan),
            )
        ],
    )
    halves = [
        [o * inner + device_at(i, inner) for i in range(inner)] for o in range(OUTER)
    ]
    got = lax.all_to_all(
        bucket, "tile", split_axis=0, concat_axis=0, axis_index_groups=halves, tiled=True
    )
    own, other = pl.pallas_call(
        functools.partial(blocks_kernel, tiles, most),
        out_shape=[
            jax.ShapeDtypeStruct((COL_DEV, width), jnp.float32),
            jax.ShapeDtypeStruct((COL_DEV, width), jnp.bfloat16),
        ],
        in_specs=[smem, vmem],
        out_specs=[vmem, vmem],
        compiler_params=pltpu.CompilerParams(vmem_limit_bytes=24 * 1024 * 1024),
        name="blocks_kernel",
    )(me, got)
    pairs = [(t, (t + inner) % tiles) for t in range(tiles)]
    return own + lax.ppermute(other, "tile", pairs).astype(jnp.float32)


def solution(mesh):
    placed = (
        P(("group", "tile"), None),
        P(("group", "tile"), None),
        P(),
        P(),
        P(),
        P(),
        P(),
        P(("group", "tile")),
        P(("group", "tile"), None),
        P(("group", "tile")),
    )
    return jax.shard_map(
        per_device,
        mesh=mesh,
        in_specs=placed,
        out_specs=P(("group", "tile"), None),
        check_vma=False,
    )
```

```python
import functools

import jax
import jax.numpy as jnp
from jax import lax
from jax.experimental import pallas as pl
from jax.experimental.pallas import tpu as pltpu
from jax.sharding import PartitionSpec as P

COL_DEV = 128
CHUNK = 256
LANES = 128
LABEL_ROWS = 8
OUTER = 2
ROWS = 256
NT = (((1,), (1,)), ((), ()))


def as_bf16(mask):
    return mask.astype(jnp.float32).astype(jnp.bfloat16)


def reversed_bits(value, count):
    bits = count.bit_length() - 1
    total = 0
    for i in range(bits):
        total = total | (((value >> i) & 1) << (bits - 1 - i))
    return total


def rank_of(device, count):
    code = reversed_bits(device, count)
    rank, shift = code, 1
    while 1 << shift < count:
        rank = rank ^ (code >> shift)
        shift += 1
    return rank


def device_at(rank, count):
    return reversed_bits(rank ^ (rank >> 1), count)


def rows_kernel(
    tiles,
    most,
    me_ref,
    count_ref,
    owner_hbm,
    column_hbm,
    prof_hbm,
    rad_hbm,
    w1_hbm,
    b1_hbm,
    w2_hbm,
    b2_hbm,
    cw_hbm,
    out_ref,
    owner_ref,
    column_ref,
    prof_ref,
    rad_ref,
    w1_ref,
    b1_ref,
    w2_ref,
    b2_ref,
    cw_ref,
    hidden_ref,
    factor_ref,
    grads_ref,
    sems,
):
    rows, width = prof_ref.shape
    hid = w1_ref.shape[1]
    chan = rad_ref.shape[1]
    starts = [0, hid // 4, hid]
    pieces = [pl.ds(lo, hi - lo) for lo, hi in zip(starts[:-1], starts[1:])]
    pairs = (
        [(prof_hbm, prof_ref), (b1_hbm, b1_ref)]
        + [(w1_hbm.at[:, piece], w1_ref.at[:, piece]) for piece in pieces]
        + [(w2_hbm, w2_ref), (rad_hbm, rad_ref), (b2_hbm, b2_ref), (cw_hbm, cw_ref)]
        + [(owner_hbm, owner_ref), (column_hbm, column_ref)]
    )
    copies = [
        pltpu.make_async_copy(src, dst, sems.at[i]) for i, (src, dst) in enumerate(pairs)
    ]
    for copy in copies:
        copy.start()

    upper = as_bf16(
        lax.broadcasted_iota(jnp.int32, (rows, rows), 0)
        <= lax.broadcasted_iota(jnp.int32, (rows, rows), 1)
    )
    copies[0].wait()
    copies[1].wait()
    prof_ref[...] = (prof_ref[...].astype(jnp.float32) * 0.5).astype(jnp.bfloat16)
    blocks = [pl.ds(i, ROWS) for i in range(0, rows, ROWS)]
    for i in range(hid // CHUNK):
        part = pl.ds(i * CHUNK, CHUNK)
        if i * CHUNK in starts:
            copies[2 + starts.index(i * CHUNK)].wait()
        if i * CHUNK == hid * 7 // 8:
            for copy in copies[2 + len(pieces) :]:
                copy.wait()
        for m in blocks:
            u = jnp.dot(prof_ref[m, :], w1_ref[:, part], preferred_element_type=jnp.float32)
            u = u + 0.5 * b1_ref[:, part]
            p = jnp.tanh(u) + 1.0
            hidden = u * p
            hidden_ref[m, part] = hidden.astype(jnp.bfloat16)
            factor_ref[m, part] = p + hidden * (2.0 - p)
    inner = out_ref.shape[0]
    live = lax.broadcasted_iota(jnp.int32, (1, rows), 1) < count_ref[0]
    owner = jnp.where(live, owner_ref[...], -1)
    mine = lax.broadcasted_iota(jnp.int32, (tiles, rows), 0) == owner
    one_hot = mine.astype(jnp.float32)
    running = jnp.dot(one_hot.astype(jnp.bfloat16), upper, preferred_element_type=jnp.float32)
    rank = jnp.sum(running * one_hot, axis=0, keepdims=True).astype(jnp.int32) - 1
    pool = tiles // inner * most
    place = rank_of(owner, inner)
    order = lax.shift_right_arithmetic(owner, inner.bit_length() - 1) * most + rank
    slot = jnp.where(live, place * pool + order, -1)
    placing = as_bf16(lax.broadcasted_iota(jnp.int32, (inner * pool, rows), 0) == slot)
    mine_at = rank_of(me_ref[0], inner)
    lane = order + (mine_at & (LANES // pool - 1)) * pool
    lane_hot = as_bf16(lax.broadcasted_iota(jnp.int32, (LANES, rows), 0) == lane)
    here = live & (lax.broadcasted_iota(jnp.int32, (inner, rows), 0) == place)
    marked = jnp.where(here, (column_ref[...] + 1).astype(jnp.float32), 0.0)
    labels = lax.dot_general(
        marked.astype(jnp.bfloat16), lane_hot, NT, preferred_element_type=jnp.float32
    )

    parts = width // LANES
    out_ref[:, parts * pool :, :] = jnp.broadcast_to(
        labels.reshape(inner, 1, LANES), (inner, LABEL_ROWS, LANES)
    ).astype(jnp.bfloat16)

    scale = 0.5 * cw_ref[...]
    for n, m in enumerate(blocks):
        output = jnp.dot(hidden_ref[m, :], w2_ref[...], preferred_element_type=jnp.float32)
        misfit = scale * (output + b2_ref[...] - rad_ref[m, :].astype(jnp.float32))
        alive = lax.broadcasted_iota(jnp.int32, (ROWS, 1), 0) + n * ROWS < count_ref[0]
        rad_ref[m, :] = jnp.where(alive, misfit, 0.0).astype(jnp.bfloat16)
    for i in range(hid // CHUNK):
        part = pl.ds(i * CHUNK, CHUNK)
        for m in blocks:
            back = lax.dot_general(
                rad_ref[m, :], w2_ref[part, :], NT, preferred_element_type=jnp.float32
            )
            hidden_ref[m, part] = (back * factor_ref[m, part]).astype(jnp.bfloat16)
    for m in blocks:
        grads = lax.dot_general(
            w1_ref[...], hidden_ref[m, :], NT, preferred_element_type=jnp.float32
        )
        grads_ref[:, m] = grads.astype(jnp.bfloat16)
    wide = ROWS // pool
    for n in range(inner // wide):
        placed = lax.dot_general(
            placing[n * ROWS : (n + 1) * ROWS],
            grads_ref[...],
            NT,
            preferred_element_type=jnp.float32,
        ).astype(jnp.bfloat16)
        some = pl.ds(n * wide, wide)
        for k in range(parts):
            out_ref[some, k * pool : (k + 1) * pool, :] = placed[
                :, k * LANES : (k + 1) * LANES
            ].reshape(wide, pool, LANES)


def sums_kernel(tiles, most, side, me_ref, got_ref, out_ref):
    inner = got_ref.shape[0]
    pool = tiles // inner * most
    group = LANES // pool
    parts = out_ref.shape[1] // LANES
    marks = got_ref[:, parts * pool :, :].astype(jnp.float32)[:, 0, :]
    index = lax.broadcasted_iota(jnp.int32, (COL_DEV, LANES), 0)
    lane = lax.broadcasted_iota(jnp.int32, (1, LANES), 1) & (pool - 1)
    turn = lax.shift_right_arithmetic(lane, most.bit_length() - 1) ^ (
        lax.shift_right_arithmetic(me_ref[0], inner.bit_length() - 1)
    )
    chosen = []
    for g in range(inner // group):
        label = jnp.sum(marks[g * group : (g + 1) * group], axis=0, keepdims=True)
        label = label.astype(jnp.int32)
        code = jnp.where((label > 0) & (turn == side), label - 1, -1)
        chosen.append(as_bf16(index == code))
    chosen = jnp.concatenate(chosen, axis=1)
    block = jnp.concatenate(
        [
            got_ref[:, k * pool : (k + 1) * pool, :].reshape(inner * pool, LANES)
            for k in range(parts)
        ],
        axis=1,
    )
    total = jnp.dot(chosen, block, preferred_element_type=jnp.float32)
    out_ref[...] = total.astype(out_ref.dtype)


def per_device(
    profiles,
    radiances,
    inner_weight,
    inner_bias,
    outer_weight,
    outer_bias,
    channel_weight,
    counts,
    owner,
    column,
):
    tiles = lax.axis_size("tile")
    rows, width = profiles.shape
    hid = inner_weight.shape[1]
    chan = radiances.shape[1]
    most = max(2, 2 * rows // tiles)
    inner = tiles // OUTER
    pool = OUTER * most
    high = width // LANES * pool + LABEL_ROWS
    me = lax.axis_index("tile").astype(jnp.int32).reshape(1)
    vmem = pl.BlockSpec(memory_space=pltpu.VMEM)
    smem = pl.BlockSpec(memory_space=pltpu.SMEM)
    anywhere = pl.BlockSpec(memory_space=pl.ANY)
    bucket = pl.pallas_call(
        functools.partial(rows_kernel, tiles, most),
        out_shape=jax.ShapeDtypeStruct((inner, high, LANES), jnp.bfloat16),
        in_specs=[smem, smem] + [anywhere] * 9,
        out_specs=vmem,
        scratch_shapes=[
            pltpu.VMEM((1, rows), jnp.int32),
            pltpu.VMEM((1, rows), jnp.int32),
            pltpu.VMEM((rows, width), jnp.bfloat16),
            pltpu.VMEM((rows, chan), jnp.bfloat16),
            pltpu.VMEM((width, hid), jnp.bfloat16),
            pltpu.VMEM((1, hid), jnp.float32),
            pltpu.VMEM((hid, chan), jnp.bfloat16),
            pltpu.VMEM((1, chan), jnp.float32),
            pltpu.VMEM((1, chan), jnp.float32),
            pltpu.VMEM((rows, hid), jnp.bfloat16),
            pltpu.VMEM((rows, hid), jnp.float32),
            pltpu.VMEM((width, rows), jnp.bfloat16),
            pltpu.SemaphoreType.DMA((10,)),
        ],
        compiler_params=pltpu.CompilerParams(vmem_limit_bytes=40 * 1024 * 1024),
        name="rows_kernel",
    )(
        me,
        counts,
        *[
            pltpu.with_memory_space_constraint(operand, pltpu.HBM)
            for operand in (
                owner.reshape(1, rows),
                column.reshape(1, rows),
                profiles,
                radiances,
                inner_weight,
                inner_bias.reshape(1, hid),
                outer_weight,
                outer_bias.reshape(1, chan),
                channel_weight.reshape(1, chan),
            )
        ],
    )
    halves = [
        [o * inner + device_at(i, inner) for i in range(inner)] for o in range(OUTER)
    ]
    got = lax.all_to_all(
        bucket, "tile", split_axis=0, concat_axis=0, axis_index_groups=halves, tiled=True
    )

    def sums(side, dtype):
        return pl.pallas_call(
            functools.partial(sums_kernel, tiles, most, side),
            out_shape=jax.ShapeDtypeStruct((COL_DEV, width), dtype),
            in_specs=[smem, vmem],
            out_specs=vmem,
            compiler_params=pltpu.CompilerParams(vmem_limit_bytes=24 * 1024 * 1024),
            cost_estimate=pl.CostEstimate(
                flops=1 << 28, bytes_accessed=1 << 20, transcendentals=0
            ),
            name="sums_kernel",
        )(me, got)

    pairs = [(t, (t + inner) % tiles) for t in range(tiles)]
    came = lax.ppermute(sums(1, jnp.bfloat16), "tile", pairs)
    return sums(0, jnp.float32) + came.astype(jnp.float32)


def solution(mesh):
    placed = (
        P(("group", "tile"), None),
        P(("group", "tile"), None),
        P(),
        P(),
        P(),
        P(),
        P(),
        P(("group", "tile")),
        P(("group", "tile"), None),
        P(("group", "tile")),
    )
    return jax.shard_map(
        per_device,
        mesh=mesh,
        in_specs=placed,
        out_specs=P(("group", "tile"), None),
        check_vma=False,
    )
```

```python
import functools

import jax
import jax.numpy as jnp
from jax import lax
from jax.experimental import pallas as pl
from jax.experimental.pallas import tpu as pltpu
from jax.sharding import PartitionSpec as P

COL_DEV = 128
CHUNK = 256
LANES = 128
LABEL_ROWS = 8
OUTER = 2
ROWS = 256
NT = (((1,), (1,)), ((), ()))


def as_bf16(mask):
    return mask.astype(jnp.float32).astype(jnp.bfloat16)


def reversed_bits(value, count):
    bits = count.bit_length() - 1
    total = 0
    for i in range(bits):
        total = total | (((value >> i) & 1) << (bits - 1 - i))
    return total


def rank_of(device, count):
    code = reversed_bits(device, count)
    rank, shift = code, 1
    while 1 << shift < count:
        rank = rank ^ (code >> shift)
        shift += 1
    return rank


def device_at(rank, count):
    return reversed_bits(rank ^ (rank >> 1), count)


def rows_kernel(
    tiles,
    most,
    me_ref,
    count_ref,
    owner_hbm,
    column_hbm,
    prof_hbm,
    rad_hbm,
    w1_hbm,
    b1_hbm,
    w2_hbm,
    b2_hbm,
    cw_hbm,
    out_ref,
    owner_ref,
    column_ref,
    prof_ref,
    rad_ref,
    w1_ref,
    b1_ref,
    w2_ref,
    b2_ref,
    cw_ref,
    hidden_ref,
    factor_ref,
    grads_ref,
    sems,
):
    rows, width = prof_ref.shape
    hid = w1_ref.shape[1]
    chan = rad_ref.shape[1]
    starts = [0, hid // 4, hid // 2, hid]
    pieces = [pl.ds(lo, hi - lo) for lo, hi in zip(starts[:-1], starts[1:])]
    pairs = (
        [(prof_hbm, prof_ref), (b1_hbm, b1_ref)]
        + [(w1_hbm.at[:, piece], w1_ref.at[:, piece]) for piece in pieces]
        + [(w2_hbm, w2_ref), (rad_hbm, rad_ref), (b2_hbm, b2_ref), (cw_hbm, cw_ref)]
        + [(owner_hbm, owner_ref), (column_hbm, column_ref)]
    )
    copies = [
        pltpu.make_async_copy(src, dst, sems.at[i]) for i, (src, dst) in enumerate(pairs)
    ]
    for copy in copies:
        copy.start()

    upper = as_bf16(
        lax.broadcasted_iota(jnp.int32, (rows, rows), 0)
        <= lax.broadcasted_iota(jnp.int32, (rows, rows), 1)
    )
    copies[0].wait()
    copies[1].wait()
    prof_ref[...] = (prof_ref[...].astype(jnp.float32) * 0.5).astype(jnp.bfloat16)
    blocks = [pl.ds(i, ROWS) for i in range(0, rows, ROWS)]
    for i in range(hid // CHUNK):
        part = pl.ds(i * CHUNK, CHUNK)
        if i * CHUNK in starts:
            copies[2 + starts.index(i * CHUNK)].wait()
        if i * CHUNK == hid * 7 // 8:
            for copy in copies[2 + len(pieces) :]:
                copy.wait()
        for m in blocks:
            u = jnp.dot(prof_ref[m, :], w1_ref[:, part], preferred_element_type=jnp.float32)
            u = u + 0.5 * b1_ref[:, part]
            p = jnp.tanh(u) + 1.0
            hidden = u * p
            hidden_ref[m, part] = hidden.astype(jnp.bfloat16)
            factor_ref[m, part] = p + hidden * (2.0 - p)
    inner = out_ref.shape[0]
    live = lax.broadcasted_iota(jnp.int32, (1, rows), 1) < count_ref[0]
    owner = jnp.where(live, owner_ref[...], -1)
    mine = lax.broadcasted_iota(jnp.int32, (tiles, rows), 0) == owner
    one_hot = mine.astype(jnp.float32)
    running = jnp.dot(one_hot.astype(jnp.bfloat16), upper, preferred_element_type=jnp.float32)
    rank = jnp.sum(running * one_hot, axis=0, keepdims=True).astype(jnp.int32) - 1
    pool = tiles // inner * most
    place = rank_of(owner, inner)
    order = lax.shift_right_arithmetic(owner, inner.bit_length() - 1) * most + rank
    slot = jnp.where(live, place * pool + order, -1)
    placing = as_bf16(lax.broadcasted_iota(jnp.int32, (inner * pool, rows), 0) == slot)
    mine_at = rank_of(me_ref[0], inner)
    lane = order + (mine_at & (LANES // pool - 1)) * pool
    lane_hot = as_bf16(lax.broadcasted_iota(jnp.int32, (LANES, rows), 0) == lane)
    here = live & (lax.broadcasted_iota(jnp.int32, (inner, rows), 0) == place)
    marked = jnp.where(here, (column_ref[...] + 1).astype(jnp.float32), 0.0)
    labels = lax.dot_general(
        marked.astype(jnp.bfloat16), lane_hot, NT, preferred_element_type=jnp.float32
    )

    parts = width // LANES
    out_ref[:, parts * pool :, :] = jnp.broadcast_to(
        labels.reshape(inner, 1, LANES), (inner, LABEL_ROWS, LANES)
    ).astype(jnp.bfloat16)

    scale = 0.5 * cw_ref[...]
    for n, m in enumerate(blocks):
        output = jnp.dot(hidden_ref[m, :], w2_ref[...], preferred_element_type=jnp.float32)
        misfit = scale * (output + b2_ref[...] - rad_ref[m, :].astype(jnp.float32))
        alive = lax.broadcasted_iota(jnp.int32, (ROWS, 1), 0) + n * ROWS < count_ref[0]
        rad_ref[m, :] = jnp.where(alive, misfit, 0.0).astype(jnp.bfloat16)
    for i in range(hid // CHUNK):
        part = pl.ds(i * CHUNK, CHUNK)
        for m in blocks:
            back = lax.dot_general(
                rad_ref[m, :], w2_ref[part, :], NT, preferred_element_type=jnp.float32
            )
            hidden_ref[m, part] = (back * factor_ref[m, part]).astype(jnp.bfloat16)
    for m in blocks:
        grads = lax.dot_general(
            w1_ref[...], hidden_ref[m, :], NT, preferred_element_type=jnp.float32
        )
        grads_ref[:, m] = grads.astype(jnp.bfloat16)
    wide = ROWS // pool
    for n in range(inner // wide):
        placed = lax.dot_general(
            placing[n * ROWS : (n + 1) * ROWS],
            grads_ref[...],
            NT,
            preferred_element_type=jnp.float32,
        ).astype(jnp.bfloat16)
        some = pl.ds(n * wide, wide)
        for k in range(parts):
            out_ref[some, k * pool : (k + 1) * pool, :] = placed[
                :, k * LANES : (k + 1) * LANES
            ].reshape(wide, pool, LANES)


def sums_kernel(tiles, most, side, me_ref, got_ref, out_ref):
    inner = got_ref.shape[0]
    pool = tiles // inner * most
    group = LANES // pool
    parts = out_ref.shape[1] // LANES
    marks = got_ref[:, parts * pool :, :].astype(jnp.float32)[:, 0, :]
    index = lax.broadcasted_iota(jnp.int32, (COL_DEV, LANES), 0)
    lane = lax.broadcasted_iota(jnp.int32, (1, LANES), 1) & (pool - 1)
    turn = lax.shift_right_arithmetic(lane, most.bit_length() - 1) ^ (
        lax.shift_right_arithmetic(me_ref[0], inner.bit_length() - 1)
    )
    chosen = []
    for g in range(inner // group):
        label = jnp.sum(marks[g * group : (g + 1) * group], axis=0, keepdims=True)
        label = label.astype(jnp.int32)
        code = jnp.where((label > 0) & (turn == side), label - 1, -1)
        chosen.append(as_bf16(index == code))
    chosen = jnp.concatenate(chosen, axis=1)
    block = jnp.concatenate(
        [
            got_ref[:, k * pool : (k + 1) * pool, :].reshape(inner * pool, LANES)
            for k in range(parts)
        ],
        axis=1,
    )
    total = jnp.dot(chosen, block, preferred_element_type=jnp.float32)
    out_ref[...] = total.astype(out_ref.dtype)


def per_device(
    profiles,
    radiances,
    inner_weight,
    inner_bias,
    outer_weight,
    outer_bias,
    channel_weight,
    counts,
    owner,
    column,
):
    tiles = lax.axis_size("tile")
    rows, width = profiles.shape
    hid = inner_weight.shape[1]
    chan = radiances.shape[1]
    most = max(2, 2 * rows // tiles)
    inner = tiles // OUTER
    pool = OUTER * most
    high = width // LANES * pool + LABEL_ROWS
    me = lax.axis_index("tile").astype(jnp.int32).reshape(1)
    vmem = pl.BlockSpec(memory_space=pltpu.VMEM)
    smem = pl.BlockSpec(memory_space=pltpu.SMEM)
    anywhere = pl.BlockSpec(memory_space=pl.ANY)
    bucket = pl.pallas_call(
        functools.partial(rows_kernel, tiles, most),
        out_shape=jax.ShapeDtypeStruct((inner, high, LANES), jnp.bfloat16),
        in_specs=[smem, smem] + [anywhere] * 9,
        out_specs=vmem,
        scratch_shapes=[
            pltpu.VMEM((1, rows), jnp.int32),
            pltpu.VMEM((1, rows), jnp.int32),
            pltpu.VMEM((rows, width), jnp.bfloat16),
            pltpu.VMEM((rows, chan), jnp.bfloat16),
            pltpu.VMEM((width, hid), jnp.bfloat16),
            pltpu.VMEM((1, hid), jnp.float32),
            pltpu.VMEM((hid, chan), jnp.bfloat16),
            pltpu.VMEM((1, chan), jnp.float32),
            pltpu.VMEM((1, chan), jnp.float32),
            pltpu.VMEM((rows, hid), jnp.bfloat16),
            pltpu.VMEM((rows, hid), jnp.float32),
            pltpu.VMEM((width, rows), jnp.bfloat16),
            pltpu.SemaphoreType.DMA((11,)),
        ],
        compiler_params=pltpu.CompilerParams(vmem_limit_bytes=40 * 1024 * 1024),
        name="rows_kernel",
    )(
        me,
        counts,
        *[
            pltpu.with_memory_space_constraint(operand, pltpu.HBM)
            for operand in (
                owner.reshape(1, rows),
                column.reshape(1, rows),
                profiles,
                radiances,
                inner_weight,
                inner_bias.reshape(1, hid),
                outer_weight,
                outer_bias.reshape(1, chan),
                channel_weight.reshape(1, chan),
            )
        ],
    )
    halves = [
        [o * inner + device_at(i, inner) for i in range(inner)] for o in range(OUTER)
    ]
    got = lax.all_to_all(
        bucket, "tile", split_axis=0, concat_axis=0, axis_index_groups=halves, tiled=True
    )

    def sums(side, dtype):
        return pl.pallas_call(
            functools.partial(sums_kernel, tiles, most, side),
            out_shape=jax.ShapeDtypeStruct((COL_DEV, width), dtype),
            in_specs=[smem, vmem],
            out_specs=vmem,
            compiler_params=pltpu.CompilerParams(vmem_limit_bytes=24 * 1024 * 1024),
            cost_estimate=pl.CostEstimate(
                flops=1 << 28, bytes_accessed=1 << 20, transcendentals=0
            ),
            name="sums_kernel",
        )(me, got)

    pairs = [(t, (t + inner) % tiles) for t in range(tiles)]
    came = lax.ppermute(sums(1, jnp.bfloat16), "tile", pairs)
    return sums(0, jnp.float32) + came.astype(jnp.float32)


def solution(mesh):
    placed = (
        P(("group", "tile"), None),
        P(("group", "tile"), None),
        P(),
        P(),
        P(),
        P(),
        P(),
        P(("group", "tile")),
        P(("group", "tile"), None),
        P(("group", "tile")),
    )
    return jax.shard_map(
        per_device,
        mesh=mesh,
        in_specs=placed,
        out_specs=P(("group", "tile"), None),
        check_vma=False,
    )
```

```python
import functools

import jax
import jax.numpy as jnp
from jax import lax
from jax.experimental import pallas as pl
from jax.experimental.pallas import tpu as pltpu
from jax.sharding import PartitionSpec as P

COL_DEV = 128
CHUNK = 256
LANES = 128
LABEL_ROWS = 8
OUTER = 2
ROWS = 256
NT = (((1,), (1,)), ((), ()))


def as_bf16(mask):
    return mask.astype(jnp.float32).astype(jnp.bfloat16)


def reversed_bits(value, count):
    bits = count.bit_length() - 1
    total = 0
    for i in range(bits):
        total = total | (((value >> i) & 1) << (bits - 1 - i))
    return total


def rank_of(device, count):
    code = reversed_bits(device, count)
    rank, shift = code, 1
    while 1 << shift < count:
        rank = rank ^ (code >> shift)
        shift += 1
    return rank


def device_at(rank, count):
    return reversed_bits(rank ^ (rank >> 1), count)


def rows_kernel(
    tiles,
    most,
    me_ref,
    count_ref,
    owner_hbm,
    column_hbm,
    prof_hbm,
    rad_hbm,
    w1_hbm,
    b1_hbm,
    w2_hbm,
    b2_hbm,
    cw_hbm,
    out_ref,
    owner_ref,
    column_ref,
    prof_ref,
    rad_ref,
    w1_ref,
    b1_ref,
    w2_ref,
    b2_ref,
    cw_ref,
    hidden_ref,
    factor_ref,
    grads_ref,
    sems,
):
    rows, width = prof_ref.shape
    hid = w1_ref.shape[1]
    chan = rad_ref.shape[1]
    starts = [0, hid // 4, hid]
    pieces = [pl.ds(lo, hi - lo) for lo, hi in zip(starts[:-1], starts[1:])]
    pairs = (
        [(prof_hbm, prof_ref), (b1_hbm, b1_ref)]
        + [(w1_hbm.at[:, piece], w1_ref.at[:, piece]) for piece in pieces]
        + [(w2_hbm, w2_ref), (rad_hbm, rad_ref), (b2_hbm, b2_ref), (cw_hbm, cw_ref)]
        + [(owner_hbm, owner_ref), (column_hbm, column_ref)]
    )
    copies = [
        pltpu.make_async_copy(src, dst, sems.at[i]) for i, (src, dst) in enumerate(pairs)
    ]
    for copy in copies:
        copy.start()

    upper = as_bf16(
        lax.broadcasted_iota(jnp.int32, (rows, rows), 0)
        <= lax.broadcasted_iota(jnp.int32, (rows, rows), 1)
    )
    copies[0].wait()
    copies[1].wait()
    prof_ref[...] = (prof_ref[...].astype(jnp.float32) * 0.5).astype(jnp.bfloat16)
    blocks = [pl.ds(i, ROWS) for i in range(0, rows, ROWS)]
    for i in range(hid // CHUNK):
        part = pl.ds(i * CHUNK, CHUNK)
        if i * CHUNK in starts:
            copies[2 + starts.index(i * CHUNK)].wait()
        if i * CHUNK == hid * 7 // 8:
            for copy in copies[2 + len(pieces) :]:
                copy.wait()
        for m in blocks:
            u = jnp.dot(prof_ref[m, :], w1_ref[:, part], preferred_element_type=jnp.float32)
            u = u + 0.5 * b1_ref[:, part]
            p = jnp.tanh(u) + 1.0
            hidden = u * p
            hidden_ref[m, part] = hidden.astype(jnp.bfloat16)
            factor_ref[m, part] = p + hidden * (2.0 - p)
    inner = out_ref.shape[0]
    live = lax.broadcasted_iota(jnp.int32, (1, rows), 1) < count_ref[0]
    owner = jnp.where(live, owner_ref[...], -1)
    mine = lax.broadcasted_iota(jnp.int32, (tiles, rows), 0) == owner
    one_hot = mine.astype(jnp.float32)
    running = jnp.dot(one_hot.astype(jnp.bfloat16), upper, preferred_element_type=jnp.float32)
    rank = jnp.sum(running * one_hot, axis=0, keepdims=True).astype(jnp.int32) - 1
    pool = tiles // inner * most
    place = rank_of(owner, inner)
    order = lax.shift_right_arithmetic(owner, inner.bit_length() - 1) * most + rank
    slot = jnp.where(live, place * pool + order, -1)
    placing = as_bf16(lax.broadcasted_iota(jnp.int32, (inner * pool, rows), 0) == slot)
    mine_at = rank_of(me_ref[0], inner)
    lane = order + (mine_at & (LANES // pool - 1)) * pool
    lane_hot = as_bf16(lax.broadcasted_iota(jnp.int32, (LANES, rows), 0) == lane)
    here = live & (lax.broadcasted_iota(jnp.int32, (inner, rows), 0) == place)
    marked = jnp.where(here, (column_ref[...] + 1).astype(jnp.float32), 0.0)
    labels = lax.dot_general(
        marked.astype(jnp.bfloat16), lane_hot, NT, preferred_element_type=jnp.float32
    )

    parts = width // LANES
    out_ref[:, parts * pool :, :] = jnp.broadcast_to(
        labels.reshape(inner, 1, LANES), (inner, LABEL_ROWS, LANES)
    ).astype(jnp.bfloat16)

    scale = 0.5 * cw_ref[...]
    for n, m in enumerate(blocks):
        output = jnp.dot(hidden_ref[m, :], w2_ref[...], preferred_element_type=jnp.float32)
        misfit = scale * (output + b2_ref[...] - rad_ref[m, :].astype(jnp.float32))
        alive = lax.broadcasted_iota(jnp.int32, (ROWS, 1), 0) + n * ROWS < count_ref[0]
        rad_ref[m, :] = jnp.where(alive, misfit, 0.0).astype(jnp.bfloat16)
    for i in range(hid // CHUNK):
        part = pl.ds(i * CHUNK, CHUNK)
        for m in blocks:
            back = lax.dot_general(
                rad_ref[m, :], w2_ref[part, :], NT, preferred_element_type=jnp.float32
            )
            hidden_ref[m, part] = (back * factor_ref[m, part]).astype(jnp.bfloat16)
    for m in blocks:
        grads = lax.dot_general(
            w1_ref[...], hidden_ref[m, :], NT, preferred_element_type=jnp.float32
        )
        grads_ref[:, m] = grads.astype(jnp.bfloat16)
    step = 2 * ROWS
    wide = step // pool
    for n in range(inner // wide):
        placed = lax.dot_general(
            placing[n * step : (n + 1) * step],
            grads_ref[...],
            NT,
            preferred_element_type=jnp.float32,
        ).astype(jnp.bfloat16)
        some = pl.ds(n * wide, wide)
        for k in range(parts):
            out_ref[some, k * pool : (k + 1) * pool, :] = placed[
                :, k * LANES : (k + 1) * LANES
            ].reshape(wide, pool, LANES)


def sums_kernel(tiles, most, side, me_ref, got_ref, out_ref):
    inner = got_ref.shape[0]
    pool = tiles // inner * most
    group = LANES // pool
    parts = out_ref.shape[1] // LANES
    marks = got_ref[:, parts * pool :, :].astype(jnp.float32)[:, 0, :]
    index = lax.broadcasted_iota(jnp.int32, (COL_DEV, LANES), 0)
    lane = lax.broadcasted_iota(jnp.int32, (1, LANES), 1) & (pool - 1)
    turn = lax.shift_right_arithmetic(lane, most.bit_length() - 1) ^ (
        lax.shift_right_arithmetic(me_ref[0], inner.bit_length() - 1)
    )
    chosen = []
    for g in range(inner // group):
        label = jnp.sum(marks[g * group : (g + 1) * group], axis=0, keepdims=True)
        label = label.astype(jnp.int32)
        code = jnp.where((label > 0) & (turn == side), label - 1, -1)
        chosen.append(as_bf16(index == code))
    chosen = jnp.concatenate(chosen, axis=1)
    block = jnp.concatenate(
        [
            got_ref[:, k * pool : (k + 1) * pool, :].reshape(inner * pool, LANES)
            for k in range(parts)
        ],
        axis=1,
    )
    total = jnp.dot(chosen, block, preferred_element_type=jnp.float32)
    out_ref[...] = total.astype(out_ref.dtype)


def per_device(
    profiles,
    radiances,
    inner_weight,
    inner_bias,
    outer_weight,
    outer_bias,
    channel_weight,
    counts,
    owner,
    column,
):
    tiles = lax.axis_size("tile")
    rows, width = profiles.shape
    hid = inner_weight.shape[1]
    chan = radiances.shape[1]
    most = max(2, 2 * rows // tiles)
    inner = tiles // OUTER
    pool = OUTER * most
    high = width // LANES * pool + LABEL_ROWS
    me = lax.axis_index("tile").astype(jnp.int32).reshape(1)
    vmem = pl.BlockSpec(memory_space=pltpu.VMEM)
    smem = pl.BlockSpec(memory_space=pltpu.SMEM)
    anywhere = pl.BlockSpec(memory_space=pl.ANY)
    bucket = pl.pallas_call(
        functools.partial(rows_kernel, tiles, most),
        out_shape=jax.ShapeDtypeStruct((inner, high, LANES), jnp.bfloat16),
        in_specs=[smem, smem] + [anywhere] * 9,
        out_specs=vmem,
        scratch_shapes=[
            pltpu.VMEM((1, rows), jnp.int32),
            pltpu.VMEM((1, rows), jnp.int32),
            pltpu.VMEM((rows, width), jnp.bfloat16),
            pltpu.VMEM((rows, chan), jnp.bfloat16),
            pltpu.VMEM((width, hid), jnp.bfloat16),
            pltpu.VMEM((1, hid), jnp.float32),
            pltpu.VMEM((hid, chan), jnp.bfloat16),
            pltpu.VMEM((1, chan), jnp.float32),
            pltpu.VMEM((1, chan), jnp.float32),
            pltpu.VMEM((rows, hid), jnp.bfloat16),
            pltpu.VMEM((rows, hid), jnp.float32),
            pltpu.VMEM((width, rows), jnp.bfloat16),
            pltpu.SemaphoreType.DMA((10,)),
        ],
        compiler_params=pltpu.CompilerParams(vmem_limit_bytes=40 * 1024 * 1024),
        name="rows_kernel",
    )(
        me,
        counts,
        *[
            pltpu.with_memory_space_constraint(operand, pltpu.HBM)
            for operand in (
                owner.reshape(1, rows),
                column.reshape(1, rows),
                profiles,
                radiances,
                inner_weight,
                inner_bias.reshape(1, hid),
                outer_weight,
                outer_bias.reshape(1, chan),
                channel_weight.reshape(1, chan),
            )
        ],
    )
    halves = [
        [o * inner + device_at(i, inner) for i in range(inner)] for o in range(OUTER)
    ]
    got = lax.all_to_all(
        bucket, "tile", split_axis=0, concat_axis=0, axis_index_groups=halves, tiled=True
    )

    def sums(side, dtype):
        return pl.pallas_call(
            functools.partial(sums_kernel, tiles, most, side),
            out_shape=jax.ShapeDtypeStruct((COL_DEV, width), dtype),
            in_specs=[smem, vmem],
            out_specs=vmem,
            compiler_params=pltpu.CompilerParams(vmem_limit_bytes=24 * 1024 * 1024),
            cost_estimate=pl.CostEstimate(
                flops=1 << 28, bytes_accessed=1 << 20, transcendentals=0
            ),
            name="sums_kernel",
        )(me, got)

    pairs = [(t, (t + inner) % tiles) for t in range(tiles)]
    came = lax.ppermute(sums(1, jnp.bfloat16), "tile", pairs)
    return sums(0, jnp.float32) + came.astype(jnp.float32)


def solution(mesh):
    placed = (
        P(("group", "tile"), None),
        P(("group", "tile"), None),
        P(),
        P(),
        P(),
        P(),
        P(),
        P(("group", "tile")),
        P(("group", "tile"), None),
        P(("group", "tile")),
    )
    return jax.shard_map(
        per_device,
        mesh=mesh,
        in_specs=placed,
        out_specs=P(("group", "tile"), None),
        check_vma=False,
    )
```
